32 devices in a mesh: row: 8 (over z, y), col: 4 (over x, core).
Axes of the slice: x: 2, y: 2, z: 4, core: 2. Of those that a mesh axis runs over, the one named last changes fastest.
Arguments:
- layer_input: bfloat16 [16384, 2048], P(('col', 'row')), may hold values from -6 to 6
- segments: int32 [16384], P('col'), may hold values from 0 to 3, as said below
- w_query: bfloat16 [2048, 2048], P('col', 'row')
- w_key: bfloat16 [2048, 2048], P('col', 'row')
- w_value: bfloat16 [2048, 2048], P('col', 'row'), may hold values from -0.125 to 0.125
- w_out: bfloat16 [2048, 2048], P('row', 'col'), may hold values from -0.125 to 0.125
- query_gain: bfloat16 [2048], P(('row', 'col'))
- key_gain: bfloat16 [2048], P(('row', 'col'))
- attn_gain: bfloat16 [2048], P('col'), may hold values from 0.25 to 1.75
- w_gate: bfloat16 [2048, 8192], P('col', 'row'), may hold values from -0.125 to 0.125
- w_up: bfloat16 [2048, 8192], P('col', 'row'), may hold values from -0.125 to 0.125
- w_down: bfloat16 [8192, 2048], P('row', 'col'), may hold values from -0.0625 to 0.0625
- mlp_gain: bfloat16 [2048], P('col'), may hold values from 0.25 to 1.75
- cotangent: bfloat16 [16384, 2048], P(('col', 'row')), may hold values from -6 to 6
Outputs:
- layer_output: bfloat16 [16384, 2048], P(('col', 'row'))
- input_grad: bfloat16 [16384, 2048], P(('col', 'row'))
- w_query_grad: float32 [2048, 2048], P('col', 'row')
- w_key_grad: float32 [2048, 2048], P('col', 'row')
- w_value_grad: float32 [2048, 2048], P('col', 'row')
- w_out_grad: float32 [2048, 2048], P('row', 'col')
- query_gain_grad: float32 [2048], P(('row', 'col'))
- key_gain_grad: float32 [2048], P(('row', 'col'))
- attn_gain_grad: float32 [2048], P('col')
- w_gate_grad: float32 [2048, 8192], P('col', 'row')
- w_up_grad: float32 [2048, 8192], P('col', 'row')
- w_down_grad: float32 [8192, 2048], P('row', 'col')
- mlp_gain_grad: float32 [2048], P('col')
The draws below stay inside these ranges and needn't reach their ends.
Inputs may be any that keep to these rules, and one draw needn't show every extreme that they name: `segments`: each packed sequence of 4096 consecutive tokens holds exactly four documents; segment numbers start at 0 and rise by one at each document boundary, and every document holds at least 204 tokens.
All inputs are finite; a program needn't handle non-finite values.
Results may differ from the reference program's by a relative error of at most 0.025.
Values may be sent and summed in bfloat16 or wider, within the bound.
A program may use at most 448 MiB of HBM per device.

```python
import jax
import jax.numpy as jnp
from jax import lax

D = 2048
HEADS = 16
FF = 8192
SEQ = 4096
TOKENS = 16384


def draw_segments(key, part):
    key = jax.random.fold_in(key, 5)
    groups = TOKENS // SEQ
    least = max(SEQ // 20, 1)
    spare = SEQ - 4 * least
    shares = jax.random.randint(key, (groups, 4), 100, 300, dtype=jnp.int32)
    running = jnp.cumsum(shares, axis=1).astype(jnp.int32)
    whole = running[:, -1:]
    steps_index = jnp.arange(1, 5, dtype=jnp.int32)
    ends = (steps_index[None, :] * least + spare * running // whole).astype(jnp.int32)
    token_index = jnp.arange(SEQ, dtype=jnp.int32)
    numbers = jnp.sum((ends[:, None, :3] <= token_index[None, :, None]).astype(jnp.int32), axis=-1)
    return numbers.reshape(TOKENS).astype(jnp.int32)


def draw_w_query(key, part):
    key = jax.random.fold_in(key, 11)
    columns = jnp.arange(D, dtype=jnp.float32) / D
    base = jax.random.normal(key, (D, D), jnp.float32)
    spread = 0.6 + 1.2 * columns
    return (base * spread[None, :] * D ** (-0.5)).astype(jnp.bfloat16)


def draw_w_key(key, part):
    key = jax.random.fold_in(key, 13)
    columns = jnp.arange(D, dtype=jnp.float32) / D
    base = jax.random.normal(key, (D, D), jnp.float32)
    spread = 0.6 + 1.2 * columns
    return (base * spread[None, :] * D ** (-0.5)).astype(jnp.bfloat16)


def draw_query_gain(key, part):
    key = jax.random.fold_in(key, 21)
    columns = (jnp.arange(D, dtype=jnp.float32) + 0.5) / D
    noise = jnp.clip(0.1 * jax.random.normal(key, (D,), jnp.float32), -0.3, 0.3)
    return (1.5 / (0.6 + 1.2 * columns) * (1.0 + noise)).astype(jnp.bfloat16)


def draw_key_gain(key, part):
    key = jax.random.fold_in(key, 23)
    columns = (jnp.arange(D, dtype=jnp.float32) + 0.5) / D
    noise = jnp.clip(0.1 * jax.random.normal(key, (D,), jnp.float32), -0.3, 0.3)
    return (1.5 / (0.6 + 1.2 * columns) * (1.0 + noise)).astype(jnp.bfloat16)


def block_scale(rng, dims, cuts, low, high):
    loudness, own = 1.0, jax.random.fold_in(rng, 6)
    for dim, shards_of in cuts:
        draws = jnp.exp(jax.random.uniform(jax.random.fold_in(own, dim), (shards_of,), jnp.float32, low / len(cuts), high / len(cuts)))
        loudness = loudness * jnp.repeat(draws, dims[dim] // shards_of).reshape([-1 if axis == dim else 1 for axis in range(len(dims))])
    return loudness


def gaussian(key, extent, scale, reach, split=(), kind=jnp.bfloat16):
    values = scale * jax.random.normal(key, extent, jnp.float32)
    if split:
        values = values * block_scale(key, extent, split, -0.22, 0.18)
    return jnp.clip(values, -reach, reach).astype(kind)


def setup_inputs(seed: int = 0) -> dict:
    key_of = jax.random.split(jax.random.key(seed), 15)
    layer_input = gaussian(key_of[0], (TOKENS, D), 1.0, 6.0, ((0, 32),))
    segments = draw_segments(jax.random.fold_in(key_of[14], 71), 0)
    w_query = draw_w_query(jax.random.fold_in(key_of[14], 71), 0)
    w_key = draw_w_key(jax.random.fold_in(key_of[14], 71), 0)
    w_value = gaussian(key_of[4], (D, D), D ** -0.5, 0.125, ((0, 4), (1, 8)))
    w_out = gaussian(key_of[5], (D, D), D ** -0.5, 0.125, ((0, 8), (1, 4)))
    query_gain = draw_query_gain(jax.random.fold_in(key_of[14], 71), 0)
    key_gain = draw_key_gain(jax.random.fold_in(key_of[14], 71), 0)
    attn_gain = jnp.clip(1.0 + 0.15 * jax.random.normal(key_of[8], (D,), jnp.float32), 0.25, 1.75).astype(jnp.bfloat16)
    w_gate = gaussian(key_of[9], (D, FF), D ** -0.5, 0.125, ((0, 4), (1, 8)))
    w_up = gaussian(key_of[10], (D, FF), D ** -0.5, 0.125, ((0, 4), (1, 8)))
    w_down = gaussian(key_of[11], (FF, D), FF ** -0.5, 0.0625, ((0, 8), (1, 4)))
    mlp_gain = jnp.clip(1.0 + 0.15 * jax.random.normal(key_of[12], (D,), jnp.float32), 0.25, 1.75).astype(jnp.bfloat16)
    cotangent = gaussian(key_of[13], (TOKENS, D), 1.0, 6.0, ((0, 32),))
    return dict(layer_input=layer_input, segments=segments, w_query=w_query, w_key=w_key, w_value=w_value, w_out=w_out, query_gain=query_gain, key_gain=key_gain, attn_gain=attn_gain, w_gate=w_gate, w_up=w_up, w_down=w_down, mlp_gain=mlp_gain, cotangent=cotangent)


EPS = 1e-06
THETA = 500000.0
MASKED = -1e+30

@jax.custom_vjp
def low(v):
    return lax.optimization_barrier(v.astype(jnp.bfloat16)).astype(jnp.float32)

@jax.custom_vjp
def low_back(v):
    return v

def low_keep(v):
    return (low(v), None)

def low_pass(kept, grad):
    return (grad,)

def back_keep(v):
    return (v, None)

def back_low(kept, grad):
    return (low(grad),)
low.defvjp(low_keep, low_pass)
low_back.defvjp(back_keep, back_low)

def rms_norm(values):
    return values * lax.rsqrt(lax.optimization_barrier(jnp.mean(values * values, axis=-1, keepdims=True)) + EPS)

def doc_positions(segments):
    token_index = jnp.arange(segments.shape[0], dtype=jnp.int32)
    change = jnp.concatenate([jnp.ones((1,), dtype=bool), segments[1:] != segments[:-1]])
    first_index = lax.cummax(jnp.where(change, token_index, 0).astype(jnp.int32), axis=0)
    return token_index - first_index

def rotate(values, places, sign):
    half = values.shape[-1] // 2
    freqs = THETA ** (-(jnp.arange(half, dtype=jnp.float32) * 2.0) / values.shape[-1])
    angle = places.astype(jnp.float32)[:, None] * freqs[None, :]
    cosine = jnp.cos(angle)[:, None, :]
    sine = sign * jnp.sin(angle)[:, None, :]
    first_half = values[..., :half]
    second_half = values[..., half:]
    return jnp.concatenate([first_half * cosine - second_half * sine, second_half * cosine + first_half * sine], axis=-1)

def attention(query_vectors, key_vectors, value_vectors, segments):
    seq_len = query_vectors.shape[0]
    block_rows = min(512, seq_len)
    head_size = query_vectors.shape[-1]
    token_index = jnp.arange(seq_len, dtype=jnp.int32)

    def one_block(block_index):
        offset = block_index * block_rows
        query_block = lax.dynamic_slice_in_dim(query_vectors, offset, block_rows, 0)
        seg_block = lax.dynamic_slice_in_dim(segments, offset, block_rows, 0)
        row_index = offset + jnp.arange(block_rows, dtype=jnp.int32)
        scores = jnp.einsum('qhd,khd->hqk', query_block, key_vectors, precision=lax.Precision.HIGHEST) * head_size ** (-0.5)
        scores = low_back(scores)
        allowed = (seg_block[:, None] == segments[None, :]) & (row_index[:, None] >= token_index[None, :])
        scores = jnp.where(allowed[None], scores, MASKED)
        row_max = lax.optimization_barrier(jnp.max(scores, axis=-1, keepdims=True))
        exp_scores = jnp.exp(scores - row_max)
        attn_probs = low(exp_scores / lax.optimization_barrier(jnp.sum(exp_scores, axis=-1, keepdims=True)))
        return jnp.einsum('hqk,khd->qhd', attn_probs, value_vectors, precision=lax.Precision.HIGHEST)
    blocks = lax.map(jax.checkpoint(one_block), jnp.arange(seq_len // block_rows, dtype=jnp.int32))
    return blocks.reshape(seq_len, -1)

def block_forward(layer_input, w_query, w_key, w_value, w_out, query_gain, key_gain, attn_gain, w_gate, w_up, w_down, mlp_gain, segments):
    highest = lax.Precision.HIGHEST
    seq_len = layer_input.shape[0]
    head_size = D // HEADS
    query_proj = low_back(jnp.dot(layer_input, w_query, precision=highest))
    key_proj = low_back(jnp.dot(layer_input, w_key, precision=highest))
    value_proj = low(low_back(jnp.dot(layer_input, w_value, precision=highest)))
    places = doc_positions(segments)
    query_vectors = low(rotate((rms_norm(query_proj) * query_gain).reshape(seq_len, HEADS, head_size), places, 1.0))
    key_vectors = low(rotate((rms_norm(key_proj) * key_gain).reshape(seq_len, HEADS, head_size), places, 1.0))
    value_vectors = value_proj.reshape(seq_len, HEADS, head_size)
    attn_out = low(low_back(attention(query_vectors, key_vectors, value_vectors, segments)))
    out_proj = low_back(jnp.dot(attn_out, w_out, precision=highest))
    hidden = layer_input + rms_norm(out_proj) * attn_gain
    hidden_low = low(hidden)
    gate = low_back(jnp.dot(hidden_low, w_gate, precision=highest))
    up_val = low_back(jnp.dot(hidden_low, w_up, precision=highest))
    activated = low(jax.nn.silu(gate) * up_val)
    mlp_out = low_back(jnp.dot(activated, w_down, precision=highest))
    return hidden + rms_norm(mlp_out) * mlp_gain

def to_float(array):
    return array.astype(jnp.float32)

def reference(layer_input, segments, w_query, w_key, w_value, w_out, query_gain, key_gain, attn_gain, w_gate, w_up, w_down, mlp_gain, cotangent):
    params = tuple((to_float(weight) for weight in (w_query, w_key, w_value, w_out, query_gain, key_gain, attn_gain, w_gate, w_up, w_down, mlp_gain)))
    groups = TOKENS // SEQ
    inputs = to_float(layer_input).reshape(groups, SEQ, D)
    seg_groups = segments.reshape(groups, SEQ)
    cot_groups = to_float(cotangent).reshape(groups, SEQ, D)

    def one_group(running, item):
        group_input, group_seg, group_cot = item

        def forward(inner, *weights):
            return block_forward(inner, *weights, group_seg)
        result, pullback = jax.vjp(forward, group_input, *params)
        grads = pullback(group_cot)
        running = tuple((total + part for total, part in zip(running, grads[1:])))
        return (running, (result, grads[0]))
    zeros = tuple((jnp.zeros_like(weight) for weight in params))
    totals, (results, input_grads) = lax.scan(one_group, zeros, (inputs, seg_groups, cot_groups))
    return (results.reshape(TOKENS, D).astype(jnp.bfloat16), input_grads.reshape(TOKENS, D).astype(jnp.bfloat16), totals[0], totals[1], totals[2], totals[3], totals[4], totals[5], totals[6], totals[7], totals[8], totals[9], totals[10])
```

```python
import functools

import jax
import jax.numpy as jnp
from jax import lax
from jax.experimental import pallas as pl
from jax.experimental.pallas import tpu as pltpu
from jax.sharding import PartitionSpec as P

HEADS = 16


EPS = 1e-06
THETA = 500000.0
MASKED = -1e30
LOG2E = 1.4426950408889634
BOTH = ("row", "col")
MESH = pl.DeviceIdType.MESH


class Plan:
    def __init__(self, mesh):
        self.rows, self.cols = mesh.shape["row"], mesh.shape["col"]
        self.half = self.rows // 2
        self.across = self.cols // 2
        self.places = [
            (zhi, rest, xx, core)
            for zhi in range(2)
            for rest in range(self.half)
            for xx in range(self.across)
            for core in range(2)
        ]
        self.token_groups = [
            [self.device(zhi, rest, xx, core) for core in range(2) for rest in range(self.half)]
            for xx in range(self.across)
            for zhi in range(2)
        ]

    def device(self, zhi, rest, xx, core):
        return (zhi * self.half + rest) * self.cols + xx * 2 + core

    def here(self):
        row, col = lax.axis_index("row"), lax.axis_index("col")
        return row // self.half, row % self.half, col // 2, col % 2

    def same(self):
        zhi, _, _, core = self.here()
        return zhi == core

    def block(self):
        _, rest, _, core = self.here()
        return core * self.half + rest

    def send(self, value, target):
        pairs = []
        for place in self.places:
            to = target(*place)
            if to is not None:
                pairs.append((self.device(*place), self.device(*to)))
        return lax.ppermute(value, BOTH, pairs)

    def swap(self, value):
        moved = self.send(
            value,
            lambda zhi, rest, xx, core: None if zhi == core else (core, rest, xx, zhi),
        )
        return jnp.where(self.same(), value, moved)

    def partner(self, value, flip):
        def target(zhi, rest, xx, core):
            to = (core * self.half + rest) ^ flip
            return zhi, to % self.half, xx, to // self.half

        return self.send(value, target)

    def token_gather(self, value):
        return lax.all_gather(
            value, BOTH, axis=0, tiled=True, axis_index_groups=self.token_groups
        )

    def token_sum(self, value):
        flip = 1
        while flip < self.rows:
            value = value + self.partner(value, flip)
            flip *= 2
        return value

    def weight_pair(self, value):
        def outward(zhi, rest, xx, core):
            return (1 - zhi, rest, xx, core) if zhi == core else (zhi, rest, xx, 1 - core)

        def over(zhi, rest, xx, core):
            return None if zhi == core else (1 - zhi, rest, xx, 1 - core)

        first = self.send(value, outward)
        second = self.send(value, over)
        same = self.same()
        return jnp.where(same, value, first), jnp.where(same, first, second)

    def weight_pieces(self, pair):
        _, _, xx, core = self.here()
        pieces = []
        for flip in range(self.across):
            for j, part in enumerate(pair):
                if flip:
                    part = self.send(part, lambda z, r, x, c: (z, r, x ^ flip, c))
                pieces.append(((xx ^ flip) * 2 + (core ^ j), part))
        return pieces

    def weight_exchange(self, value, axis):
        xx = self.here()[2]
        size = value.shape[axis] // self.across
        received = []
        for step in range(1, self.across):
            part = lax.dynamic_slice_in_dim(value, (xx + step) % self.across * size, size, axis)
            received.append(
                self.send(part, lambda z, r, x, c: (z, r, (x + step) % self.across, c))
            )
        return jnp.stack(received)

    def weight_sum(self, value, received, axis):
        size = value.shape[axis] // self.across
        total = lax.dynamic_slice_in_dim(value, self.here()[2] * size, size, axis)
        total = total.astype(jnp.float32)
        for step in range(self.across - 1):
            total = total + received[step].astype(jnp.float32)
        return total.astype(jnp.bfloat16)

    def weight_send(self, total, axis):
        core = self.here()[3]
        size = total.shape[axis] // 2
        near = lax.dynamic_slice_in_dim(total, core * size, size, axis)
        far = lax.dynamic_slice_in_dim(total, (1 - core) * size, size, axis)
        same = self.same()

        def outward(zhi, rest, xx, core):
            return (zhi, rest, xx, 1 - core) if zhi == core else (1 - zhi, rest, xx, core)

        def over(zhi, rest, xx, core):
            return None if zhi == core else (1 - zhi, rest, xx, 1 - core)

        first = self.send(jnp.where(same, far, near), outward)
        second = self.send(far, over)
        return jnp.where(same, near, second).astype(jnp.float32) + first.astype(jnp.float32)


def join(shape, pieces):
    whole = jnp.zeros(shape, pieces[0][2].dtype)
    for row, col, piece in pieces:
        whole = lax.dynamic_update_slice(whole, piece, (row, col))
    return whole


def after(value, *others):
    return lax.optimization_barrier((value, *others))[0]


def contract_rows(left, right):
    return lax.dot_general(
        left, right, (((0,), (0,)), ((), ())), preferred_element_type=jnp.float32
    )


def contract_cols(left, right):
    return lax.dot_general(
        left, right, (((1,), (1,)), ((), ())), preferred_element_type=jnp.float32
    )


def position(plan):
    row, col = lax.axis_index("row"), lax.axis_index("col")
    zhi, rest, core = row // plan.half, row % plan.half, col % 2
    return zhi, rest, col - core, core


def remote(source, target, send_sem, recv_sem, row, col):
    return pltpu.make_async_remote_copy(
        src_ref=source,
        dst_ref=target,
        send_sem=send_sem,
        recv_sem=recv_sem,
        device_id=(row, col),
        device_id_type=MESH,
    )


def gather_kernel(plan, own, weight, out, weights, *sems):
    have_sem, swap_sem, send_sem, recv_sem, near_sem, near_recv_sem = sems[:6]
    block_sem, block_recv_sem, side_sem, side_recv_sem = sems[6:]
    half, across = plan.half, plan.across
    zhi, rest, base, core = position(plan)
    xx = base // 2
    row, col = zhi * half + rest, base + core
    far_row, near_col = (1 - zhi) * half + rest, base + 1 - core
    rows = own.shape[0]
    part = rows // 2
    depth = weight.shape[0]
    moved, stays = zhi != core, zhi == core

    barrier = pltpu.get_barrier_semaphore()
    greeted = [(row, near_col), (far_row, col), (far_row, near_col)]
    greeted += [(zhi * half + (rest + step) % half, col) for step in range(1, half)]
    greeted += [(row, (xx + step) % across * 2 + core) for step in range(1, across)]
    for device in greeted:
        pl.semaphore_signal(barrier, 1, device_id=device, device_id_type=MESH)
    pl.semaphore_wait(barrier, len(greeted))

    def lines(block, h):
        return pl.ds(pl.multiple_of(block * rows + h * part, part), part)

    def entry_near(h):
        source = own.at[pl.ds(h * part, part)]
        return pltpu.make_async_copy(
            source, out.at[lines(core * half + rest, h)], have_sem.at[h]
        )

    def entry_far(h):
        return remote(
            own.at[pl.ds(h * part, part)],
            out.at[lines(zhi * half + rest, h)],
            swap_sem.at[h],
            have_sem.at[h],
            far_row,
            near_col,
        )

    def sibling(step, h):
        at = out.at[lines(core * half + (rest + half - step) % half, h)]
        return remote(
            at, at, near_sem.at[step, h], near_recv_sem.at[step, h], row, near_col
        )

    def outward(step, h):
        at = out.at[lines(core * half + rest, h)]
        chip = zhi * half + (rest + step) % half
        return remote(at, at, send_sem.at[step - 1, h], recv_sem.at[step - 1, h], chip, col)

    def place(other, j):
        return pl.ds(pl.multiple_of((other * 2 + j) * depth, depth), depth)

    def block_keep():
        return pltpu.make_async_copy(
            weight, weights.at[place(xx, core)], block_recv_sem.at[core]
        )

    def block_send(index, to_row, to_col):
        return remote(
            weight,
            weights.at[place(xx, core)],
            block_sem.at[index],
            block_recv_sem.at[core],
            to_row,
            to_col,
        )

    def side(step, j):
        at = weights.at[place(xx, j)]
        other = (xx + step) % across * 2 + core
        return remote(
            at, at, side_sem.at[step - 1, j], side_recv_sem.at[step - 1, j], row, other
        )

    @pl.when(moved)
    def _():
        for h in range(2):
            entry_far(h).start()
        block_send(0, row, near_col).start()
        block_send(1, far_row, near_col).start()

    @pl.when(stays)
    def _():
        for h in range(2):
            entry_near(h).start()
        block_keep().start()
        block_send(0, far_row, col).start()

    for h in range(2):

        @pl.when(moved)
        def _():
            entry_far(h).wait_recv()

        @pl.when(stays)
        def _():
            entry_near(h).wait()

        for step in range(1, half):
            outward(step, h).start()
        sibling(0, h).start()
        if h == 0:
            for j in range(2):
                pltpu.make_async_copy(weight, weights.at[place(xx, j)], block_recv_sem.at[j]).wait()
                for step in range(1, across):
                    side(step, j).start()
    for h in range(2):
        for step in range(1, half):
            outward(step, h).wait_recv()
            sibling(step, h).start()
    for h in range(2):
        for step in range(half):
            sibling(step, h).wait()
        for step in range(1, half):
            outward(step, h).wait_send()
    for j in range(2):
        for step in range(1, across):
            side(step, j).wait()

    @pl.when(moved)
    def _():
        for h in range(2):
            entry_far(h).wait_send()
        block_send(0, row, near_col).wait_send()
        block_send(1, far_row, near_col).wait_send()

    @pl.when(stays)
    def _():
        block_send(0, far_row, col).wait_send()


def swap_gather(plan, own, weight, collective_id):
    half = plan.half
    dma = pltpu.SemaphoreType.DMA
    shape = (own.shape[0] * plan.rows, own.shape[1])
    anywhere = pl.BlockSpec(memory_space=pl.ANY)
    return pl.pallas_call(
        functools.partial(gather_kernel, plan),
        in_specs=[anywhere] * 2,
        out_specs=[anywhere] * 2,
        out_shape=[
            jax.ShapeDtypeStruct(shape, own.dtype),
            jax.ShapeDtypeStruct((weight.shape[0] * plan.cols, weight.shape[1]), weight.dtype),
        ],
        scratch_shapes=[
            dma((2,)),
            dma((2,)),
            dma((half - 1, 2)),
            dma((half - 1, 2)),
            dma((half, 2)),
            dma((half, 2)),
            dma((2,)),
            dma((2,)),
            dma((plan.across - 1, 2)),
            dma((plan.across - 1, 2)),
        ],
        cost_estimate=pl.CostEstimate(
            flops=0, bytes_accessed=20 * shape[0] * shape[1], transcendentals=0
        ),
        compiler_params=pltpu.CompilerParams(collective_id=collective_id, has_side_effects=True),
    )(own, weight)


def scatter_kernel(plan, parts, axes, turned, last, *refs):
    half, across, count = plan.half, plan.across, len(axes)
    lefts, weight, refs = refs[:parts], refs[parts], refs[parts + 1 :]
    grads, refs = refs[:count], refs[count:]
    if last:
        residual, refs = refs[0], refs[1:]
    out, blocks, refs = refs[0], refs[1 : count + 1], refs[count + 1 :]
    if last:
        sums, refs = refs[0], refs[1:]
    loaded, near_out, near_in, far_out, far_in = refs[:5]
    load_sem, near_sem, near_recv_sem, far_sem, far_recv_sem, block_sem, block_recv_sem = refs[5:12]
    refs = refs[12:]
    zhi, rest, base, core = position(plan)
    xx = base // 2
    row, col = zhi * half + rest, base + core
    far_row, near_col = (1 - zhi) * half + rest, base + 1 - core
    moved, stays = zhi != core, zhi == core
    part, width = near_out.shape[1:]
    rows = 2 * part
    tile = min(512, width)

    barrier = pltpu.get_barrier_semaphore()
    greeted = [(row, near_col)]
    greeted += [(zhi * half + (rest + step) % half, col) for step in range(1, half)]
    if count:
        greeted += [(row, (xx + step) % across * 2 + core) for step in range(1, across)]
    if last:
        greeted += [(far_row, col), (far_row, near_col)]
    for device in greeted:
        pl.semaphore_signal(barrier, 1, device_id=device, device_id_type=MESH)

    def block(index, step):
        grad, axis = grads[index], axes[index]
        other = (xx + step) % across
        size = grad.shape[axis] // across
        at = pl.ds(pl.multiple_of(other * size, size), size)
        return remote(
            grad.at[at] if axis == 0 else grad.at[:, at],
            blocks[index].at[step - 1],
            block_sem.at[index, step - 1],
            block_recv_sem.at[index, step - 1],
            row,
            other * 2 + core,
        )

    def load(unit, whose, slot):
        h, step = unit // half, half - 1 - unit % half
        side = (1 - core) if whose == 0 else core
        index = side * half + (rest + step) % half
        target, sem = loaded.at[slot, whose], load_sem.at[slot, whose]
        if parts == 1:
            at = pl.ds(pl.multiple_of(index * rows + h * part, part), part)
            return [(None, pltpu.make_async_copy(lefts[0].at[at], target, sem))]
        at = pl.ds(pl.multiple_of(index * part, part), part)
        return [
            (h == k, pltpu.make_async_copy(lefts[k].at[at], target, sem)) for k in range(2)
        ]

    def start(copies):
        for when, copy in copies:
            if when is None:
                copy.start()
            else:
                pl.when(when)(copy.start)

    def near(unit, slot):
        return remote(
            near_out.at[slot],
            near_in.at[unit],
            near_sem.at[unit],
            near_recv_sem.at[unit],
            row,
            near_col,
        )

    def far(unit):
        step = half - 1 - unit % half
        chip = zhi * half + (rest + step) % half
        return remote(
            far_out.at[unit], far_in.at[unit], far_sem.at[unit], far_recv_sem.at[unit], chip, col
        )

    def product(left, cols):
        if turned:
            return contract_cols(left, weight[cols, :])
        return jnp.dot(left, weight[:, cols], preferred_element_type=jnp.float32)

    def columns(n):
        return pl.ds(pl.multiple_of(n * tile, tile), tile)

    start(load(0, 0, 0))
    pl.semaphore_wait(barrier, len(greeted))
    for index in range(count):
        for step in range(1, across):
            block(index, step).start()

    def body(unit, carry):
        slot = unit % 2
        before = unit - 1

        @pl.when(unit + 1 < 2 * half)
        def _():
            start(load(unit + 1, 0, 1 - slot))

        @pl.when(unit < 2 * half)
        def _():
            start(load(unit, 1, 1 - slot))
            load(unit, 0, slot)[0][1].wait()

            @pl.when(unit >= 2)
            def _():
                near(unit - 2, slot).wait_send()

            @pl.loop(0, width // tile)
            def _(n):
                value = product(loaded[slot, 0], columns(n))
                near_out[slot, :, columns(n)] = value.astype(near_out.dtype)

            near(unit, slot).start()

        @pl.when(unit >= 1)
        def _():
            load(before, 1, slot)[0][1].wait()
            near(before, 1 - slot).wait_recv()

            @pl.loop(0, width // tile)
            def _(n):
                value = product(loaded[slot, 1], columns(n))
                value = value + near_in[before, :, columns(n)].astype(jnp.float32)
                far_out[before, :, columns(n)] = value.astype(far_out.dtype)

            @pl.when(before % half < half - 1)
            def _():
                far(before).start()

        return carry

    lax.fori_loop(0, 2 * half + 1, body, 0)

    def total(h):
        for step in range(half - 1):
            far(h * half + step).wait_recv()
        value = far_out[h * half + half - 1].astype(jnp.float32)
        for step in range(half - 1):
            value = value + far_in[h * half + step].astype(jnp.float32)
        return value

    if last:
        finish_sum = finish(
            (zhi, rest, xx, core), (row, col, far_row, near_col), grads, blocks, block, sums, refs
        )
        final, final_sem, final_recv_sem = refs[:3]

        def swap_far(h):
            return remote(
                final.at[h],
                out.at[pl.ds(h * part, part)],
                final_sem.at[h],
                final_recv_sem.at[h],
                far_row,
                near_col,
            )

        def swap_near(h):
            return pltpu.make_async_copy(
                final.at[h], out.at[pl.ds(h * part, part)], final_recv_sem.at[h]
            )

        for h in range(2):
            value = total(h) + residual[h * part : (h + 1) * part, :]
            final[h] = value.astype(final.dtype)

            @pl.when(moved)
            def _():
                swap_far(h).start()

            @pl.when(stays)
            def _():
                swap_near(h).start()

            if h == 0:
                finish_sum()

        for h in range(2):

            @pl.when(moved)
            def _():
                swap_far(h).wait()

            @pl.when(stays)
            def _():
                swap_near(h).wait()

    else:
        for h in range(2):
            out[h * part : (h + 1) * part, :] = total(h)
        for index in range(count):
            for step in range(1, across):
                block(index, step).wait_recv()
    for h in range(2):
        for unit in range(h * half, h * half + half - 1):
            far(unit).wait_send()
    for unit in range(2 * half - 2, 2 * half):
        near(unit, unit % 2).wait_send()
    for index in range(count):
        for step in range(1, across):
            block(index, step).wait_send()


def finish(place, devices, grads, blocks, block, sums, refs):
    zhi, _, xx, core = place
    row, col, far_row, near_col = devices
    grad, blocks = grads[0], blocks[0]
    mine, others, pair, landed, mine_sem, pair_sem, landed_sem = refs[3:]
    size = pair.shape[1]
    across = blocks.shape[0] + 1
    own = pltpu.make_async_copy(
        grad.at[pl.ds(pl.multiple_of(xx * 2 * size, size), 2 * size)], mine, mine_sem.at[0]
    )
    rest = [
        pltpu.make_async_copy(blocks.at[step], others.at[step], mine_sem.at[step + 1])
        for step in range(across - 1)
    ]

    def give(index, slot, to_row, to_col, to_slot):
        return remote(
            pair.at[slot],
            landed.at[to_slot],
            pair_sem.at[index],
            landed_sem.at[to_slot],
            to_row,
            to_col,
        )

    to_sibling = give(0, 1 - core, row, near_col, 0)
    to_same = give(0, core, far_row, col, 0)
    to_cross = give(1, 1 - core, far_row, near_col, 1)
    own.start()

    def run():
        for step in range(1, across):
            block(0, step).wait_recv()
            rest[step - 1].start()
        own.wait()
        for copy in rest:
            copy.wait()
        value = mine[...].astype(jnp.float32)
        for step in range(across - 1):
            value = value + others[step].astype(jnp.float32)
        pair[0] = value[:size].astype(pair.dtype)
        pair[1] = value[size:].astype(pair.dtype)

        @pl.when(zhi == core)
        def _():
            to_sibling.start()
            to_sibling.wait_send()
            give(0, core, far_row, col, 0).wait_recv()
            sums[...] = pair[core].astype(jnp.float32) + landed[0].astype(jnp.float32)

        @pl.when(zhi != core)
        def _():
            to_same.start()
            to_cross.start()
            to_same.wait_send()
            to_cross.wait_send()
            to_same.wait_recv()
            to_cross.wait_recv()
            sums[...] = landed[1].astype(jnp.float32) + landed[0].astype(jnp.float32)

    return run


def cut(shape, axis, pieces):
    return tuple(size // pieces if dim == axis else size for dim, size in enumerate(shape))


def multiply_scatter(plan, lefts, weight, turned, collective_id, grads=(), axes=(), residual=None):
    half, across, count = plan.half, plan.across, len(grads)
    depth = lefts[0].shape[1]
    width = weight.shape[0 if turned else 1]
    rows = sum(left.shape[0] for left in lefts) // plan.rows
    part = rows // 2
    low = jnp.bfloat16
    dma = pltpu.SemaphoreType.DMA
    anywhere = pl.BlockSpec(memory_space=pl.ANY)
    inside = pl.BlockSpec(memory_space=pltpu.VMEM)
    last = residual is not None
    in_specs = [anywhere] * len(lefts) + [inside] + [anywhere] * count + [inside] * last
    out_specs = [anywhere if last else inside] + [anywhere] * count + [inside] * last
    out_shape = [jax.ShapeDtypeStruct((rows, width), low if last else jnp.float32)]
    out_shape += [
        jax.ShapeDtypeStruct((across - 1, *cut(grad.shape, axis, across)), low)
        for grad, axis in zip(grads, axes, strict=True)
    ]
    scratch = [
        pltpu.VMEM((2, 2, part, depth), low),
        pltpu.VMEM((2, part, width), low),
        pltpu.VMEM((2 * half, part, width), low),
        pltpu.VMEM((2 * half, part, width), low),
        pltpu.VMEM((2 * half, part, width), low),
        dma((2, 2)),
        dma((2 * half,)),
        dma((2 * half,)),
        dma((2 * half,)),
        dma((2 * half,)),
        dma((max(count, 1), across - 1)),
        dma((max(count, 1), across - 1)),
    ]
    if last:
        size, wide = grads[0].shape[0] // plan.cols, grads[0].shape[1]
        out_shape.append(jax.ShapeDtypeStruct((size, wide), jnp.float32))
        scratch += [
            pltpu.VMEM((2, part, width), low),
            dma((2,)),
            dma((2,)),
            pltpu.VMEM((2 * size, wide), low),
            pltpu.VMEM((across - 1, 2 * size, wide), low),
            pltpu.VMEM((2, size, wide), low),
            pltpu.VMEM((2, size, wide), low),
            dma((across,)),
            dma((2,)),
            dma((2,)),
        ]
    return pl.pallas_call(
        functools.partial(scatter_kernel, plan, len(lefts), axes, turned, last),
        in_specs=in_specs,
        out_specs=out_specs,
        out_shape=out_shape,
        scratch_shapes=scratch,
        cost_estimate=pl.CostEstimate(
            flops=2 * rows * plan.rows * depth * width,
            bytes_accessed=20 * rows * plan.rows * width,
            transcendentals=0,
        ),
        compiler_params=pltpu.CompilerParams(
            collective_id=collective_id, has_side_effects=True, vmem_limit_bytes=58 * 2**20
        ),
    )(*lefts, weight, *grads, *([residual] if last else []))


def full(rows, width):
    return pl.BlockSpec((rows, width), lambda *_: (0, 0))


def turn(values, cosine, sine):
    return values * cosine + pltpu.roll(values, values.shape[-1] // 2, 1) * sine


def column(row_vector, width):
    return jnp.transpose(jnp.broadcast_to(row_vector, (width, row_vector.shape[1])))


def prepare_kernel(
    head_size, proj, query_inv, key_inv, cosine, sine, query_gain, key_gain, query, key, value
):
    width = query.shape[1]
    turns = (cosine[...], sine[...])
    for source, inv, gain, target in (
        (0, query_inv, query_gain, query),
        (width, key_inv, key_gain, key),
    ):
        factor = column(inv[...], head_size)
        for start in range(0, width, head_size):
            part = proj[:, source + start : source + start + head_size]
            scaled = part * factor * gain[:, start : start + head_size]
            target[:, start : start + head_size] = turn(scaled, *turns).astype(target.dtype)
    value[...] = proj[:, 2 * width :].astype(value.dtype)


def prepare(proj, query_inv, key_inv, cosine, sine, query_gain, key_gain, head_size):
    seq_len, width = proj.shape[0], proj.shape[1] // 3
    rows = min(512, seq_len)
    return pl.pallas_call(
        functools.partial(prepare_kernel, head_size),
        grid=(seq_len // rows,),
        in_specs=[
            pl.BlockSpec((rows, 3 * width), lambda i: (i, 0)),
            pl.BlockSpec((1, rows), lambda i: (0, i)),
            pl.BlockSpec((1, rows), lambda i: (0, i)),
            pl.BlockSpec((rows, head_size), lambda i: (i, 0)),
            pl.BlockSpec((rows, head_size), lambda i: (i, 0)),
            full(1, width),
            full(1, width),
        ],
        out_specs=[pl.BlockSpec((rows, width), lambda i: (i, 0))] * 3,
        out_shape=[jax.ShapeDtypeStruct((seq_len, width), jnp.bfloat16)] * 3,
        cost_estimate=pl.CostEstimate(
            flops=10 * seq_len * width, bytes_accessed=seq_len * width * 20, transcendentals=0
        ),
        compiler_params=pltpu.CompilerParams(vmem_limit_bytes=40 * 2**20),
    )(proj, query_inv, key_inv, cosine, sine, query_gain, key_gain)


def allowed(first, key_block, query_block, key_rows, query_rows):
    key_index = key_block * key_rows + lax.broadcasted_iota(
        jnp.int32, (key_rows, query_rows), 0
    )
    query_index = query_block * query_rows + lax.broadcasted_iota(
        jnp.int32, (key_rows, query_rows), 1
    )
    return (key_index <= query_index) & (key_index >= first)


def attend_kernel(rows, low, first, query, key, value, *refs):
    out, log_sum = refs[-2:]
    step = pl.program_id(1)
    head_size = query.shape[1]
    factor = LOG2E * head_size**-0.5
    queries = query[...]
    starts = first[...]

    def one(index, carry):
        top, total, acc = carry
        at = pl.ds(pl.multiple_of(index * rows, rows), rows)
        scores = contract_cols(key[at, :], queries) * factor
        scores = jnp.where(allowed(starts, index, step, rows, rows), scores, MASKED)
        new_top = jnp.maximum(top, jnp.max(scores, axis=0, keepdims=True))
        probs = jnp.exp2(scores - new_top)
        fade = jnp.exp2(top - new_top)
        total = total * fade + jnp.sum(probs, axis=0, keepdims=True)
        acc = acc * fade + contract_rows(value[at, :], probs.astype(jnp.bfloat16))
        return new_top, total, acc

    top, total, acc = lax.fori_loop(
        low[step],
        step + 1,
        one,
        (
            jnp.full((1, rows), MASKED, jnp.float32),
            jnp.zeros((1, rows), jnp.float32),
            jnp.zeros((head_size, rows), jnp.float32),
        ),
    )
    out[...] = jnp.transpose(acc / total).astype(out.dtype)
    log_sum[0] = top + jnp.log2(total)


def attend(low, first, query, key, value, head_size, rows, more):
    seq_len, width = query.shape
    heads = width // head_size
    whole = pl.BlockSpec((seq_len, head_size), lambda h, i, *_: (0, h))
    block = pl.BlockSpec((rows, head_size), lambda h, i, *_: (i, h))
    return pl.pallas_call(
        functools.partial(attend_kernel, rows),
        grid_spec=pltpu.PrefetchScalarGridSpec(
            num_scalar_prefetch=1,
            grid=(heads, seq_len // rows),
            in_specs=[
                pl.BlockSpec((1, rows), lambda h, i, *_: (0, i)),
                block,
                whole,
                whole,
            ]
            + [pl.BlockSpec(memory_space=pl.ANY)] * len(more),
            out_specs=[block, pl.BlockSpec((1, 1, rows), lambda h, i, *_: (h, 0, i))],
        ),
        out_shape=[
            jax.ShapeDtypeStruct((seq_len, width), jnp.bfloat16),
            jax.ShapeDtypeStruct((heads, 1, seq_len), jnp.float32),
        ],
        cost_estimate=pl.CostEstimate(
            flops=seq_len * seq_len * width, bytes_accessed=seq_len * width * 8, transcendentals=0
        ),
        compiler_params=pltpu.CompilerParams(vmem_limit_bytes=40 * 2**20),
    )(low, first, query, key, value, *more)


def attend_back_kernel(
    rows,
    high,
    first,
    query,
    key,
    value,
    out,
    out_grad,
    log_sum,
    query_grad,
    key_grad,
    value_grad,
    delta,
):
    step = pl.program_id(1)
    seq_len, head_size = query.shape
    factor = LOG2E * head_size**-0.5

    @pl.when(step == 0)
    def _():
        query_grad[...] = jnp.zeros_like(query_grad)

        @pl.loop(0, seq_len // rows)
        def _(index):
            at = pl.ds(pl.multiple_of(index * rows, rows), rows)
            product = out_grad[at, :].astype(jnp.float32) * out[at, :].astype(jnp.float32)
            delta[:, at] = jnp.sum(jnp.transpose(product), axis=0, keepdims=True)

    keys = key[...]
    values = value[...]

    def one(index, carry):
        key_acc, value_acc = carry
        at = pl.ds(pl.multiple_of(index * rows, rows), rows)
        queries = query[at, :]
        grads = out_grad[at, :]
        scores = contract_cols(keys, queries) * factor
        mask = allowed(first[:, at], step, index, rows, rows)
        probs = jnp.exp2(jnp.where(mask, scores - log_sum[0, :, at], MASKED))
        value_acc = value_acc + jnp.dot(
            probs.astype(jnp.bfloat16), grads, preferred_element_type=jnp.float32
        )
        prob_grad = contract_cols(values, grads)
        score_grad = (probs * (prob_grad - delta[:, at])).astype(jnp.bfloat16)
        key_acc = key_acc + jnp.dot(score_grad, queries, preferred_element_type=jnp.float32)
        query_grad[at, :] += contract_rows(score_grad, keys)
        return key_acc, value_acc

    zeros = jnp.zeros((rows, head_size), jnp.float32)
    key_acc, value_acc = lax.fori_loop(step, high[step] + 1, one, (zeros, zeros))
    key_grad[...] = key_acc
    value_grad[...] = value_acc.astype(value_grad.dtype)


def attend_back(high, first, query, key, value, out, out_grad, log_sum, head_size, rows):
    seq_len, width = query.shape
    heads = width // head_size
    whole = pl.BlockSpec((seq_len, head_size), lambda h, j, *_: (0, h))
    block = pl.BlockSpec((rows, head_size), lambda h, j, *_: (j, h))
    return pl.pallas_call(
        functools.partial(attend_back_kernel, rows),
        grid_spec=pltpu.PrefetchScalarGridSpec(
            num_scalar_prefetch=1,
            grid=(heads, seq_len // rows),
            in_specs=[
                full(1, seq_len),
                whole,
                block,
                block,
                whole,
                whole,
                pl.BlockSpec((1, 1, seq_len), lambda h, j, *_: (h, 0, 0)),
            ],
            out_specs=[whole, block, block],
            scratch_shapes=[pltpu.VMEM((1, seq_len), jnp.float32)],
        ),
        out_shape=[
            jax.ShapeDtypeStruct((seq_len, width), jnp.float32),
            jax.ShapeDtypeStruct((seq_len, width), jnp.float32),
            jax.ShapeDtypeStruct((seq_len, width), jnp.bfloat16),
        ],
        cost_estimate=pl.CostEstimate(
            flops=3 * seq_len * seq_len * width,
            bytes_accessed=seq_len * width * 20,
            transcendentals=0,
        ),
        compiler_params=pltpu.CompilerParams(vmem_limit_bytes=48 * 2**20),
    )(high, first, query, key, value, out, out_grad, log_sum)


def norm_back_kernel(
    head_size,
    proj,
    query_inv,
    key_inv,
    cosine,
    sine,
    query_gain,
    key_gain,
    query_grad,
    key_grad,
    dots,
    gain_sums,
):
    width = query_grad.shape[1]
    turns = (cosine[...], -sine[...])
    scale = head_size**-0.5

    @pl.when(pl.program_id(0) == 0)
    def _():
        gain_sums[...] = jnp.zeros_like(gain_sums)

    for place, (source, inv, gain, grad) in enumerate(
        ((0, query_inv, query_gain, query_grad), (width, key_inv, key_gain, key_grad))
    ):
        factor = column(inv[...], head_size)
        row_part = None
        for start in range(0, width, head_size):
            cols = slice(start, start + head_size)
            hat = proj[:, source + start : source + start + head_size] * factor
            product = turn(grad[:, cols] * scale, *turns) * hat
            gain_sums[place : place + 1, cols] += jnp.sum(product, axis=0, keepdims=True)
            product = product * gain[:, cols]
            row_part = product if row_part is None else row_part + product
        dots[place : place + 1, :] = jnp.sum(jnp.transpose(row_part), axis=0, keepdims=True)


def norm_back(
    proj, query_inv, key_inv, cosine, sine, query_gain, key_gain, query_grad, key_grad, head_size
):
    seq_len, width = query_grad.shape
    rows = min(512, seq_len)
    wide = pl.BlockSpec((rows, width), lambda i: (i, 0))
    return pl.pallas_call(
        functools.partial(norm_back_kernel, head_size),
        grid=(seq_len // rows,),
        in_specs=[
            pl.BlockSpec((rows, 2 * width), lambda i: (i, 0)),
            pl.BlockSpec((1, rows), lambda i: (0, i)),
            pl.BlockSpec((1, rows), lambda i: (0, i)),
            pl.BlockSpec((rows, head_size), lambda i: (i, 0)),
            pl.BlockSpec((rows, head_size), lambda i: (i, 0)),
            full(1, width),
            full(1, width),
            wide,
            wide,
        ],
        out_specs=[pl.BlockSpec((2, rows), lambda i: (0, i)), full(2, width)],
        out_shape=[
            jax.ShapeDtypeStruct((2, seq_len), jnp.float32),
            jax.ShapeDtypeStruct((2, width), jnp.float32),
        ],
        cost_estimate=pl.CostEstimate(
            flops=20 * seq_len * width, bytes_accessed=seq_len * width * 20, transcendentals=0
        ),
        compiler_params=pltpu.CompilerParams(vmem_limit_bytes=40 * 2**20),
    )(proj, query_inv, key_inv, cosine, sine, query_gain, key_gain, query_grad, key_grad)


def proj_back_kernel(
    head_size,
    features,
    proj,
    query_inv,
    key_inv,
    cosine,
    sine,
    query_gain,
    key_gain,
    query_grad,
    key_grad,
    value_grad,
    dots,
    *rest,
):
    out = rest[-1]
    width = query_grad.shape[1]
    turns = (cosine[...], -sine[...])
    scale = head_size**-0.5
    for place, (source, inv, gain, grad) in enumerate(
        ((0, query_inv, query_gain, query_grad), (width, key_inv, key_gain, key_grad))
    ):
        factor = column(inv[...], head_size)
        mean = column(dots[place : place + 1, :] * (1.0 / features), head_size)
        for start in range(0, width, head_size):
            cols = slice(start, start + head_size)
            at = slice(source + start, source + start + head_size)
            hat = proj[:, at] * factor
            scaled = turn(grad[:, cols] * scale, *turns) * gain[:, cols]
            out[:, at] = (factor * (scaled - hat * mean)).astype(out.dtype)
    out[:, 2 * width :] = value_grad[...]


def proj_back(
    proj,
    query_inv,
    key_inv,
    cosine,
    sine,
    query_gain,
    key_gain,
    query_grad,
    key_grad,
    value_grad,
    dots,
    head_size,
    features,
    more,
):
    seq_len, width = query_grad.shape
    rows = min(512, seq_len)
    wide = pl.BlockSpec((rows, width), lambda i: (i, 0))
    return pl.pallas_call(
        functools.partial(proj_back_kernel, head_size, features),
        grid=(seq_len // rows,),
        in_specs=[
            pl.BlockSpec((rows, 2 * width), lambda i: (i, 0)),
            pl.BlockSpec((1, rows), lambda i: (0, i)),
            pl.BlockSpec((1, rows), lambda i: (0, i)),
            pl.BlockSpec((rows, head_size), lambda i: (i, 0)),
            pl.BlockSpec((rows, head_size), lambda i: (i, 0)),
            full(1, width),
            full(1, width),
            wide,
            wide,
            wide,
            pl.BlockSpec((2, rows), lambda i: (0, i)),
        ]
        + [pl.BlockSpec(memory_space=pl.ANY)] * len(more),
        out_specs=pl.BlockSpec((rows, 3 * width), lambda i: (i, 0)),
        out_shape=jax.ShapeDtypeStruct((seq_len, 3 * width), jnp.bfloat16),
        cost_estimate=pl.CostEstimate(
            flops=20 * seq_len * width, bytes_accessed=seq_len * width * 24, transcendentals=0
        ),
        compiler_params=pltpu.CompilerParams(vmem_limit_bytes=40 * 2**20),
    )(
        proj,
        query_inv,
        key_inv,
        cosine,
        sine,
        query_gain,
        key_gain,
        query_grad,
        key_grad,
        value_grad,
        dots,
        *more,
    )


def body(
    plan,
    layer_input,
    segments,
    w_query,
    w_key,
    w_value,
    w_out,
    query_gain,
    key_gain,
    attn_gain,
    w_gate,
    w_up,
    w_down,
    mlp_gain,
    cotangent,
):
    rows = plan.rows
    mine = plan.block()
    model_width = layer_input.shape[1]
    head_size = model_width // HEADS
    seq_len = segments.shape[0]
    own_tokens = seq_len // rows
    part = own_tokens // 2
    f32 = jnp.float32
    bf16 = jnp.bfloat16
    chunks = range(2)

    def chunk_of(value, k):
        return value[k * part : (k + 1) * part]

    qkv_own = jnp.concatenate([w_query, w_key, w_value], axis=1)
    own_depth, wide = qkv_own.shape
    small_own = jnp.concatenate([query_gain, key_gain, attn_gain, mlp_gain])
    gain_size, post_size = query_gain.shape[0], attn_gain.shape[0]
    cuts = (gain_size, 2 * gain_size, 2 * gain_size + post_size)
    small_size = small_own.shape[0]
    extra = 16

    def lines(vector):
        return jnp.pad(vector, (0, extra * wide - small_size)).reshape(extra, wide)

    own_weight = jnp.concatenate([qkv_own, lines(small_own)], axis=0)
    gathered_x, both = swap_gather(plan, layer_input, own_weight, 1)
    both = both.reshape(plan.cols, own_depth + extra, wide)
    proj_weight = both[:, :own_depth].reshape(-1, wide)
    small = both[:, own_depth:].reshape(plan.cols, extra * wide)[:, :small_size].astype(f32)
    query_scale, key_scale, attn_scale, mlp_scale = (
        value.reshape(1, -1) for value in jnp.split(small, cuts, axis=1)
    )

    own_x = lax.dynamic_slice_in_dim(gathered_x, mine * own_tokens, own_tokens)
    segments = plan.swap(segments)
    gate_pair = plan.weight_pair(after(w_gate, gathered_x))
    out_pair = plan.weight_pair(after(w_out, gathered_x))
    up_pair = plan.weight_pair(after(w_up, gathered_x))
    down_pair = plan.weight_pair(after(w_down, gathered_x))
    ff_width = w_gate.shape[1]

    local_width = wide // 3
    token_index = jnp.arange(seq_len, dtype=jnp.int32)
    change = jnp.concatenate([jnp.ones((1,), dtype=bool), segments[1:] != segments[:-1]])
    first = lax.cummax(jnp.where(change, token_index, 0), axis=0)
    places = (token_index - first).astype(f32)
    lane = jnp.arange(head_size, dtype=jnp.int32)
    half = head_size // 2
    freqs = THETA ** (-((lane % half).astype(f32) * 2.0) / head_size)
    angle = places[:, None] * freqs[None, :]
    cosine = jnp.cos(angle)
    sine = jnp.sin(angle) * jnp.where(lane < half, -1.0, 1.0)[None, :]
    tile = min(512, seq_len)
    low = first[::tile] // tile
    last = token_index[tile - 1 :: tile]
    ends = jnp.min(
        jnp.where(change[None, :] & (token_index[None, :] > last[:, None]), token_index, seq_len),
        axis=1,
    )
    high = (ends - 1) // tile
    first_row = first[None, :]

    proj = jnp.dot(gathered_x, proj_weight, preferred_element_type=f32)
    squares = jnp.stack(
        [
            jnp.sum(proj[:, start : start + local_width] ** 2, axis=-1)
            for start in (0, local_width)
        ]
    )
    invs = lax.rsqrt(plan.token_sum(squares) / model_width + EPS)
    query_inv, key_inv = invs[:1], invs[1:]
    query, key, value = prepare(
        proj, query_inv, key_inv, cosine, sine, query_scale, key_scale, head_size
    )
    attn_out, log_sum = attend(
        low, first_row, query, key, value, head_size, tile, (*gate_pair, *out_pair)
    )
    post_depth = w_out.shape[1]
    out_full = plan.token_gather(
        join(
            (local_width, model_width),
            [(0, c * post_depth, piece) for c, piece in plan.weight_pieces(out_pair)],
        )
    )
    own_cot = plan.swap(after(cotangent, attn_out))

    attn_tokens = jnp.zeros((own_tokens, model_width), bf16)
    for flip in range(rows):
        other = mine ^ flip
        piece = lax.dynamic_slice(attn_out, (other * own_tokens, 0), (own_tokens, local_width))
        if flip:
            piece = plan.partner(piece, flip)
        attn_tokens = lax.dynamic_update_slice(attn_tokens, piece, (0, other * local_width))

    attn_tokens, *up_pair = lax.optimization_barrier((attn_tokens, *up_pair))
    gate_pieces = plan.weight_pieces(gate_pair)
    places, gate_pieces = zip(*gate_pieces, strict=True)
    attn_tokens, *gate_pieces = lax.optimization_barrier((attn_tokens, *gate_pieces))
    gate_pieces = list(zip(places, gate_pieces, strict=True))
    ff_weight = join(
        (model_width, 2 * ff_width),
        [
            (c * own_depth, start, piece)
            for start, pieces in ((0, gate_pieces), (ff_width, plan.weight_pieces(up_pair)))
            for c, piece in pieces
        ],
    )
    down_rows = join(
        (ff_width, model_width),
        [(0, c * post_depth, piece) for c, piece in plan.weight_pieces(down_pair)],
    )

    def normed(value):
        inv = lax.rsqrt(jnp.mean(value * value, axis=-1, keepdims=True) + EPS)
        return inv, value * inv

    def norm_grad(inv, hat, scaled):
        mean = jnp.mean(scaled * hat, axis=-1, keepdims=True)
        return (inv * (scaled - hat * mean)).astype(bf16)

    attn_inv, attn_hat, hidden, gathered_h = [], [], [], []
    for k in chunks:
        out_proj = jnp.dot(chunk_of(attn_tokens, k), out_full, preferred_element_type=f32)
        inv, hat = normed(out_proj)
        attn_inv.append(inv)
        attn_hat.append(hat)
        hidden.append(chunk_of(own_x, k).astype(f32) + hat * attn_scale)
        gathered_h.append(plan.token_gather(hidden[k].astype(bf16)))

    gate, up, activated = [], [], []
    for k in chunks:
        both = jnp.dot(gathered_h[k], ff_weight, preferred_element_type=f32).astype(bf16)
        gate.append(both[:, :ff_width])
        up.append(both[:, ff_width:])
        activated.append((jax.nn.silu(gate[k].astype(f32)) * up[k].astype(f32)).astype(bf16))
    (mlp_out,) = multiply_scatter(plan, activated, down_rows, False, 2)

    outputs, upstream, shard_rows = [], [], []
    mlp_gain_part = 0.0
    for k in chunks:
        inv, hat = normed(chunk_of(mlp_out, k))
        outputs.append((hidden[k] + hat * mlp_scale).astype(bf16))
        upstream.append(chunk_of(own_cot, k).astype(f32))
        mlp_gain_part += jnp.sum(upstream[k] * hat, axis=0)
        shard_rows.append(plan.token_gather(norm_grad(inv, hat, upstream[k] * mlp_scale)))
    layer_output = plan.swap(jnp.concatenate(outputs))

    ff_grad = []
    for k in chunks:
        act_part = contract_cols(shard_rows[k], down_rows)
        gate_val, up_val = gate[k].astype(f32), up[k].astype(f32)
        gate_sigmoid = jax.nn.sigmoid(gate_val)
        gate_grad = act_part * up_val * gate_sigmoid * (1.0 + gate_val * (1.0 - gate_sigmoid))
        up_grad = act_part * gate_val * gate_sigmoid
        ff_grad.append(jnp.concatenate([gate_grad, up_grad], axis=1).astype(bf16))
    down_grad = sum(contract_rows(activated[k], shard_rows[k]) for k in chunks).astype(bf16)
    ff_weight_grad = sum(contract_rows(gathered_h[k], ff_grad[k]) for k in chunks).astype(bf16)
    hidden_grad_mlp, down_blocks, ff_blocks = multiply_scatter(
        plan, ff_grad, ff_weight, True, 3, (down_grad, ff_weight_grad), (1, 0)
    )
    hidden_grad = [upstream[k] + chunk_of(hidden_grad_mlp, k) for k in chunks]
    ff_sum = plan.weight_send(plan.weight_sum(ff_weight_grad, ff_blocks, 0), 0)
    down_sum = plan.weight_send(plan.weight_sum(down_grad, down_blocks, 1), 1)

    attn_gain_part = 0.0
    proj_grads, token_grads = [], []
    for k in chunks:
        attn_gain_part += jnp.sum(hidden_grad[k] * attn_hat[k], axis=0)
        proj_grads.append(norm_grad(attn_inv[k], attn_hat[k], hidden_grad[k] * attn_scale))
        token_grads.append(contract_cols(proj_grads[k], out_full).astype(bf16))
    out_token_grad = jnp.concatenate(token_grads)

    attn_grad = jnp.zeros((seq_len, local_width), bf16)
    for flip in range(rows):
        other = mine ^ flip
        piece = lax.dynamic_slice(
            out_token_grad, (0, other * local_width), (own_tokens, local_width)
        )
        if flip:
            piece = plan.partner(piece, flip)
        attn_grad = lax.dynamic_update_slice(attn_grad, piece, (other * own_tokens, 0))

    out_grad = sum(
        contract_rows(
            attn_out.reshape(rows, 2, part, local_width)[:, k].reshape(-1, local_width),
            plan.token_gather(after(proj_grads[k], attn_grad)),
        )
        for k in chunks
    ).astype(bf16)
    out_sum = plan.weight_sum(out_grad, plan.weight_exchange(out_grad, 1), 1)
    query_grad, key_grad, value_grad = attend_back(
        high, first_row, query, key, value, attn_out, attn_grad, log_sum, head_size, tile
    )
    shared = (proj, query_inv, key_inv, cosine, sine, query_scale, key_scale, query_grad, key_grad)
    dots, gain_sums = norm_back(*shared, head_size)
    dots = plan.token_sum(dots)
    proj_grad_all = proj_back(
        *shared, value_grad, dots, head_size, model_width, (ff_sum, down_sum)
    )
    proj_grad_all = after(proj_grad_all, out_sum)
    proj_weight_grad = contract_rows(gathered_x, proj_grad_all).astype(bf16)
    post_sums = plan.token_sum(jnp.stack([attn_gain_part, mlp_gain_part]))
    small = jnp.concatenate(
        [
            gain_sums[0].reshape(plan.cols, -1),
            gain_sums[1].reshape(plan.cols, -1),
            post_sums[0].reshape(plan.cols, -1),
            post_sums[1].reshape(plan.cols, -1),
        ],
        axis=1,
    )
    small = jnp.pad(small, ((0, 0), (0, extra * wide - small_size)))
    small = small.reshape(plan.cols, extra, wide).astype(bf16)
    stacked = jnp.concatenate(
        [proj_weight_grad.reshape(plan.cols, own_depth, wide), small], axis=1
    )
    stacked = stacked.reshape(-1, wide)
    out_sum = plan.weight_send(out_sum, 1)
    stacked = after(stacked, out_sum)
    input_grad, _, proj_sum = multiply_scatter(
        plan,
        [proj_grad_all],
        proj_weight,
        True,
        4,
        (stacked,),
        (0,),
        jnp.concatenate(hidden_grad),
    )
    small = proj_sum[own_depth:].reshape(-1)[:small_size]
    query_gain_sum, key_gain_sum, attn_gain_sum, mlp_gain_sum = jnp.split(small, cuts)
    proj_sum = proj_sum[:own_depth]
    own_ff = w_gate.shape[1]
    return (
        layer_output,
        input_grad,
        proj_sum[:, :local_width],
        proj_sum[:, local_width : 2 * local_width],
        proj_sum[:, 2 * local_width :],
        out_sum,
        query_gain_sum,
        key_gain_sum,
        attn_gain_sum,
        ff_sum[:, :own_ff],
        ff_sum[:, own_ff:],
        down_sum,
        mlp_gain_sum,
    )


def solution(mesh):
    tokens = P(("col", "row"), None)
    columns = P("col", "row")
    across = P("row", "col")
    vector = P(("row", "col"))
    return jax.shard_map(
        functools.partial(body, Plan(mesh)),
        mesh=mesh,
        in_specs=(
            tokens,
            P("col"),
            columns,
            columns,
            columns,
            across,
            vector,
            vector,
            P("col"),
            columns,
            columns,
            across,
            P("col"),
            tokens,
        ),
        out_specs=(
            tokens,
            tokens,
            columns,
            columns,
            columns,
            across,
            vector,
            vector,
            P("col"),
            columns,
            columns,
            across,
            P("col"),
        ),
        check_vma=False,
    )
```

```python
import functools

import jax
import jax.numpy as jnp
from jax import lax
from jax.experimental import pallas as pl
from jax.experimental.pallas import tpu as pltpu
from jax.sharding import PartitionSpec as P

HEADS = 16


EPS = 1e-06
THETA = 500000.0
MASKED = -1e30
LOG2E = 1.4426950408889634
BOTH = ("row", "col")
MESH = pl.DeviceIdType.MESH


class Plan:
    def __init__(self, mesh):
        self.rows, self.cols = mesh.shape["row"], mesh.shape["col"]
        self.half = self.rows // 2
        self.across = self.cols // 2
        self.places = [
            (zhi, rest, xx, core)
            for zhi in range(2)
            for rest in range(self.half)
            for xx in range(self.across)
            for core in range(2)
        ]
        self.token_groups = [
            [self.device(zhi, rest, xx, core) for core in range(2) for rest in range(self.half)]
            for xx in range(self.across)
            for zhi in range(2)
        ]

    def device(self, zhi, rest, xx, core):
        return (zhi * self.half + rest) * self.cols + xx * 2 + core

    def here(self):
        row, col = lax.axis_index("row"), lax.axis_index("col")
        return row // self.half, row % self.half, col // 2, col % 2

    def same(self):
        zhi, _, _, core = self.here()
        return zhi == core

    def block(self):
        _, rest, _, core = self.here()
        return core * self.half + rest

    def send(self, value, target):
        pairs = []
        for place in self.places:
            to = target(*place)
            if to is not None:
                pairs.append((self.device(*place), self.device(*to)))
        return lax.ppermute(value, BOTH, pairs)

    def swap(self, value):
        moved = self.send(
            value,
            lambda zhi, rest, xx, core: None if zhi == core else (core, rest, xx, zhi),
        )
        return jnp.where(self.same(), value, moved)

    def partner(self, value, flip):
        def target(zhi, rest, xx, core):
            to = (core * self.half + rest) ^ flip
            return zhi, to % self.half, xx, to // self.half

        return self.send(value, target)

    def token_gather(self, value):
        return lax.all_gather(
            value, BOTH, axis=0, tiled=True, axis_index_groups=self.token_groups
        )

    def weight_pair(self, value):
        def outward(zhi, rest, xx, core):
            return (1 - zhi, rest, xx, core) if zhi == core else (zhi, rest, xx, 1 - core)

        def over(zhi, rest, xx, core):
            return None if zhi == core else (1 - zhi, rest, xx, 1 - core)

        first = self.send(value, outward)
        second = self.send(value, over)
        same = self.same()
        return jnp.where(same, value, first), jnp.where(same, first, second)

    def weight_pieces(self, pair):
        _, _, xx, core = self.here()
        pieces = []
        for flip in range(self.across):
            for j, part in enumerate(pair):
                if flip:
                    part = self.send(part, lambda z, r, x, c: (z, r, x ^ flip, c))
                pieces.append(((xx ^ flip) * 2 + (core ^ j), part))
        return pieces

    def weight_exchange(self, value, axis):
        xx = self.here()[2]
        size = value.shape[axis] // self.across
        received = []
        for step in range(1, self.across):
            part = lax.dynamic_slice_in_dim(value, (xx + step) % self.across * size, size, axis)
            received.append(
                self.send(part, lambda z, r, x, c: (z, r, (x + step) % self.across, c))
            )
        return jnp.stack(received)

    def weight_sum(self, value, received, axis):
        size = value.shape[axis] // self.across
        total = lax.dynamic_slice_in_dim(value, self.here()[2] * size, size, axis)
        total = total.astype(jnp.float32)
        for step in range(self.across - 1):
            total = total + received[step].astype(jnp.float32)
        return total.astype(jnp.bfloat16)

    def weight_send(self, total, axis):
        core = self.here()[3]
        size = total.shape[axis] // 2
        near = lax.dynamic_slice_in_dim(total, core * size, size, axis)
        far = lax.dynamic_slice_in_dim(total, (1 - core) * size, size, axis)
        same = self.same()

        def outward(zhi, rest, xx, core):
            return (zhi, rest, xx, 1 - core) if zhi == core else (1 - zhi, rest, xx, core)

        def over(zhi, rest, xx, core):
            return None if zhi == core else (1 - zhi, rest, xx, 1 - core)

        first = self.send(jnp.where(same, far, near), outward)
        second = self.send(far, over)
        return jnp.where(same, near, second).astype(jnp.float32) + first.astype(jnp.float32)


def join(shape, pieces):
    whole = jnp.zeros(shape, pieces[0][2].dtype)
    for row, col, piece in pieces:
        whole = lax.dynamic_update_slice(whole, piece, (row, col))
    return whole


def after(value, *others):
    return lax.optimization_barrier((value, *others))[0]


def contract_rows(left, right):
    return lax.dot_general(
        left, right, (((0,), (0,)), ((), ())), preferred_element_type=jnp.float32
    )


def contract_cols(left, right):
    return lax.dot_general(
        left, right, (((1,), (1,)), ((), ())), preferred_element_type=jnp.float32
    )


def position(plan):
    row, col = lax.axis_index("row"), lax.axis_index("col")
    zhi, rest, core = row // plan.half, row % plan.half, col % 2
    return zhi, rest, col - core, core


def remote(source, target, send_sem, recv_sem, row, col):
    return pltpu.make_async_remote_copy(
        src_ref=source,
        dst_ref=target,
        send_sem=send_sem,
        recv_sem=recv_sem,
        device_id=(row, col),
        device_id_type=MESH,
    )


def gather_kernel(plan, pieces, axes, own, *refs):
    count = len(axes)
    weights, out, wholes, sems = refs[:count], refs[count], refs[count + 1 :][:count], refs[2 * count + 1 :]
    have_sem, swap_sem, send_sem, recv_sem, near_sem, near_recv_sem = sems[:6]
    block_sem, block_recv_sem, side_sem, side_recv_sem = sems[6:]
    half, across = plan.half, plan.across
    zhi, rest, base, core = position(plan)
    xx = base // 2
    row, col = zhi * half + rest, base + core
    far_row, near_col = (1 - zhi) * half + rest, base + 1 - core
    rows = own.shape[0]
    part = rows // pieces
    moved, stays = zhi != core, zhi == core

    barrier = pltpu.get_barrier_semaphore()
    side_y = half // 2
    zlo, y = rest // side_y, rest % side_y
    base_row = zhi * half

    greeted = [(row, near_col), (far_row, col), (far_row, near_col)]
    greeted += [(base_row + (1 - zlo) * side_y + y, col)]
    greeted += [(base_row + zlo * side_y + (y + step) % side_y, col) for step in range(1, side_y)]
    greeted += [(row, (xx + step) % across * 2 + core) for step in range(1, across)]
    for device in greeted:
        pl.semaphore_signal(barrier, 1, device_id=device, device_id_type=MESH)
    pl.semaphore_wait(barrier, len(greeted))

    def lines(block, h):
        return pl.ds(pl.multiple_of(block * rows + h * part, part), part)

    def entry_near(h):
        source = own.at[pl.ds(h * part, part)]
        return pltpu.make_async_copy(
            source, out.at[lines(core * half + rest, h)], have_sem.at[h]
        )

    def entry_far(h):
        return remote(
            own.at[pl.ds(h * part, part)],
            out.at[lines(zhi * half + rest, h)],
            swap_sem.at[h],
            have_sem.at[h],
            far_row,
            near_col,
        )

    def block_at(over, step):
        other = zlo + over * (1 - 2 * zlo)
        return core * half + other * side_y + (y + side_y - step) % side_y

    def sibling(over, step, h):
        at = out.at[lines(block_at(over, step), h)]
        return remote(
            at,
            at,
            near_sem.at[over, step, h],
            near_recv_sem.at[over, step, h],
            row,
            near_col,
        )

    def along_z(h):
        at = out.at[lines(block_at(0, 0), h)]
        chip = base_row + (1 - zlo) * side_y + y
        return remote(at, at, send_sem.at[0, 0, h], recv_sem.at[1, 0, h], chip, col)

    def along_y(over, step, h):
        at = out.at[lines(block_at(over, 0), h)]
        chip = base_row + zlo * side_y + (y + step) % side_y
        return remote(at, at, send_sem.at[over, step, h], recv_sem.at[over, step, h], chip, col)

    def place(index, other, j):
        axis = axes[index]
        size = weights[index].shape[axis]
        at = pl.ds(pl.multiple_of((other * 2 + j) * size, size), size)
        return wholes[index].at[at] if axis == 0 else wholes[index].at[:, at]

    def block_keep(index, j):
        return pltpu.make_async_copy(
            weights[index], place(index, xx, j), block_recv_sem.at[index, j]
        )

    def block_send(index, way, to_row, to_col):
        return remote(
            weights[index],
            place(index, xx, core),
            block_sem.at[index, way],
            block_recv_sem.at[index, core],
            to_row,
            to_col,
        )

    def side(index, step, j):
        at = place(index, xx, j)
        other = (xx + step) % across * 2 + core
        return remote(
            at, at, side_sem.at[index, step - 1, j], side_recv_sem.at[index, step - 1, j], row, other
        )

    @pl.when(moved)
    def _():
        for h in range(pieces):
            entry_far(h).start()

    @pl.when(stays)
    def _():
        for h in range(pieces):
            entry_near(h).start()
        for index in range(count):
            block_keep(index, core).start()

    for h in range(pieces):

        @pl.when(moved)
        def _():
            entry_far(h).wait_recv()

        @pl.when(stays)
        def _():
            entry_near(h).wait()

        along_z(h).start()
        for step in range(1, side_y):
            along_y(0, step, h).start()
        sibling(0, 0, h).start()

    for h in range(pieces):
        along_z(h).wait_recv()
        for step in range(1, side_y):
            along_y(1, step, h).start()
        sibling(1, 0, h).start()
        sibling(0, 0, h).wait_recv()
        if h == pieces // 2:
            for index in range(count):

                @pl.when(moved)
                def _():
                    block_send(index, 0, row, near_col).start()
                    block_send(index, 1, far_row, near_col).start()

                @pl.when(stays)
                def _():
                    block_send(index, 0, far_row, col).start()

    for over in range(2):
        for h in range(pieces):
            for step in range(1, side_y):
                along_y(over, step, h).wait_recv()
                sibling(over, step, h).start()
    for index in range(count):
        for j in range(2):
            block_keep(index, j).wait()
            for step in range(1, across):
                side(index, step, j).start()
    for h in range(pieces):
        along_z(h).wait_send()
        for over in range(2):
            sibling(over, 0, h).wait_send()
            if over:
                sibling(over, 0, h).wait_recv()
            for step in range(1, side_y):
                sibling(over, step, h).wait()
                along_y(over, step, h).wait_send()
    for index in range(count):
        for j in range(2):
            for step in range(1, across):
                side(index, step, j).wait()

        @pl.when(moved)
        def _():
            block_send(index, 0, row, near_col).wait_send()
            block_send(index, 1, far_row, near_col).wait_send()

        @pl.when(stays)
        def _():
            block_send(index, 0, far_row, col).wait_send()

    @pl.when(moved)
    def _():
        for h in range(pieces):
            entry_far(h).wait_send()


def swap_gather(plan, own, weights, axes, collective_id):
    half, count = plan.half, len(weights)
    pieces = 4
    dma = pltpu.SemaphoreType.DMA
    shape = (own.shape[0] * plan.rows, own.shape[1])
    anywhere = pl.BlockSpec(memory_space=pl.ANY)
    return pl.pallas_call(
        functools.partial(gather_kernel, plan, pieces, axes),
        in_specs=[anywhere] * (1 + count),
        out_specs=[anywhere] * (1 + count),
        out_shape=[jax.ShapeDtypeStruct(shape, own.dtype)]
        + [
            jax.ShapeDtypeStruct(grow(weight.shape, axis, plan.cols), weight.dtype)
            for weight, axis in zip(weights, axes, strict=True)
        ],
        scratch_shapes=[
            dma((pieces,)),
            dma((pieces,)),
            dma((2, half // 2, pieces)),
            dma((2, half // 2, pieces)),
            dma((2, half // 2, pieces)),
            dma((2, half // 2, pieces)),
            dma((count, 2)),
            dma((count, 2)),
            dma((count, plan.across - 1, 2)),
            dma((count, plan.across - 1, 2)),
        ],
        cost_estimate=pl.CostEstimate(
            flops=0, bytes_accessed=20 * shape[0] * shape[1], transcendentals=0
        ),
        compiler_params=pltpu.CompilerParams(collective_id=collective_id, has_side_effects=True),
    )(own, *weights)


def sum_kernel(plan, own, out, landed, send_sem, recv_sem):
    half, rows = plan.half, plan.rows
    zhi, rest, base, core = position(plan)

    def device(step):
        block = (core * half + rest + step) % rows
        return zhi * half + block % half, base + block // half

    barrier = pltpu.get_barrier_semaphore()
    for step in range(1, rows):
        pl.semaphore_signal(barrier, 1, device_id=device(step), device_id_type=MESH)
    pl.semaphore_wait(barrier, rows - 1)
    copies = [
        remote(
            own, landed.at[step - 1], send_sem.at[step - 1], recv_sem.at[step - 1], *device(step)
        )
        for step in range(1, rows)
    ]
    for copy in copies:
        copy.start()
    total = own[...]
    for step, copy in enumerate(copies):
        copy.wait_recv()
        total = total + landed[step]
    out[...] = total
    for copy in copies:
        copy.wait_send()


def group_sum(plan, value, collective_id):
    others = plan.rows - 1
    inside = pl.BlockSpec(memory_space=pltpu.VMEM)
    dma = pltpu.SemaphoreType.DMA
    return pl.pallas_call(
        functools.partial(sum_kernel, plan),
        in_specs=[inside],
        out_specs=inside,
        out_shape=jax.ShapeDtypeStruct(value.shape, value.dtype),
        scratch_shapes=[
            pltpu.VMEM((others, *value.shape), value.dtype),
            dma((others,)),
            dma((others,)),
        ],
        cost_estimate=pl.CostEstimate(
            flops=value.size * others, bytes_accessed=2**24, transcendentals=0
        ),
        compiler_params=pltpu.CompilerParams(collective_id=collective_id, has_side_effects=True),
    )(value)


def scatter_kernel(plan, parts, axes, turned, last, swaps, *refs):
    half, across, count = plan.half, plan.across, len(axes)
    lefts, weight, refs = refs[:parts], refs[parts], refs[parts + 1 :]
    grads, refs = refs[:count], refs[count:]
    if last:
        residual, refs = refs[0], refs[1:]
    if swaps:
        given, refs = refs[0], refs[1:]
    out, blocks, refs = refs[0], refs[1 : count + 1], refs[count + 1 :]
    if last:
        sums, refs = refs[0], refs[1:]
    if swaps:
        taken, refs = refs[0], refs[1:]
    loaded, near_out, near_in, far_out, far_in = refs[:5]
    load_sem, near_sem, near_recv_sem, far_sem, far_recv_sem, block_sem, block_recv_sem = refs[5:12]
    refs = refs[12:]
    zhi, rest, base, core = position(plan)
    xx = base // 2
    row, col = zhi * half + rest, base + core
    far_row, near_col = (1 - zhi) * half + rest, base + 1 - core
    moved, stays = zhi != core, zhi == core
    part, width = near_out.shape[1:]
    rows = 2 * part
    tile = min(512, width)

    barrier = pltpu.get_barrier_semaphore()
    side_y = half // 2
    zlo, y = rest // side_y, rest % side_y
    base_row = zhi * half

    def split(unit):
        h, index = unit // half, unit % half
        first = side_y + h * (2 - side_y)
        second = half // first
        ahead = first - 1 - index // second
        aside = second - 1 - index % second
        place = y + h * (zlo - y)
        other = zlo + h * (y - zlo)
        return h, (place + ahead) % first, (other + aside) % second, place, other, ahead

    def chip_of(h, along, beside):
        return (beside + h * (along - beside)) * side_y + along + h * (beside - along)

    greeted = [(row, near_col), (base_row + (1 - zlo) * side_y + y, col)]
    greeted += [(base_row + zlo * side_y + (y + step) % side_y, col) for step in range(1, side_y)]
    if count:
        greeted += [(row, (xx + step) % across * 2 + core) for step in range(1, across)]
    if last:
        greeted += [(far_row, col)]
    if last or swaps:
        greeted += [(far_row, near_col)]
    for device in greeted:
        pl.semaphore_signal(barrier, 1, device_id=device, device_id_type=MESH)

    def block(index, step):
        grad, axis = grads[index], axes[index]
        other = (xx + step) % across
        size = grad.shape[axis] // across
        at = pl.ds(pl.multiple_of(other * size, size), size)
        return remote(
            grad.at[at] if axis == 0 else grad.at[:, at],
            blocks[index].at[step - 1],
            block_sem.at[index, step - 1],
            block_recv_sem.at[index, step - 1],
            row,
            other * 2 + core,
        )

    def load(unit, whose, slot):
        h, along, beside = split(unit)[:3]
        side = (1 - core) if whose == 0 else core
        index = side * half + chip_of(h, along, beside)
        target, sem = loaded.at[slot, whose], load_sem.at[slot, whose]
        if parts == 1:
            at = pl.ds(pl.multiple_of(index * rows + h * part, part), part)
            return [(None, pltpu.make_async_copy(lefts[0].at[at], target, sem))]
        at = pl.ds(pl.multiple_of(index * part, part), part)
        return [
            (h == k, pltpu.make_async_copy(lefts[k].at[at], target, sem)) for k in range(2)
        ]

    def start(copies):
        for when, copy in copies:
            if when is None:
                copy.start()
            else:
                pl.when(when)(copy.start)

    def near(unit, slot):
        return remote(
            near_out.at[slot],
            near_in.at[unit],
            near_sem.at[unit],
            near_recv_sem.at[unit],
            row,
            near_col,
        )

    def far(unit):
        h, along, beside, place, other, ahead = split(unit)
        straight = (ahead + half - 1) // half
        chip = chip_of(h, along, beside + straight * (other - beside))
        return remote(
            far_out.at[unit],
            far_in.at[unit],
            far_sem.at[unit],
            far_recv_sem.at[unit],
            base_row + chip,
            col,
        )

    def product(left, cols):
        if turned:
            return contract_cols(left, weight[cols, :])
        return jnp.dot(left, weight[:, cols], preferred_element_type=jnp.float32)

    def columns(n):
        return pl.ds(pl.multiple_of(n * tile, tile), tile)

    def exchange():
        return remote(given, taken, refs[0], refs[1], far_row, near_col)

    def keep():
        return pltpu.make_async_copy(given, taken, refs[1])

    start(load(0, 0, 0))
    pl.semaphore_wait(barrier, len(greeted))
    if swaps:
        pl.when(moved)(lambda: exchange().start())
        pl.when(stays)(lambda: keep().start())
    for index in range(count):
        for step in range(1, across):
            block(index, step).start()

    def body(unit, carry):
        slot = unit % 2
        before = unit - 1

        @pl.when(unit + 1 < 2 * half)
        def _():
            start(load(unit + 1, 0, 1 - slot))

        @pl.when(unit < 2 * half)
        def _():
            start(load(unit, 1, 1 - slot))
            load(unit, 0, slot)[0][1].wait()

            @pl.when(unit >= 2)
            def _():
                near(unit - 2, slot).wait_send()

            @pl.loop(0, width // tile)
            def _(n):
                value = product(loaded[slot, 0], columns(n))
                near_out[slot, :, columns(n)] = value.astype(near_out.dtype)

            near(unit, slot).start()

        @pl.when(unit >= 1)
        def _():
            load(before, 1, slot)[0][1].wait()
            near(before, 1 - slot).wait_recv()

            @pl.loop(0, width // tile)
            def _(n):
                value = product(loaded[slot, 1], columns(n))
                value = value + near_in[before, :, columns(n)].astype(jnp.float32)
                far_out[before, :, columns(n)] = value.astype(far_out.dtype)

            @pl.when(split(before)[5] > 0)
            def _():
                far(before).start()

        return carry

    lax.fori_loop(0, 2 * half + 1, body, 0)

    def line_sum(h, aside):
        first = side_y if h == 0 else 2
        second = half // first
        at = h * half + second - 1 - aside
        value = far_out[at + (first - 1) * second].astype(jnp.float32)
        for ahead in range(first - 1):
            unit = at + ahead * second
            far(unit).wait_recv()
            value = value + far_in[unit].astype(jnp.float32)
        return value

    for h in range(2):
        second = 2 if h == 0 else side_y
        for aside in range(second - 1, 0, -1):
            unit = (h + 1) * half - 1 - aside
            far_out[unit] = line_sum(h, aside).astype(far_out.dtype)
            far(unit).start()

    def total(h):
        value = line_sum(h, 0)
        second = 2 if h == 0 else side_y
        for aside in range(second - 1, 0, -1):
            unit = (h + 1) * half - 1 - aside
            far(unit).wait_recv()
            value = value + far_in[unit].astype(jnp.float32)
        return value

    if last:
        finish_sum = finish(
            (zhi, rest, xx, core), (row, col, far_row, near_col), grads, blocks, block, sums, refs
        )
        final, final_sem, final_recv_sem = refs[:3]

        def swap_far(h):
            return remote(
                final.at[h],
                out.at[pl.ds(h * part, part)],
                final_sem.at[h],
                final_recv_sem.at[h],
                far_row,
                near_col,
            )

        def swap_near(h):
            return pltpu.make_async_copy(
                final.at[h], out.at[pl.ds(h * part, part)], final_recv_sem.at[h]
            )

        for h in range(2):
            value = total(h) + residual[h * part : (h + 1) * part, :]
            final[h] = value.astype(final.dtype)

            @pl.when(moved)
            def _():
                swap_far(h).start()

            @pl.when(stays)
            def _():
                swap_near(h).start()

            if h == 0:
                finish_sum()

        for h in range(2):

            @pl.when(moved)
            def _():
                swap_far(h).wait()

            @pl.when(stays)
            def _():
                swap_near(h).wait()

    else:
        for h in range(2):
            out[h * part : (h + 1) * part, :] = total(h)
        for index in range(count):
            for step in range(1, across):
                block(index, step).wait_recv()
    if swaps:
        pl.when(moved)(lambda: exchange().wait())
        pl.when(stays)(lambda: keep().wait())
    for h in range(2):
        for unit in range(h * half, h * half + half - 1):
            far(unit).wait_send()
    for unit in range(2 * half - 2, 2 * half):
        near(unit, unit % 2).wait_send()
    for index in range(count):
        for step in range(1, across):
            block(index, step).wait_send()


def finish(place, devices, grads, blocks, block, sums, refs):
    zhi, _, xx, core = place
    row, col, far_row, near_col = devices
    grad, blocks = grads[0], blocks[0]
    mine, others, pair, landed, mine_sem, pair_sem, landed_sem = refs[3:]
    size = pair.shape[1]
    across = blocks.shape[0] + 1
    own = pltpu.make_async_copy(
        grad.at[pl.ds(pl.multiple_of(xx * 2 * size, size), 2 * size)], mine, mine_sem.at[0]
    )
    rest = [
        pltpu.make_async_copy(blocks.at[step], others.at[step], mine_sem.at[step + 1])
        for step in range(across - 1)
    ]

    def give(index, slot, to_row, to_col, to_slot):
        return remote(
            pair.at[slot],
            landed.at[to_slot],
            pair_sem.at[index],
            landed_sem.at[to_slot],
            to_row,
            to_col,
        )

    to_sibling = give(0, 1 - core, row, near_col, 0)
    to_same = give(0, core, far_row, col, 0)
    to_cross = give(1, 1 - core, far_row, near_col, 1)
    own.start()

    def run():
        for step in range(1, across):
            block(0, step).wait_recv()
            rest[step - 1].start()
        own.wait()
        for copy in rest:
            copy.wait()
        value = mine[...].astype(jnp.float32)
        for step in range(across - 1):
            value = value + others[step].astype(jnp.float32)
        pair[0] = value[:size].astype(pair.dtype)
        pair[1] = value[size:].astype(pair.dtype)

        @pl.when(zhi == core)
        def _():
            to_sibling.start()
            to_sibling.wait_send()
            give(0, core, far_row, col, 0).wait_recv()
            sums[...] = pair[core].astype(jnp.float32) + landed[0].astype(jnp.float32)

        @pl.when(zhi != core)
        def _():
            to_same.start()
            to_cross.start()
            to_same.wait_send()
            to_cross.wait_send()
            to_same.wait_recv()
            to_cross.wait_recv()
            sums[...] = landed[1].astype(jnp.float32) + landed[0].astype(jnp.float32)

    return run


def grow(shape, axis, pieces):
    return tuple(size * pieces if dim == axis else size for dim, size in enumerate(shape))


def cut(shape, axis, pieces):
    return tuple(size // pieces if dim == axis else size for dim, size in enumerate(shape))


def multiply_scatter(
    plan, lefts, weight, turned, collective_id, grads=(), axes=(), residual=None, swapped=None
):
    half, across, count = plan.half, plan.across, len(grads)
    depth = lefts[0].shape[1]
    width = weight.shape[0 if turned else 1]
    rows = sum(left.shape[0] for left in lefts) // plan.rows
    part = rows // 2
    low = jnp.bfloat16
    dma = pltpu.SemaphoreType.DMA
    anywhere = pl.BlockSpec(memory_space=pl.ANY)
    inside = pl.BlockSpec(memory_space=pltpu.VMEM)
    last = residual is not None
    swaps = swapped is not None
    in_specs = [anywhere] * len(lefts) + [inside] + [anywhere] * count + [inside] * last
    in_specs += [anywhere] * swaps
    out_specs = [anywhere if last else inside] + [anywhere] * count + [inside] * last
    out_shape = [jax.ShapeDtypeStruct((rows, width), low if last else jnp.float32)]
    out_shape += [
        jax.ShapeDtypeStruct((across - 1, *cut(grad.shape, axis, across)), low)
        for grad, axis in zip(grads, axes, strict=True)
    ]
    scratch = [
        pltpu.VMEM((2, 2, part, depth), low),
        pltpu.VMEM((2, part, width), low),
        pltpu.VMEM((2 * half, part, width), low),
        pltpu.VMEM((2 * half, part, width), low),
        pltpu.VMEM((2 * half, part, width), low),
        dma((2, 2)),
        dma((2 * half,)),
        dma((2 * half,)),
        dma((2 * half,)),
        dma((2 * half,)),
        dma((max(count, 1), across - 1)),
        dma((max(count, 1), across - 1)),
    ]
    if last:
        size, wide = grads[0].shape[0] // plan.cols, grads[0].shape[1]
        out_shape.append(jax.ShapeDtypeStruct((size, wide), jnp.float32))
        scratch += [
            pltpu.VMEM((2, part, width), low),
            dma((2,)),
            dma((2,)),
            pltpu.VMEM((2 * size, wide), low),
            pltpu.VMEM((across - 1, 2 * size, wide), low),
            pltpu.VMEM((2, size, wide), low),
            pltpu.VMEM((2, size, wide), low),
            dma((across,)),
            dma((2,)),
            dma((2,)),
        ]
    if swaps:
        out_shape.append(jax.ShapeDtypeStruct(swapped.shape, swapped.dtype))
        scratch += [dma, dma]
    return pl.pallas_call(
        functools.partial(scatter_kernel, plan, len(lefts), axes, turned, last, swaps),
        in_specs=in_specs,
        out_specs=out_specs + [anywhere] * swaps,
        out_shape=out_shape,
        scratch_shapes=scratch,
        cost_estimate=pl.CostEstimate(
            flops=2 * rows * plan.rows * depth * width,
            bytes_accessed=20 * rows * plan.rows * width,
            transcendentals=0,
        ),
        compiler_params=pltpu.CompilerParams(
            collective_id=collective_id, has_side_effects=True, vmem_limit_bytes=58 * 2**20
        ),
    )(*lefts, weight, *grads, *([residual] if last else []), *([swapped] if swaps else []))


def full(rows, width):
    return pl.BlockSpec((rows, width), lambda *_: (0, 0))


def turn(values, cosine, sine):
    return values * cosine + pltpu.roll(values, values.shape[-1] // 2, 1) * sine


def column(row_vector, width):
    return jnp.transpose(jnp.broadcast_to(row_vector, (width, row_vector.shape[1])))


def project_kernel(head_size, left, weight, proj, squares):
    value = jnp.dot(left[...], weight[...], preferred_element_type=jnp.float32)
    proj[...] = value
    width = proj.shape[1] // 3
    for place in range(2):
        total = None
        for start in range(place * width, (place + 1) * width, head_size):
            part = value[:, start : start + head_size] ** 2
            total = part if total is None else total + part
        squares[place : place + 1, :] = jnp.sum(jnp.transpose(total), axis=0, keepdims=True)


def project(left, weight, head_size):
    seq_len, depth = left.shape
    rows = min(512, seq_len)
    wide = weight.shape[1]
    return pl.pallas_call(
        functools.partial(project_kernel, head_size),
        grid=(seq_len // rows,),
        in_specs=[pl.BlockSpec((rows, depth), lambda i: (i, 0)), full(depth, wide)],
        out_specs=[
            pl.BlockSpec((rows, wide), lambda i: (i, 0)),
            pl.BlockSpec((2, rows), lambda i: (0, i)),
        ],
        out_shape=[
            jax.ShapeDtypeStruct((seq_len, wide), jnp.float32),
            jax.ShapeDtypeStruct((2, seq_len), jnp.float32),
        ],
        cost_estimate=pl.CostEstimate(
            flops=2 * seq_len * depth * wide,
            bytes_accessed=2 * seq_len * depth + 4 * seq_len * wide,
            transcendentals=0,
        ),
        compiler_params=pltpu.CompilerParams(vmem_limit_bytes=40 * 2**20),
    )(left, weight)


def prepare_kernel(
    head_size, proj, query_inv, key_inv, cosine, sine, query_gain, key_gain, query, key, value
):
    width = query.shape[1]
    turns = (cosine[...], sine[...])
    for source, inv, gain, target in (
        (0, query_inv, query_gain, query),
        (width, key_inv, key_gain, key),
    ):
        factor = column(inv[...], head_size)
        for start in range(0, width, head_size):
            part = proj[:, source + start : source + start + head_size]
            scaled = part * factor * gain[:, start : start + head_size]
            target[:, start : start + head_size] = turn(scaled, *turns).astype(target.dtype)
    value[...] = proj[:, 2 * width :].astype(value.dtype)


def prepare(proj, query_inv, key_inv, cosine, sine, query_gain, key_gain, head_size):
    seq_len, width = proj.shape[0], proj.shape[1] // 3
    rows = min(512, seq_len)
    return pl.pallas_call(
        functools.partial(prepare_kernel, head_size),
        grid=(seq_len // rows,),
        in_specs=[
            pl.BlockSpec((rows, 3 * width), lambda i: (i, 0)),
            pl.BlockSpec((1, rows), lambda i: (0, i)),
            pl.BlockSpec((1, rows), lambda i: (0, i)),
            pl.BlockSpec((rows, head_size), lambda i: (i, 0)),
            pl.BlockSpec((rows, head_size), lambda i: (i, 0)),
            full(1, width),
            full(1, width),
        ],
        out_specs=[pl.BlockSpec((rows, width), lambda i: (i, 0))] * 3,
        out_shape=[jax.ShapeDtypeStruct((seq_len, width), jnp.bfloat16)] * 3,
        cost_estimate=pl.CostEstimate(
            flops=10 * seq_len * width, bytes_accessed=seq_len * width * 20, transcendentals=0
        ),
        compiler_params=pltpu.CompilerParams(vmem_limit_bytes=40 * 2**20),
    )(proj, query_inv, key_inv, cosine, sine, query_gain, key_gain)


def allowed(first, key_block, query_block, key_rows, query_rows):
    key_index = key_block * key_rows + lax.broadcasted_iota(
        jnp.int32, (key_rows, query_rows), 0
    )
    query_index = query_block * query_rows + lax.broadcasted_iota(
        jnp.int32, (key_rows, query_rows), 1
    )
    return (key_index <= query_index) & (key_index >= first)


def attend_kernel(rows, low, first, query, key, value, *refs):
    out, log_sum = refs[-2:]
    step = pl.program_id(1)
    head_size = query.shape[1]
    factor = LOG2E * head_size**-0.5
    queries = query[...]
    starts = first[...]

    def one(index, carry):
        top, total, acc = carry
        at = pl.ds(pl.multiple_of(index * rows, rows), rows)
        scores = contract_cols(key[at, :], queries) * factor
        scores = jnp.where(allowed(starts, index, step, rows, rows), scores, MASKED)
        new_top = jnp.maximum(top, jnp.max(scores, axis=0, keepdims=True))
        probs = jnp.exp2(scores - new_top)
        fade = jnp.exp2(top - new_top)
        total = total * fade + jnp.sum(probs, axis=0, keepdims=True)
        acc = acc * fade + contract_rows(value[at, :], probs.astype(jnp.bfloat16))
        return new_top, total, acc

    top, total, acc = lax.fori_loop(
        low[step],
        step + 1,
        one,
        (
            jnp.full((1, rows), MASKED, jnp.float32),
            jnp.zeros((1, rows), jnp.float32),
            jnp.zeros((head_size, rows), jnp.float32),
        ),
    )
    out[...] = jnp.transpose(acc / total).astype(out.dtype)
    log_sum[0] = top + jnp.log2(total)


def attend(low, first, query, key, value, head_size, rows, more):
    seq_len, width = query.shape
    heads = width // head_size
    whole = pl.BlockSpec((seq_len, head_size), lambda h, i, *_: (0, h))
    block = pl.BlockSpec((rows, head_size), lambda h, i, *_: (i, h))
    return pl.pallas_call(
        functools.partial(attend_kernel, rows),
        grid_spec=pltpu.PrefetchScalarGridSpec(
            num_scalar_prefetch=1,
            grid=(heads, seq_len // rows),
            in_specs=[
                pl.BlockSpec((1, rows), lambda h, i, *_: (0, i)),
                block,
                whole,
                whole,
            ]
            + [pl.BlockSpec(memory_space=pl.ANY)] * len(more),
            out_specs=[block, pl.BlockSpec((1, 1, rows), lambda h, i, *_: (h, 0, i))],
        ),
        out_shape=[
            jax.ShapeDtypeStruct((seq_len, width), jnp.bfloat16),
            jax.ShapeDtypeStruct((heads, 1, seq_len), jnp.float32),
        ],
        cost_estimate=pl.CostEstimate(
            flops=seq_len * seq_len * width, bytes_accessed=seq_len * width * 8, transcendentals=0
        ),
        compiler_params=pltpu.CompilerParams(vmem_limit_bytes=40 * 2**20),
    )(low, first, query, key, value, *more)


def attend_back_kernel(
    rows,
    high,
    first,
    query,
    key,
    value,
    out,
    out_grad,
    log_sum,
    *refs,
):
    query_grad, key_grad, value_grad, delta = refs[-4:]
    step = pl.program_id(1)
    seq_len, head_size = query.shape
    factor = LOG2E * head_size**-0.5

    @pl.when(step == 0)
    def _():
        query_grad[...] = jnp.zeros_like(query_grad)

        @pl.loop(0, seq_len // rows)
        def _(index):
            at = pl.ds(pl.multiple_of(index * rows, rows), rows)
            product = out_grad[at, :].astype(jnp.float32) * out[at, :].astype(jnp.float32)
            delta[:, at] = jnp.sum(jnp.transpose(product), axis=0, keepdims=True)

    keys = key[...]
    values = value[...]

    def one(index, carry):
        key_acc, value_acc = carry
        at = pl.ds(pl.multiple_of(index * rows, rows), rows)
        queries = query[at, :]
        grads = out_grad[at, :]
        scores = contract_cols(keys, queries) * factor
        mask = allowed(first[:, at], step, index, rows, rows)
        probs = jnp.exp2(jnp.where(mask, scores - log_sum[0, :, at], MASKED))
        value_acc = value_acc + jnp.dot(
            probs.astype(jnp.bfloat16), grads, preferred_element_type=jnp.float32
        )
        prob_grad = contract_cols(values, grads)
        score_grad = (probs * (prob_grad - delta[:, at])).astype(jnp.bfloat16)
        key_acc = key_acc + jnp.dot(score_grad, queries, preferred_element_type=jnp.float32)
        query_grad[at, :] += contract_rows(score_grad, keys)
        return key_acc, value_acc

    zeros = jnp.zeros((rows, head_size), jnp.float32)
    key_acc, value_acc = lax.fori_loop(step, high[step] + 1, one, (zeros, zeros))
    key_grad[...] = key_acc
    value_grad[...] = value_acc.astype(value_grad.dtype)


def attend_back(high, first, query, key, value, out, out_grad, log_sum, head_size, rows, more):
    seq_len, width = query.shape
    heads = width // head_size
    whole = pl.BlockSpec((seq_len, head_size), lambda h, j, *_: (0, h))
    block = pl.BlockSpec((rows, head_size), lambda h, j, *_: (j, h))
    return pl.pallas_call(
        functools.partial(attend_back_kernel, rows),
        grid_spec=pltpu.PrefetchScalarGridSpec(
            num_scalar_prefetch=1,
            grid=(heads, seq_len // rows),
            in_specs=[
                full(1, seq_len),
                whole,
                block,
                block,
                whole,
                whole,
                pl.BlockSpec((1, 1, seq_len), lambda h, j, *_: (h, 0, 0)),
            ]
            + [pl.BlockSpec(memory_space=pl.ANY)] * len(more),
            out_specs=[whole, block, block],
            scratch_shapes=[pltpu.VMEM((1, seq_len), jnp.float32)],
        ),
        out_shape=[
            jax.ShapeDtypeStruct((seq_len, width), jnp.float32),
            jax.ShapeDtypeStruct((seq_len, width), jnp.float32),
            jax.ShapeDtypeStruct((seq_len, width), jnp.bfloat16),
        ],
        cost_estimate=pl.CostEstimate(
            flops=3 * seq_len * seq_len * width,
            bytes_accessed=seq_len * width * 20,
            transcendentals=0,
        ),
        compiler_params=pltpu.CompilerParams(vmem_limit_bytes=48 * 2**20),
    )(high, first, query, key, value, out, out_grad, log_sum, *more)


def norm_back_kernel(
    head_size,
    proj,
    query_inv,
    key_inv,
    cosine,
    sine,
    query_gain,
    key_gain,
    query_grad,
    key_grad,
    dots,
    gain_sums,
):
    width = query_grad.shape[1]
    turns = (cosine[...], -sine[...])
    scale = head_size**-0.5

    @pl.when(pl.program_id(0) == 0)
    def _():
        gain_sums[...] = jnp.zeros_like(gain_sums)

    for place, (source, inv, gain, grad) in enumerate(
        ((0, query_inv, query_gain, query_grad), (width, key_inv, key_gain, key_grad))
    ):
        factor = column(inv[...], head_size)
        row_part = None
        for start in range(0, width, head_size):
            cols = slice(start, start + head_size)
            hat = proj[:, source + start : source + start + head_size] * factor
            product = turn(grad[:, cols] * scale, *turns) * hat
            gain_sums[place : place + 1, cols] += jnp.sum(product, axis=0, keepdims=True)
            product = product * gain[:, cols]
            row_part = product if row_part is None else row_part + product
        dots[place : place + 1, :] = jnp.sum(jnp.transpose(row_part), axis=0, keepdims=True)


def norm_back(
    proj, query_inv, key_inv, cosine, sine, query_gain, key_gain, query_grad, key_grad, head_size
):
    seq_len, width = query_grad.shape
    rows = min(512, seq_len)
    wide = pl.BlockSpec((rows, width), lambda i: (i, 0))
    return pl.pallas_call(
        functools.partial(norm_back_kernel, head_size),
        grid=(seq_len // rows,),
        in_specs=[
            pl.BlockSpec((rows, 2 * width), lambda i: (i, 0)),
            pl.BlockSpec((1, rows), lambda i: (0, i)),
            pl.BlockSpec((1, rows), lambda i: (0, i)),
            pl.BlockSpec((rows, head_size), lambda i: (i, 0)),
            pl.BlockSpec((rows, head_size), lambda i: (i, 0)),
            full(1, width),
            full(1, width),
            wide,
            wide,
        ],
        out_specs=[pl.BlockSpec((2, rows), lambda i: (0, i)), full(2, width)],
        out_shape=[
            jax.ShapeDtypeStruct((2, seq_len), jnp.float32),
            jax.ShapeDtypeStruct((2, width), jnp.float32),
        ],
        cost_estimate=pl.CostEstimate(
            flops=20 * seq_len * width, bytes_accessed=seq_len * width * 20, transcendentals=0
        ),
        compiler_params=pltpu.CompilerParams(vmem_limit_bytes=40 * 2**20),
    )(proj, query_inv, key_inv, cosine, sine, query_gain, key_gain, query_grad, key_grad)


def proj_back_kernel(
    head_size,
    features,
    proj,
    query_inv,
    key_inv,
    cosine,
    sine,
    query_gain,
    key_gain,
    query_grad,
    key_grad,
    value_grad,
    dots,
    *rest,
):
    out = rest[-1]
    width = query_grad.shape[1]
    turns = (cosine[...], -sine[...])
    scale = head_size**-0.5
    for place, (source, inv, gain, grad) in enumerate(
        ((0, query_inv, query_gain, query_grad), (width, key_inv, key_gain, key_grad))
    ):
        factor = column(inv[...], head_size)
        mean = column(dots[place : place + 1, :] * (1.0 / features), head_size)
        for start in range(0, width, head_size):
            cols = slice(start, start + head_size)
            at = slice(source + start, source + start + head_size)
            hat = proj[:, at] * factor
            scaled = turn(grad[:, cols] * scale, *turns) * gain[:, cols]
            out[:, at] = (factor * (scaled - hat * mean)).astype(out.dtype)
    out[:, 2 * width :] = value_grad[...]


def proj_back(
    proj,
    query_inv,
    key_inv,
    cosine,
    sine,
    query_gain,
    key_gain,
    query_grad,
    key_grad,
    value_grad,
    dots,
    head_size,
    features,
    more,
):
    seq_len, width = query_grad.shape
    rows = min(512, seq_len)
    wide = pl.BlockSpec((rows, width), lambda i: (i, 0))
    return pl.pallas_call(
        functools.partial(proj_back_kernel, head_size, features),
        grid=(seq_len // rows,),
        in_specs=[
            pl.BlockSpec((rows, 2 * width), lambda i: (i, 0)),
            pl.BlockSpec((1, rows), lambda i: (0, i)),
            pl.BlockSpec((1, rows), lambda i: (0, i)),
            pl.BlockSpec((rows, head_size), lambda i: (i, 0)),
            pl.BlockSpec((rows, head_size), lambda i: (i, 0)),
            full(1, width),
            full(1, width),
            wide,
            wide,
            wide,
            pl.BlockSpec((2, rows), lambda i: (0, i)),
        ]
        + [pl.BlockSpec(memory_space=pl.ANY)] * len(more),
        out_specs=pl.BlockSpec((rows, 3 * width), lambda i: (i, 0)),
        out_shape=jax.ShapeDtypeStruct((seq_len, 3 * width), jnp.bfloat16),
        cost_estimate=pl.CostEstimate(
            flops=20 * seq_len * width, bytes_accessed=seq_len * width * 24, transcendentals=0
        ),
        compiler_params=pltpu.CompilerParams(vmem_limit_bytes=40 * 2**20),
    )(
        proj,
        query_inv,
        key_inv,
        cosine,
        sine,
        query_gain,
        key_gain,
        query_grad,
        key_grad,
        value_grad,
        dots,
        *more,
    )


def body(
    plan,
    layer_input,
    segments,
    w_query,
    w_key,
    w_value,
    w_out,
    query_gain,
    key_gain,
    attn_gain,
    w_gate,
    w_up,
    w_down,
    mlp_gain,
    cotangent,
):
    rows = plan.rows
    mine = plan.block()
    model_width = layer_input.shape[1]
    head_size = model_width // HEADS
    seq_len = segments.shape[0]
    own_tokens = seq_len // rows
    part = own_tokens // 2
    f32 = jnp.float32
    bf16 = jnp.bfloat16
    chunks = range(2)

    def chunk_of(value, k):
        return value[k * part : (k + 1) * part]

    qkv_own = jnp.concatenate([w_query, w_key, w_value], axis=1)
    own_depth, wide = qkv_own.shape
    small_own = jnp.concatenate([query_gain, key_gain, attn_gain, mlp_gain])
    gain_size, post_size = query_gain.shape[0], attn_gain.shape[0]
    cuts = (gain_size, 2 * gain_size, 2 * gain_size + post_size)
    small_size = small_own.shape[0]
    extra = 16

    def lines(vector):
        return jnp.pad(vector, (0, extra * wide - small_size)).reshape(extra, wide)

    own_weight = jnp.concatenate([qkv_own, lines(small_own)], axis=0)
    gathered_x, both, out_rows = swap_gather(
        plan, layer_input, (own_weight, w_out), (0, 1), 1
    )
    both = both.reshape(plan.cols, own_depth + extra, wide)
    proj_weight = both[:, :own_depth].reshape(-1, wide)
    small = both[:, own_depth:].reshape(plan.cols, extra * wide)[:, :small_size].astype(f32)
    query_scale, key_scale, attn_scale, mlp_scale = (
        value.reshape(1, -1) for value in jnp.split(small, cuts, axis=1)
    )

    own_x = lax.dynamic_slice_in_dim(gathered_x, mine * own_tokens, own_tokens)
    segments = plan.swap(segments)
    out_full = plan.token_gather(out_rows)
    ff_width = w_gate.shape[1]

    local_width = wide // 3
    token_index = jnp.arange(seq_len, dtype=jnp.int32)
    change = jnp.concatenate([jnp.ones((1,), dtype=bool), segments[1:] != segments[:-1]])
    first = lax.cummax(jnp.where(change, token_index, 0), axis=0)
    places = (token_index - first).astype(f32)
    lane = jnp.arange(head_size, dtype=jnp.int32)
    half = head_size // 2
    freqs = THETA ** (-((lane % half).astype(f32) * 2.0) / head_size)
    angle = places[:, None] * freqs[None, :]
    cosine = jnp.cos(angle)
    sine = jnp.sin(angle) * jnp.where(lane < half, -1.0, 1.0)[None, :]
    tile = min(512, seq_len)
    low = first[::tile] // tile
    last = token_index[tile - 1 :: tile]
    ends = jnp.min(
        jnp.where(change[None, :] & (token_index[None, :] > last[:, None]), token_index, seq_len),
        axis=1,
    )
    high = (ends - 1) // tile
    first_row = first[None, :]

    proj, squares = project(gathered_x, proj_weight, head_size)
    invs = lax.rsqrt(group_sum(plan, squares, 5) / model_width + EPS)
    query_inv, key_inv = invs[:1], invs[1:]
    query, key, value = prepare(
        proj, query_inv, key_inv, cosine, sine, query_scale, key_scale, head_size
    )
    gate_pair = plan.weight_pair(after(w_gate, invs))
    up_pair = plan.weight_pair(after(w_up, query))
    attn_out, log_sum = attend(
        low, first_row, query, key, value, head_size, tile, gate_pair
    )
    post_depth = w_out.shape[1]

    attn_tokens = jnp.zeros((own_tokens, model_width), bf16)
    for flip in range(rows):
        other = mine ^ flip
        piece = lax.dynamic_slice(attn_out, (other * own_tokens, 0), (own_tokens, local_width))
        if flip:
            piece = plan.partner(piece, flip)
        attn_tokens = lax.dynamic_update_slice(attn_tokens, piece, (0, other * local_width))

    places, gate_pieces = zip(*plan.weight_pieces(gate_pair), strict=True)
    attn_tokens, *others = lax.optimization_barrier((attn_tokens, *gate_pieces, *up_pair))
    gate_pieces, up_pair = zip(places, others[:-2], strict=True), others[-2:]
    up_pieces = plan.weight_pieces(up_pair)
    down_pair = plan.weight_pair(after(w_down, *(piece for _, piece in up_pieces)))
    ff_weight = join(
        (model_width, 2 * ff_width),
        [
            (c * own_depth, start, piece)
            for start, pieces in ((0, gate_pieces), (ff_width, up_pieces))
            for c, piece in pieces
        ],
    )
    down_rows = join(
        (ff_width, model_width),
        [(0, c * post_depth, piece) for c, piece in plan.weight_pieces(down_pair)],
    )

    def normed(value):
        inv = lax.rsqrt(jnp.mean(value * value, axis=-1, keepdims=True) + EPS)
        return inv, value * inv

    def norm_grad(inv, hat, scaled):
        mean = jnp.mean(scaled * hat, axis=-1, keepdims=True)
        return (inv * (scaled - hat * mean)).astype(bf16)

    attn_inv, attn_hat, hidden, gathered_h = [], [], [], []
    for k in chunks:
        out_proj = jnp.dot(chunk_of(attn_tokens, k), out_full, preferred_element_type=f32)
        inv, hat = normed(out_proj)
        attn_inv.append(inv)
        attn_hat.append(hat)
        hidden.append(chunk_of(own_x, k).astype(f32) + hat * attn_scale)
        gathered_h.append(plan.token_gather(hidden[k].astype(bf16)))

    gate, up, activated = [], [], []
    for k in chunks:
        both = jnp.dot(gathered_h[k], ff_weight, preferred_element_type=f32).astype(bf16)
        gate.append(both[:, :ff_width])
        up.append(both[:, ff_width:])
        activated.append((jax.nn.silu(gate[k].astype(f32)) * up[k].astype(f32)).astype(bf16))
    mlp_out, own_cot = multiply_scatter(
        plan, activated, down_rows, False, 2, swapped=cotangent
    )

    outputs, upstream, shard_rows = [], [], []
    mlp_gain_part = 0.0
    for k in chunks:
        inv, hat = normed(chunk_of(mlp_out, k))
        outputs.append((hidden[k] + hat * mlp_scale).astype(bf16))
        upstream.append(chunk_of(own_cot, k).astype(f32))
        mlp_gain_part += jnp.sum(upstream[k] * hat, axis=0)
        shard_rows.append(plan.token_gather(norm_grad(inv, hat, upstream[k] * mlp_scale)))

    ff_grad = []
    for k in chunks:
        act_part = contract_cols(shard_rows[k], down_rows)
        gate_val, up_val = gate[k].astype(f32), up[k].astype(f32)
        gate_sigmoid = jax.nn.sigmoid(gate_val)
        gate_grad = act_part * up_val * gate_sigmoid * (1.0 + gate_val * (1.0 - gate_sigmoid))
        up_grad = act_part * gate_val * gate_sigmoid
        ff_grad.append(jnp.concatenate([gate_grad, up_grad], axis=1).astype(bf16))
    down_grad = sum(contract_rows(activated[k], shard_rows[k]) for k in chunks).astype(bf16)
    ff_weight_grad = sum(contract_rows(gathered_h[k], ff_grad[k]) for k in chunks).astype(bf16)
    hidden_grad_mlp, ff_blocks, layer_output = multiply_scatter(
        plan,
        ff_grad,
        ff_weight,
        True,
        3,
        (ff_weight_grad,),
        (0,),
        swapped=jnp.concatenate(outputs),
    )
    hidden_grad = [upstream[k] + chunk_of(hidden_grad_mlp, k) for k in chunks]
    ff_sum = plan.weight_send(plan.weight_sum(ff_weight_grad, ff_blocks, 0), 0)
    down_blocks = plan.weight_exchange(after(down_grad, ff_blocks), 1)

    attn_gain_part = 0.0
    proj_grads, token_grads = [], []
    for k in chunks:
        attn_gain_part += jnp.sum(hidden_grad[k] * attn_hat[k], axis=0)
        proj_grads.append(norm_grad(attn_inv[k], attn_hat[k], hidden_grad[k] * attn_scale))
        token_grads.append(contract_cols(proj_grads[k], out_full).astype(bf16))
    out_token_grad = jnp.concatenate(token_grads)

    attn_grad = jnp.zeros((seq_len, local_width), bf16)
    for flip in range(rows):
        other = mine ^ flip
        piece = lax.dynamic_slice(
            out_token_grad, (0, other * local_width), (own_tokens, local_width)
        )
        if flip:
            piece = plan.partner(piece, flip)
        attn_grad = lax.dynamic_update_slice(attn_grad, piece, (other * own_tokens, 0))

    out_grad = sum(
        contract_rows(
            attn_out.reshape(rows, 2, part, local_width)[:, k].reshape(-1, local_width),
            plan.token_gather(proj_grads[k]),
        )
        for k in chunks
    ).astype(bf16)
    out_sum = plan.weight_sum(out_grad, plan.weight_exchange(out_grad, 1), 1)
    query_grad, key_grad, value_grad = attend_back(
        high,
        first_row,
        query,
        key,
        value,
        attn_out,
        attn_grad,
        log_sum,
        head_size,
        tile,
        (down_blocks,),
    )
    down_sum = plan.weight_send(plan.weight_sum(down_grad, down_blocks, 1), 1)
    shared = (proj, query_inv, key_inv, cosine, sine, query_scale, key_scale, query_grad, key_grad)
    dots, gain_sums = norm_back(*shared, head_size)
    dots = group_sum(
        plan,
        jnp.concatenate([dots, jnp.stack([attn_gain_part, mlp_gain_part])], axis=1),
        6,
    )
    dots, post_sums = dots[:, :seq_len], dots[:, seq_len:]
    proj_grad_all = proj_back(
        *shared, value_grad, dots, head_size, model_width, (ff_sum,)
    )
    proj_grad_all = after(proj_grad_all, out_sum)
    proj_weight_grad = contract_rows(gathered_x, proj_grad_all).astype(bf16)
    small = jnp.concatenate(
        [
            gain_sums[0].reshape(plan.cols, -1),
            gain_sums[1].reshape(plan.cols, -1),
            post_sums[0].reshape(plan.cols, -1),
            post_sums[1].reshape(plan.cols, -1),
        ],
        axis=1,
    )
    small = jnp.pad(small, ((0, 0), (0, extra * wide - small_size)))
    small = small.reshape(plan.cols, extra, wide).astype(bf16)
    stacked = jnp.concatenate(
        [proj_weight_grad.reshape(plan.cols, own_depth, wide), small], axis=1
    )
    stacked = stacked.reshape(-1, wide)
    out_sum = plan.weight_send(out_sum, 1)
    stacked = after(stacked, out_sum, down_sum)
    input_grad, _, proj_sum = multiply_scatter(
        plan,
        [proj_grad_all],
        proj_weight,
        True,
        4,
        (stacked,),
        (0,),
        jnp.concatenate(hidden_grad),
    )
    small = proj_sum[own_depth:].reshape(-1)[:small_size]
    query_gain_sum, key_gain_sum, attn_gain_sum, mlp_gain_sum = jnp.split(small, cuts)
    proj_sum = proj_sum[:own_depth]
    own_ff = w_gate.shape[1]
    return (
        layer_output,
        input_grad,
        proj_sum[:, :local_width],
        proj_sum[:, local_width : 2 * local_width],
        proj_sum[:, 2 * local_width :],
        out_sum,
        query_gain_sum,
        key_gain_sum,
        attn_gain_sum,
        ff_sum[:, :own_ff],
        ff_sum[:, own_ff:],
        down_sum,
        mlp_gain_sum,
    )


def solution(mesh):
    tokens = P(("col", "row"), None)
    columns = P("col", "row")
    across = P("row", "col")
    vector = P(("row", "col"))
    return jax.shard_map(
        functools.partial(body, Plan(mesh)),
        mesh=mesh,
        in_specs=(
            tokens,
            P("col"),
            columns,
            columns,
            columns,
            across,
            vector,
            vector,
            P("col"),
            columns,
            columns,
            across,
            P("col"),
            tokens,
        ),
        out_specs=(
            tokens,
            tokens,
            columns,
            columns,
            columns,
            across,
            vector,
            vector,
            P("col"),
            columns,
            columns,
            across,
            P("col"),
        ),
        check_vma=False,
    )
```

```python
import functools

import jax
import jax.numpy as jnp
from jax import lax
from jax.experimental import pallas as pl
from jax.experimental.pallas import tpu as pltpu
from jax.sharding import PartitionSpec as P

HEADS = 16


EPS = 1e-06
THETA = 500000.0
MASKED = -1e30
LOG2E = 1.4426950408889634
BOTH = ("row", "col")
MESH = pl.DeviceIdType.MESH


class Plan:
    def __init__(self, mesh):
        self.rows, self.cols = mesh.shape["row"], mesh.shape["col"]
        self.half = self.rows // 2
        self.across = self.cols // 2
        self.places = [
            (zhi, rest, xx, core)
            for zhi in range(2)
            for rest in range(self.half)
            for xx in range(self.across)
            for core in range(2)
        ]
        self.token_groups = [
            [self.device(zhi, rest, xx, core) for core in range(2) for rest in range(self.half)]
            for xx in range(self.across)
            for zhi in range(2)
        ]

    def device(self, zhi, rest, xx, core):
        return (zhi * self.half + rest) * self.cols + xx * 2 + core

    def here(self):
        row, col = lax.axis_index("row"), lax.axis_index("col")
        return row // self.half, row % self.half, col // 2, col % 2

    def same(self):
        zhi, _, _, core = self.here()
        return zhi == core

    def block(self):
        _, rest, _, core = self.here()
        return core * self.half + rest

    def send(self, value, target):
        pairs = []
        for place in self.places:
            to = target(*place)
            if to is not None:
                pairs.append((self.device(*place), self.device(*to)))
        return lax.ppermute(value, BOTH, pairs)

    def swap(self, value):
        moved = self.send(
            value,
            lambda zhi, rest, xx, core: None if zhi == core else (core, rest, xx, zhi),
        )
        return jnp.where(self.same(), value, moved)

    def partner(self, value, flip):
        def target(zhi, rest, xx, core):
            to = (core * self.half + rest) ^ flip
            return zhi, to % self.half, xx, to // self.half

        return self.send(value, target)

    def token_gather(self, value):
        return lax.all_gather(
            value, BOTH, axis=0, tiled=True, axis_index_groups=self.token_groups
        )

    def weight_pair(self, value):
        def outward(zhi, rest, xx, core):
            return (1 - zhi, rest, xx, core) if zhi == core else (zhi, rest, xx, 1 - core)

        def over(zhi, rest, xx, core):
            return None if zhi == core else (1 - zhi, rest, xx, 1 - core)

        first = self.send(value, outward)
        second = self.send(value, over)
        same = self.same()
        return jnp.where(same, value, first), jnp.where(same, first, second)

    def weight_pieces(self, pair):
        _, _, xx, core = self.here()
        pieces = []
        for flip in range(self.across):
            for j, part in enumerate(pair):
                if flip:
                    part = self.send(part, lambda z, r, x, c: (z, r, x ^ flip, c))
                pieces.append(((xx ^ flip) * 2 + (core ^ j), part))
        return pieces

    def weight_exchange(self, value, axis):
        xx = self.here()[2]
        size = value.shape[axis] // self.across
        received = []
        for step in range(1, self.across):
            part = lax.dynamic_slice_in_dim(value, (xx + step) % self.across * size, size, axis)
            received.append(
                self.send(part, lambda z, r, x, c: (z, r, (x + step) % self.across, c))
            )
        return jnp.stack(received)

    def weight_sum(self, value, received, axis):
        size = value.shape[axis] // self.across
        total = lax.dynamic_slice_in_dim(value, self.here()[2] * size, size, axis)
        total = total.astype(jnp.float32)
        for step in range(self.across - 1):
            total = total + received[step].astype(jnp.float32)
        return total.astype(jnp.bfloat16)

    def weight_send(self, total, axis):
        core = self.here()[3]
        size = total.shape[axis] // 2
        near = lax.dynamic_slice_in_dim(total, core * size, size, axis)
        far = lax.dynamic_slice_in_dim(total, (1 - core) * size, size, axis)
        same = self.same()

        def outward(zhi, rest, xx, core):
            return (zhi, rest, xx, 1 - core) if zhi == core else (1 - zhi, rest, xx, core)

        def over(zhi, rest, xx, core):
            return None if zhi == core else (1 - zhi, rest, xx, 1 - core)

        first = self.send(jnp.where(same, far, near), outward)
        second = self.send(far, over)
        return jnp.where(same, near, second).astype(jnp.float32) + first.astype(jnp.float32)


def join(shape, pieces):
    whole = jnp.zeros(shape, pieces[0][2].dtype)
    for row, col, piece in pieces:
        whole = lax.dynamic_update_slice(whole, piece, (row, col))
    return whole


def after(value, *others):
    return lax.optimization_barrier((value, *others))[0]


def contract_rows(left, right):
    return lax.dot_general(
        left, right, (((0,), (0,)), ((), ())), preferred_element_type=jnp.float32
    )


def contract_cols(left, right):
    return lax.dot_general(
        left, right, (((1,), (1,)), ((), ())), preferred_element_type=jnp.float32
    )


def position(plan):
    row, col = lax.axis_index("row"), lax.axis_index("col")
    zhi, rest, core = row // plan.half, row % plan.half, col % 2
    return zhi, rest, col - core, core


def remote(source, target, send_sem, recv_sem, row, col):
    return pltpu.make_async_remote_copy(
        src_ref=source,
        dst_ref=target,
        send_sem=send_sem,
        recv_sem=recv_sem,
        device_id=(row, col),
        device_id_type=MESH,
    )


def swap_kernel(plan, given, taken, send_sem, recv_sem):
    zhi, rest, base, core = position(plan)
    far_row, near_col = (1 - zhi) * plan.half + rest, base + 1 - core
    barrier = pltpu.get_barrier_semaphore()
    pl.semaphore_signal(barrier, 1, device_id=(far_row, near_col), device_id_type=MESH)
    pl.semaphore_wait(barrier, 1)

    @pl.when(zhi != core)
    def _():
        remote(given, taken, send_sem, recv_sem, far_row, near_col).start()
        remote(given, taken, send_sem, recv_sem, far_row, near_col).wait()

    @pl.when(zhi == core)
    def _():
        pltpu.make_async_copy(given, taken, recv_sem).start()
        pltpu.make_async_copy(given, taken, recv_sem).wait()


def swap_tokens(plan, value, collective_id):
    anywhere = pl.BlockSpec(memory_space=pl.ANY)
    return pl.pallas_call(
        functools.partial(swap_kernel, plan),
        in_specs=[anywhere],
        out_specs=anywhere,
        out_shape=jax.ShapeDtypeStruct(value.shape, value.dtype),
        scratch_shapes=[pltpu.SemaphoreType.DMA, pltpu.SemaphoreType.DMA],
        cost_estimate=pl.CostEstimate(flops=0, bytes_accessed=2**27, transcendentals=0),
        compiler_params=pltpu.CompilerParams(collective_id=collective_id, has_side_effects=True),
    )(value)


def gather_kernel(plan, axes, *refs):
    count = len(axes)
    weights, wholes, sems = refs[:count], refs[count : 2 * count], refs[2 * count :]
    block_sem, block_recv_sem, side_sem, side_recv_sem = sems
    half, across = plan.half, plan.across
    zhi, rest, base, core = position(plan)
    xx = base // 2
    row, col = zhi * half + rest, base + core
    far_row, near_col = (1 - zhi) * half + rest, base + 1 - core
    moved, stays = zhi != core, zhi == core

    barrier = pltpu.get_barrier_semaphore()
    greeted = [(row, near_col), (far_row, col), (far_row, near_col)]
    greeted += [(row, (xx + step) % across * 2 + core) for step in range(1, across)]
    for device in greeted:
        pl.semaphore_signal(barrier, 1, device_id=device, device_id_type=MESH)
    pl.semaphore_wait(barrier, len(greeted))

    def place(index, other, j):
        axis = axes[index]
        size = weights[index].shape[axis]
        at = pl.ds(pl.multiple_of((other * 2 + j) * size, size), size)
        return wholes[index].at[at] if axis == 0 else wholes[index].at[:, at]

    def block_keep(index, j):
        return pltpu.make_async_copy(
            weights[index], place(index, xx, j), block_recv_sem.at[index, j]
        )

    def block_send(index, way, to_row, to_col):
        return remote(
            weights[index],
            place(index, xx, core),
            block_sem.at[index, way],
            block_recv_sem.at[index, core],
            to_row,
            to_col,
        )

    def side(index, step, j):
        at = place(index, xx, j)
        other = (xx + step) % across * 2 + core
        return remote(
            at, at, side_sem.at[index, step - 1, j], side_recv_sem.at[index, step - 1, j], row, other
        )

    for index in range(count):

        @pl.when(moved)
        def _():
            block_send(index, 0, row, near_col).start()
            block_send(index, 1, far_row, near_col).start()

        @pl.when(stays)
        def _():
            block_keep(index, core).start()
            block_send(index, 0, far_row, col).start()

    for index in range(count):
        for j in range(2):
            block_keep(index, j).wait()
            for step in range(1, across):
                side(index, step, j).start()
    for index in range(count):
        for j in range(2):
            for step in range(1, across):
                side(index, step, j).wait()

        @pl.when(moved)
        def _():
            block_send(index, 0, row, near_col).wait_send()
            block_send(index, 1, far_row, near_col).wait_send()

        @pl.when(stays)
        def _():
            block_send(index, 0, far_row, col).wait_send()


def gather_weights(plan, weights, axes, collective_id):
    count = len(weights)
    dma = pltpu.SemaphoreType.DMA
    anywhere = pl.BlockSpec(memory_space=pl.ANY)
    return pl.pallas_call(
        functools.partial(gather_kernel, plan, axes),
        in_specs=[anywhere] * count,
        out_specs=[anywhere] * count,
        out_shape=[
            jax.ShapeDtypeStruct(grow(weight.shape, axis, plan.cols), weight.dtype)
            for weight, axis in zip(weights, axes, strict=True)
        ],
        scratch_shapes=[
            dma((count, 2)),
            dma((count, 2)),
            dma((count, plan.across - 1, 2)),
            dma((count, plan.across - 1, 2)),
        ],
        cost_estimate=pl.CostEstimate(flops=0, bytes_accessed=2**28, transcendentals=0),
        compiler_params=pltpu.CompilerParams(collective_id=collective_id, has_side_effects=True),
    )(*weights)


def sum_kernel(plan, own, out, landed, send_sem, recv_sem):
    half, rows = plan.half, plan.rows
    zhi, rest, base, core = position(plan)

    def device(step):
        block = (core * half + rest + step) % rows
        return zhi * half + block % half, base + block // half

    barrier = pltpu.get_barrier_semaphore()
    for step in range(1, rows):
        pl.semaphore_signal(barrier, 1, device_id=device(step), device_id_type=MESH)
    pl.semaphore_wait(barrier, rows - 1)
    copies = [
        remote(
            own, landed.at[step - 1], send_sem.at[step - 1], recv_sem.at[step - 1], *device(step)
        )
        for step in range(1, rows)
    ]
    for copy in copies:
        copy.start()
    total = own[...]
    for step, copy in enumerate(copies):
        copy.wait_recv()
        total = total + landed[step]
    out[...] = total
    for copy in copies:
        copy.wait_send()


def group_sum(plan, value, collective_id):
    others = plan.rows - 1
    inside = pl.BlockSpec(memory_space=pltpu.VMEM)
    dma = pltpu.SemaphoreType.DMA
    return pl.pallas_call(
        functools.partial(sum_kernel, plan),
        in_specs=[inside],
        out_specs=inside,
        out_shape=jax.ShapeDtypeStruct(value.shape, value.dtype),
        scratch_shapes=[
            pltpu.VMEM((others, *value.shape), value.dtype),
            dma((others,)),
            dma((others,)),
        ],
        cost_estimate=pl.CostEstimate(
            flops=value.size * others, bytes_accessed=2**24, transcendentals=0
        ),
        compiler_params=pltpu.CompilerParams(collective_id=collective_id, has_side_effects=True),
    )(value)


def scatter_kernel(plan, parts, axes, turned, last, swaps, *refs):
    half, across, count = plan.half, plan.across, len(axes)
    lefts, weight, refs = refs[:parts], refs[parts], refs[parts + 1 :]
    grads, refs = refs[:count], refs[count:]
    if last:
        residual, refs = refs[0], refs[1:]
    if swaps:
        given, refs = refs[0], refs[1:]
    out, blocks, refs = refs[0], refs[1 : count + 1], refs[count + 1 :]
    if last:
        sums, refs = refs[0], refs[1:]
    if swaps:
        taken, refs = refs[0], refs[1:]
    loaded, near_out, near_in, far_out, far_in = refs[:5]
    load_sem, near_sem, near_recv_sem, far_sem, far_recv_sem, block_sem, block_recv_sem = refs[5:12]
    refs = refs[12:]
    zhi, rest, base, core = position(plan)
    xx = base // 2
    row, col = zhi * half + rest, base + core
    far_row, near_col = (1 - zhi) * half + rest, base + 1 - core
    moved, stays = zhi != core, zhi == core
    part, width = near_out.shape[1:]
    rows = 2 * part
    tile = min(512, width)

    barrier = pltpu.get_barrier_semaphore()
    side_y = half // 2
    zlo, y = rest // side_y, rest % side_y
    base_row = zhi * half

    def split(unit):
        h, index = unit // half, unit % half
        first = side_y + h * (2 - side_y)
        second = half // first
        ahead = first - 1 - index // second
        aside = second - 1 - index % second
        place = y + h * (zlo - y)
        other = zlo + h * (y - zlo)
        return h, (place + ahead) % first, (other + aside) % second, place, other, ahead

    def chip_of(h, along, beside):
        return (beside + h * (along - beside)) * side_y + along + h * (beside - along)

    greeted = [(row, near_col), (base_row + (1 - zlo) * side_y + y, col)]
    greeted += [(base_row + zlo * side_y + (y + step) % side_y, col) for step in range(1, side_y)]
    if count:
        greeted += [(row, (xx + step) % across * 2 + core) for step in range(1, across)]
    if last:
        greeted += [(far_row, col)]
    if last or swaps:
        greeted += [(far_row, near_col)]
    for device in greeted:
        pl.semaphore_signal(barrier, 1, device_id=device, device_id_type=MESH)

    def block(index, step):
        grad, axis = grads[index], axes[index]
        other = (xx + step) % across
        size = grad.shape[axis] // across
        at = pl.ds(pl.multiple_of(other * size, size), size)
        return remote(
            grad.at[at] if axis == 0 else grad.at[:, at],
            blocks[index].at[step - 1],
            block_sem.at[index, step - 1],
            block_recv_sem.at[index, step - 1],
            row,
            other * 2 + core,
        )

    def load(unit, whose, slot):
        h, along, beside = split(unit)[:3]
        side = (1 - core) if whose == 0 else core
        index = side * half + chip_of(h, along, beside)
        target, sem = loaded.at[slot, whose], load_sem.at[slot, whose]
        if parts == 1:
            at = pl.ds(pl.multiple_of(index * rows + h * part, part), part)
            return [(None, pltpu.make_async_copy(lefts[0].at[at], target, sem))]
        at = pl.ds(pl.multiple_of(index * part, part), part)
        return [
            (h == k, pltpu.make_async_copy(lefts[k].at[at], target, sem)) for k in range(2)
        ]

    def start(copies):
        for when, copy in copies:
            if when is None:
                copy.start()
            else:
                pl.when(when)(copy.start)

    def near(unit, slot):
        return remote(
            near_out.at[slot],
            near_in.at[unit],
            near_sem.at[unit],
            near_recv_sem.at[unit],
            row,
            near_col,
        )

    def far(unit):
        h, along, beside, place, other, ahead = split(unit)
        straight = (ahead + half - 1) // half
        chip = chip_of(h, along, beside + straight * (other - beside))
        return remote(
            far_out.at[unit],
            far_in.at[unit],
            far_sem.at[unit],
            far_recv_sem.at[unit],
            base_row + chip,
            col,
        )

    def product(left, cols):
        if turned:
            return contract_cols(left, weight[cols, :])
        return jnp.dot(left, weight[:, cols], preferred_element_type=jnp.float32)

    def columns(n):
        return pl.ds(pl.multiple_of(n * tile, tile), tile)

    def exchange():
        return remote(given, taken, refs[0], refs[1], far_row, near_col)

    def keep():
        return pltpu.make_async_copy(given, taken, refs[1])

    start(load(0, 0, 0))
    pl.semaphore_wait(barrier, len(greeted))
    if swaps:
        pl.when(moved)(lambda: exchange().start())
        pl.when(stays)(lambda: keep().start())
    for index in range(count):
        for step in range(1, across):
            block(index, step).start()

    def line_sum(h, aside):
        first = side_y if h == 0 else 2
        second = half // first
        at = h * half + second - 1 - aside
        value = far_out[at + (first - 1) * second].astype(jnp.float32)
        for ahead in range(first - 1):
            unit = at + ahead * second
            far(unit).wait_recv()
            value = value + far_in[unit].astype(jnp.float32)
        return value

    def second_stage(h):
        second = 2 if h == 0 else side_y
        for aside in range(second - 1, 0, -1):
            unit = (h + 1) * half - 1 - aside
            far_out[unit] = line_sum(h, aside).astype(far_out.dtype)
            far(unit).start()

    def body(unit, carry):
        slot = unit % 2
        before = unit - 1

        @pl.when(unit + 1 < 2 * half)
        def _():
            start(load(unit + 1, 0, 1 - slot))

        @pl.when(unit < 2 * half)
        def _():
            start(load(unit, 1, 1 - slot))
            load(unit, 0, slot)[0][1].wait()

            @pl.when(unit >= 2)
            def _():
                near(unit - 2, slot).wait_send()

            @pl.loop(0, width // tile)
            def _(n):
                value = product(loaded[slot, 0], columns(n))
                near_out[slot, :, columns(n)] = value.astype(near_out.dtype)

            near(unit, slot).start()

        @pl.when(unit >= 1)
        def _():
            load(before, 1, slot)[0][1].wait()
            near(before, 1 - slot).wait_recv()

            @pl.loop(0, width // tile)
            def _(n):
                value = product(loaded[slot, 1], columns(n))
                value = value + near_in[before, :, columns(n)].astype(jnp.float32)
                far_out[before, :, columns(n)] = value.astype(far_out.dtype)

            @pl.when(split(before)[5] > 0)
            def _():
                far(before).start()

            @pl.when(unit == half + half // 2)
            def _():
                second_stage(0)

        return carry

    lax.fori_loop(0, 2 * half + 1, body, 0)

    def total(h):
        value = line_sum(h, 0)
        second = 2 if h == 0 else side_y
        for aside in range(second - 1, 0, -1):
            unit = (h + 1) * half - 1 - aside
            far(unit).wait_recv()
            value = value + far_in[unit].astype(jnp.float32)
        return value

    if last:
        finish_sum = finish(
            (zhi, rest, xx, core), (row, col, far_row, near_col), grads, blocks, block, sums, refs
        )
        final, final_sem, final_recv_sem = refs[:3]

        def swap_far(h):
            return remote(
                final.at[h],
                out.at[pl.ds(h * part, part)],
                final_sem.at[h],
                final_recv_sem.at[h],
                far_row,
                near_col,
            )

        def swap_near(h):
            return pltpu.make_async_copy(
                final.at[h], out.at[pl.ds(h * part, part)], final_recv_sem.at[h]
            )

        for h in range(2):
            value = total(h) + residual[h * part : (h + 1) * part, :]
            final[h] = value.astype(final.dtype)

            @pl.when(moved)
            def _():
                swap_far(h).start()

            @pl.when(stays)
            def _():
                swap_near(h).start()

            if h == 0:
                second_stage(1)
                finish_sum()

        for h in range(2):

            @pl.when(moved)
            def _():
                swap_far(h).wait()

            @pl.when(stays)
            def _():
                swap_near(h).wait()

    else:
        second_stage(1)
        for h in range(2):
            out[h * part : (h + 1) * part, :] = total(h)
        for index in range(count):
            for step in range(1, across):
                block(index, step).wait_recv()
    if swaps:
        pl.when(moved)(lambda: exchange().wait())
        pl.when(stays)(lambda: keep().wait())
    for h in range(2):
        for unit in range(h * half, h * half + half - 1):
            far(unit).wait_send()
    for unit in range(2 * half - 2, 2 * half):
        near(unit, unit % 2).wait_send()
    for index in range(count):
        for step in range(1, across):
            block(index, step).wait_send()


def finish(place, devices, grads, blocks, block, sums, refs):
    zhi, _, xx, core = place
    row, col, far_row, near_col = devices
    grad, blocks = grads[0], blocks[0]
    mine, others, pair, landed, mine_sem, pair_sem, landed_sem = refs[3:]
    size = pair.shape[1]
    across = blocks.shape[0] + 1
    own = pltpu.make_async_copy(
        grad.at[pl.ds(pl.multiple_of(xx * 2 * size, size), 2 * size)], mine, mine_sem.at[0]
    )
    rest = [
        pltpu.make_async_copy(blocks.at[step], others.at[step], mine_sem.at[step + 1])
        for step in range(across - 1)
    ]

    def give(index, slot, to_row, to_col, to_slot):
        return remote(
            pair.at[slot],
            landed.at[to_slot],
            pair_sem.at[index],
            landed_sem.at[to_slot],
            to_row,
            to_col,
        )

    to_sibling = give(0, 1 - core, row, near_col, 0)
    to_same = give(0, core, far_row, col, 0)
    to_cross = give(1, 1 - core, far_row, near_col, 1)
    own.start()

    def run():
        for step in range(1, across):
            block(0, step).wait_recv()
            rest[step - 1].start()
        own.wait()
        for copy in rest:
            copy.wait()
        value = mine[...].astype(jnp.float32)
        for step in range(across - 1):
            value = value + others[step].astype(jnp.float32)
        pair[0] = value[:size].astype(pair.dtype)
        pair[1] = value[size:].astype(pair.dtype)

        @pl.when(zhi == core)
        def _():
            to_sibling.start()
            to_sibling.wait_send()
            give(0, core, far_row, col, 0).wait_recv()
            sums[...] = pair[core].astype(jnp.float32) + landed[0].astype(jnp.float32)

        @pl.when(zhi != core)
        def _():
            to_same.start()
            to_cross.start()
            to_same.wait_send()
            to_cross.wait_send()
            to_same.wait_recv()
            to_cross.wait_recv()
            sums[...] = landed[1].astype(jnp.float32) + landed[0].astype(jnp.float32)

    return run


def grow(shape, axis, pieces):
    return tuple(size * pieces if dim == axis else size for dim, size in enumerate(shape))


def cut(shape, axis, pieces):
    return tuple(size // pieces if dim == axis else size for dim, size in enumerate(shape))


def multiply_scatter(
    plan, lefts, weight, turned, collective_id, grads=(), axes=(), residual=None, swapped=None
):
    half, across, count = plan.half, plan.across, len(grads)
    depth = lefts[0].shape[1]
    width = weight.shape[0 if turned else 1]
    rows = sum(left.shape[0] for left in lefts) // plan.rows
    part = rows // 2
    low = jnp.bfloat16
    dma = pltpu.SemaphoreType.DMA
    anywhere = pl.BlockSpec(memory_space=pl.ANY)
    inside = pl.BlockSpec(memory_space=pltpu.VMEM)
    last = residual is not None
    swaps = swapped is not None
    in_specs = [anywhere] * len(lefts) + [inside] + [anywhere] * count + [inside] * last
    in_specs += [anywhere] * swaps
    out_specs = [anywhere if last else inside] + [anywhere] * count + [inside] * last
    out_shape = [jax.ShapeDtypeStruct((rows, width), low if last else jnp.float32)]
    out_shape += [
        jax.ShapeDtypeStruct((across - 1, *cut(grad.shape, axis, across)), low)
        for grad, axis in zip(grads, axes, strict=True)
    ]
    scratch = [
        pltpu.VMEM((2, 2, part, depth), low),
        pltpu.VMEM((2, part, width), low),
        pltpu.VMEM((2 * half, part, width), low),
        pltpu.VMEM((2 * half, part, width), low),
        pltpu.VMEM((2 * half, part, width), low),
        dma((2, 2)),
        dma((2 * half,)),
        dma((2 * half,)),
        dma((2 * half,)),
        dma((2 * half,)),
        dma((max(count, 1), across - 1)),
        dma((max(count, 1), across - 1)),
    ]
    if last:
        size, wide = grads[0].shape[0] // plan.cols, grads[0].shape[1]
        out_shape.append(jax.ShapeDtypeStruct((size, wide), jnp.float32))
        scratch += [
            pltpu.VMEM((2, part, width), low),
            dma((2,)),
            dma((2,)),
            pltpu.VMEM((2 * size, wide), low),
            pltpu.VMEM((across - 1, 2 * size, wide), low),
            pltpu.VMEM((2, size, wide), low),
            pltpu.VMEM((2, size, wide), low),
            dma((across,)),
            dma((2,)),
            dma((2,)),
        ]
    if swaps:
        out_shape.append(jax.ShapeDtypeStruct(swapped.shape, swapped.dtype))
        scratch += [dma, dma]
    return pl.pallas_call(
        functools.partial(scatter_kernel, plan, len(lefts), axes, turned, last, swaps),
        in_specs=in_specs,
        out_specs=out_specs + [anywhere] * swaps,
        out_shape=out_shape,
        scratch_shapes=scratch,
        cost_estimate=pl.CostEstimate(
            flops=2 * rows * plan.rows * depth * width,
            bytes_accessed=20 * rows * plan.rows * width,
            transcendentals=0,
        ),
        compiler_params=pltpu.CompilerParams(
            collective_id=collective_id, has_side_effects=True, vmem_limit_bytes=58 * 2**20
        ),
    )(*lefts, weight, *grads, *([residual] if last else []), *([swapped] if swaps else []))


def unit_grad_kernel(left, weight, both, out):
    width = weight.shape[0]
    grad = contract_cols(left[...], weight[...])
    gate = both[:, :width].astype(jnp.float32)
    up = both[:, width:].astype(jnp.float32)
    sigmoid = jax.nn.sigmoid(gate)
    scaled = grad * sigmoid
    out[:, :width] = (scaled * up * (1.0 + gate * (1.0 - sigmoid))).astype(out.dtype)
    out[:, width:] = (scaled * gate).astype(out.dtype)


def unit_grad(left, weight, both):
    seq_len, depth = left.shape
    rows = min(256, seq_len)
    width = weight.shape[0]
    wide = pl.BlockSpec((rows, 2 * width), lambda i: (i, 0))
    return pl.pallas_call(
        unit_grad_kernel,
        grid=(seq_len // rows,),
        in_specs=[pl.BlockSpec((rows, depth), lambda i: (i, 0)), full(width, depth), wide],
        out_specs=wide,
        out_shape=jax.ShapeDtypeStruct((seq_len, 2 * width), jnp.bfloat16),
        cost_estimate=pl.CostEstimate(
            flops=2 * seq_len * depth * width,
            bytes_accessed=2 * seq_len * (depth + 4 * width),
            transcendentals=seq_len * width,
        ),
        compiler_params=pltpu.CompilerParams(vmem_limit_bytes=40 * 2**20),
    )(left, weight, both)


def full(rows, width):
    return pl.BlockSpec((rows, width), lambda *_: (0, 0))


def turn(values, cosine, sine):
    return values * cosine + pltpu.roll(values, values.shape[-1] // 2, 1) * sine


def column(row_vector, width):
    return jnp.transpose(jnp.broadcast_to(row_vector, (width, row_vector.shape[1])))


def project_kernel(head_size, first, second, weight, proj, squares):
    width = proj.shape[1] // 3
    rows = first.shape[0]
    for chunk, left in enumerate((first, second)):
        at = slice(chunk * rows, (chunk + 1) * rows)
        value = jnp.dot(left[...], weight[...], preferred_element_type=jnp.float32)
        proj[at, :] = value
        for place in range(2):
            total = None
            for start in range(place * width, (place + 1) * width, head_size):
                part = value[:, start : start + head_size] ** 2
                total = part if total is None else total + part
            squares[place : place + 1, at] = jnp.sum(jnp.transpose(total), axis=0, keepdims=True)


def project(lefts, weight, head_size, own_tokens):
    rows, depth = lefts[0].shape
    wide = weight.shape[1]
    part = pl.BlockSpec((own_tokens // 2, depth), lambda i: (i, 0))
    return pl.pallas_call(
        functools.partial(project_kernel, head_size),
        grid=(2 * rows // own_tokens,),
        in_specs=[part, part, full(depth, wide)],
        out_specs=[
            pl.BlockSpec((own_tokens, wide), lambda i: (i, 0)),
            pl.BlockSpec((2, own_tokens), lambda i: (0, i)),
        ],
        out_shape=[
            jax.ShapeDtypeStruct((2 * rows, wide), jnp.float32),
            jax.ShapeDtypeStruct((2, 2 * rows), jnp.float32),
        ],
        cost_estimate=pl.CostEstimate(
            flops=4 * rows * depth * wide,
            bytes_accessed=4 * rows * depth + 8 * rows * wide,
            transcendentals=0,
        ),
        compiler_params=pltpu.CompilerParams(vmem_limit_bytes=40 * 2**20),
    )(*lefts, weight)


def prepare_kernel(
    head_size, proj, query_inv, key_inv, cosine, sine, query_gain, key_gain, query, key, value
):
    width = query.shape[1]
    turns = (cosine[...], sine[...])
    for source, inv, gain, target in (
        (0, query_inv, query_gain, query),
        (width, key_inv, key_gain, key),
    ):
        factor = column(inv[...], head_size)
        for start in range(0, width, head_size):
            part = proj[:, source + start : source + start + head_size]
            scaled = part * factor * gain[:, start : start + head_size]
            target[:, start : start + head_size] = turn(scaled, *turns).astype(target.dtype)
    value[...] = proj[:, 2 * width :].astype(value.dtype)


def prepare(proj, query_inv, key_inv, cosine, sine, query_gain, key_gain, head_size):
    seq_len, width = proj.shape[0], proj.shape[1] // 3
    rows = min(512, seq_len)
    return pl.pallas_call(
        functools.partial(prepare_kernel, head_size),
        grid=(seq_len // rows,),
        in_specs=[
            pl.BlockSpec((rows, 3 * width), lambda i: (i, 0)),
            pl.BlockSpec((1, rows), lambda i: (0, i)),
            pl.BlockSpec((1, rows), lambda i: (0, i)),
            pl.BlockSpec((rows, head_size), lambda i: (i, 0)),
            pl.BlockSpec((rows, head_size), lambda i: (i, 0)),
            full(1, width),
            full(1, width),
        ],
        out_specs=[pl.BlockSpec((rows, width), lambda i: (i, 0))] * 3,
        out_shape=[jax.ShapeDtypeStruct((seq_len, width), jnp.bfloat16)] * 3,
        cost_estimate=pl.CostEstimate(
            flops=10 * seq_len * width, bytes_accessed=seq_len * width * 20, transcendentals=0
        ),
        compiler_params=pltpu.CompilerParams(vmem_limit_bytes=40 * 2**20),
    )(proj, query_inv, key_inv, cosine, sine, query_gain, key_gain)


def allowed(first, key_block, query_block, key_rows, query_rows):
    key_index = key_block * key_rows + lax.broadcasted_iota(
        jnp.int32, (key_rows, query_rows), 0
    )
    query_index = query_block * query_rows + lax.broadcasted_iota(
        jnp.int32, (key_rows, query_rows), 1
    )
    return (key_index <= query_index) & (key_index >= first)


def attend_kernel(rows, low, first, query, key, value, *refs):
    out, log_sum = refs[-2:]
    step = pl.program_id(1)
    head_size = query.shape[1]
    factor = LOG2E * head_size**-0.5
    queries = query[...]
    starts = first[...]

    def one(index, carry):
        top, total, acc = carry
        at = pl.ds(pl.multiple_of(index * rows, rows), rows)
        scores = contract_cols(key[at, :], queries) * factor
        scores = jnp.where(allowed(starts, index, step, rows, rows), scores, MASKED)
        new_top = jnp.maximum(top, jnp.max(scores, axis=0, keepdims=True))
        probs = jnp.exp2(scores - new_top)
        fade = jnp.exp2(top - new_top)
        total = total * fade + jnp.sum(probs, axis=0, keepdims=True)
        acc = acc * fade + contract_rows(value[at, :], probs.astype(jnp.bfloat16))
        return new_top, total, acc

    top, total, acc = lax.fori_loop(
        low[step],
        step + 1,
        one,
        (
            jnp.full((1, rows), MASKED, jnp.float32),
            jnp.zeros((1, rows), jnp.float32),
            jnp.zeros((head_size, rows), jnp.float32),
        ),
    )
    out[...] = jnp.transpose(acc / total).astype(out.dtype)
    log_sum[0] = top + jnp.log2(total)


def attend(low, first, query, key, value, head_size, rows, more):
    seq_len, width = query.shape
    heads = width // head_size
    whole = pl.BlockSpec((seq_len, head_size), lambda h, i, *_: (0, h))
    block = pl.BlockSpec((rows, head_size), lambda h, i, *_: (i, h))
    return pl.pallas_call(
        functools.partial(attend_kernel, rows),
        grid_spec=pltpu.PrefetchScalarGridSpec(
            num_scalar_prefetch=1,
            grid=(heads, seq_len // rows),
            in_specs=[
                pl.BlockSpec((1, rows), lambda h, i, *_: (0, i)),
                block,
                whole,
                whole,
            ]
            + [pl.BlockSpec(memory_space=pl.ANY)] * len(more),
            out_specs=[block, pl.BlockSpec((1, 1, rows), lambda h, i, *_: (h, 0, i))],
        ),
        out_shape=[
            jax.ShapeDtypeStruct((seq_len, width), jnp.bfloat16),
            jax.ShapeDtypeStruct((heads, 1, seq_len), jnp.float32),
        ],
        cost_estimate=pl.CostEstimate(
            flops=seq_len * seq_len * width, bytes_accessed=seq_len * width * 8, transcendentals=0
        ),
        compiler_params=pltpu.CompilerParams(vmem_limit_bytes=40 * 2**20),
    )(low, first, query, key, value, *more)


def attend_back_kernel(
    rows,
    high,
    first,
    query,
    key,
    value,
    out,
    out_grad,
    log_sum,
    *refs,
):
    query_grad, key_grad, value_grad, delta = refs[-4:]
    step = pl.program_id(1)
    seq_len, head_size = query.shape
    factor = LOG2E * head_size**-0.5

    @pl.when(step == 0)
    def _():
        query_grad[...] = jnp.zeros_like(query_grad)

        @pl.loop(0, seq_len // rows)
        def _(index):
            at = pl.ds(pl.multiple_of(index * rows, rows), rows)
            product = out_grad[at, :].astype(jnp.float32) * out[at, :].astype(jnp.float32)
            delta[:, at] = jnp.sum(jnp.transpose(product), axis=0, keepdims=True)

    keys = key[...]
    values = value[...]

    def one(index, carry):
        key_acc, value_acc = carry
        at = pl.ds(pl.multiple_of(index * rows, rows), rows)
        queries = query[at, :]
        grads = out_grad[at, :]
        scores = contract_cols(keys, queries) * factor
        mask = allowed(first[:, at], step, index, rows, rows)
        probs = jnp.exp2(jnp.where(mask, scores - log_sum[0, :, at], MASKED))
        value_acc = value_acc + jnp.dot(
            probs.astype(jnp.bfloat16), grads, preferred_element_type=jnp.float32
        )
        prob_grad = contract_cols(values, grads)
        score_grad = (probs * (prob_grad - delta[:, at])).astype(jnp.bfloat16)
        key_acc = key_acc + jnp.dot(score_grad, queries, preferred_element_type=jnp.float32)
        query_grad[at, :] += contract_rows(score_grad, keys)
        return key_acc, value_acc

    zeros = jnp.zeros((rows, head_size), jnp.float32)
    key_acc, value_acc = lax.fori_loop(step, high[step] + 1, one, (zeros, zeros))
    key_grad[...] = key_acc
    value_grad[...] = value_acc.astype(value_grad.dtype)


def attend_back(high, first, query, key, value, out, out_grad, log_sum, head_size, rows, more):
    seq_len, width = query.shape
    heads = width // head_size
    whole = pl.BlockSpec((seq_len, head_size), lambda h, j, *_: (0, h))
    block = pl.BlockSpec((rows, head_size), lambda h, j, *_: (j, h))
    return pl.pallas_call(
        functools.partial(attend_back_kernel, rows),
        grid_spec=pltpu.PrefetchScalarGridSpec(
            num_scalar_prefetch=1,
            grid=(heads, seq_len // rows),
            in_specs=[
                full(1, seq_len),
                whole,
                block,
                block,
                whole,
                whole,
                pl.BlockSpec((1, 1, seq_len), lambda h, j, *_: (h, 0, 0)),
            ]
            + [pl.BlockSpec(memory_space=pl.ANY)] * len(more),
            out_specs=[whole, block, block],
            scratch_shapes=[pltpu.VMEM((1, seq_len), jnp.float32)],
        ),
        out_shape=[
            jax.ShapeDtypeStruct((seq_len, width), jnp.float32),
            jax.ShapeDtypeStruct((seq_len, width), jnp.float32),
            jax.ShapeDtypeStruct((seq_len, width), jnp.bfloat16),
        ],
        cost_estimate=pl.CostEstimate(
            flops=3 * seq_len * seq_len * width,
            bytes_accessed=seq_len * width * 20,
            transcendentals=0,
        ),
        compiler_params=pltpu.CompilerParams(vmem_limit_bytes=48 * 2**20),
    )(high, first, query, key, value, out, out_grad, log_sum, *more)


def norm_back_kernel(
    head_size,
    proj,
    query_inv,
    key_inv,
    cosine,
    sine,
    query_gain,
    key_gain,
    query_grad,
    key_grad,
    dots,
    gain_sums,
):
    width = query_grad.shape[1]
    turns = (cosine[...], -sine[...])
    scale = head_size**-0.5

    @pl.when(pl.program_id(0) == 0)
    def _():
        gain_sums[...] = jnp.zeros_like(gain_sums)

    for place, (source, inv, gain, grad) in enumerate(
        ((0, query_inv, query_gain, query_grad), (width, key_inv, key_gain, key_grad))
    ):
        factor = column(inv[...], head_size)
        row_part = None
        for start in range(0, width, head_size):
            cols = slice(start, start + head_size)
            hat = proj[:, source + start : source + start + head_size] * factor
            product = turn(grad[:, cols] * scale, *turns) * hat
            gain_sums[place : place + 1, cols] += jnp.sum(product, axis=0, keepdims=True)
            product = product * gain[:, cols]
            row_part = product if row_part is None else row_part + product
        dots[place : place + 1, :] = jnp.sum(jnp.transpose(row_part), axis=0, keepdims=True)


def norm_back(
    proj, query_inv, key_inv, cosine, sine, query_gain, key_gain, query_grad, key_grad, head_size
):
    seq_len, width = query_grad.shape
    rows = min(512, seq_len)
    wide = pl.BlockSpec((rows, width), lambda i: (i, 0))
    return pl.pallas_call(
        functools.partial(norm_back_kernel, head_size),
        grid=(seq_len // rows,),
        in_specs=[
            pl.BlockSpec((rows, 2 * width), lambda i: (i, 0)),
            pl.BlockSpec((1, rows), lambda i: (0, i)),
            pl.BlockSpec((1, rows), lambda i: (0, i)),
            pl.BlockSpec((rows, head_size), lambda i: (i, 0)),
            pl.BlockSpec((rows, head_size), lambda i: (i, 0)),
            full(1, width),
            full(1, width),
            wide,
            wide,
        ],
        out_specs=[pl.BlockSpec((2, rows), lambda i: (0, i)), full(2, width)],
        out_shape=[
            jax.ShapeDtypeStruct((2, seq_len), jnp.float32),
            jax.ShapeDtypeStruct((2, width), jnp.float32),
        ],
        cost_estimate=pl.CostEstimate(
            flops=20 * seq_len * width, bytes_accessed=seq_len * width * 20, transcendentals=0
        ),
        compiler_params=pltpu.CompilerParams(vmem_limit_bytes=40 * 2**20),
    )(proj, query_inv, key_inv, cosine, sine, query_gain, key_gain, query_grad, key_grad)


def proj_back_kernel(
    head_size,
    features,
    proj,
    query_inv,
    key_inv,
    cosine,
    sine,
    query_gain,
    key_gain,
    query_grad,
    key_grad,
    value_grad,
    dots,
    *rest,
):
    out = rest[-1]
    width = query_grad.shape[1]
    turns = (cosine[...], -sine[...])
    scale = head_size**-0.5
    for place, (source, inv, gain, grad) in enumerate(
        ((0, query_inv, query_gain, query_grad), (width, key_inv, key_gain, key_grad))
    ):
        factor = column(inv[...], head_size)
        mean = column(dots[place : place + 1, :] * (1.0 / features), head_size)
        for start in range(0, width, head_size):
            cols = slice(start, start + head_size)
            at = slice(source + start, source + start + head_size)
            hat = proj[:, at] * factor
            scaled = turn(grad[:, cols] * scale, *turns) * gain[:, cols]
            out[:, at] = (factor * (scaled - hat * mean)).astype(out.dtype)
    out[:, 2 * width :] = value_grad[...]


def proj_back(
    proj,
    query_inv,
    key_inv,
    cosine,
    sine,
    query_gain,
    key_gain,
    query_grad,
    key_grad,
    value_grad,
    dots,
    head_size,
    features,
    more,
):
    seq_len, width = query_grad.shape
    rows = min(512, seq_len)
    wide = pl.BlockSpec((rows, width), lambda i: (i, 0))
    return pl.pallas_call(
        functools.partial(proj_back_kernel, head_size, features),
        grid=(seq_len // rows,),
        in_specs=[
            pl.BlockSpec((rows, 2 * width), lambda i: (i, 0)),
            pl.BlockSpec((1, rows), lambda i: (0, i)),
            pl.BlockSpec((1, rows), lambda i: (0, i)),
            pl.BlockSpec((rows, head_size), lambda i: (i, 0)),
            pl.BlockSpec((rows, head_size), lambda i: (i, 0)),
            full(1, width),
            full(1, width),
            wide,
            wide,
            wide,
            pl.BlockSpec((2, rows), lambda i: (0, i)),
        ]
        + [pl.BlockSpec(memory_space=pl.ANY)] * len(more),
        out_specs=pl.BlockSpec((rows, 3 * width), lambda i: (i, 0)),
        out_shape=jax.ShapeDtypeStruct((seq_len, 3 * width), jnp.bfloat16),
        cost_estimate=pl.CostEstimate(
            flops=20 * seq_len * width, bytes_accessed=seq_len * width * 24, transcendentals=0
        ),
        compiler_params=pltpu.CompilerParams(vmem_limit_bytes=40 * 2**20),
    )(
        proj,
        query_inv,
        key_inv,
        cosine,
        sine,
        query_gain,
        key_gain,
        query_grad,
        key_grad,
        value_grad,
        dots,
        *more,
    )


def body(
    plan,
    layer_input,
    segments,
    w_query,
    w_key,
    w_value,
    w_out,
    query_gain,
    key_gain,
    attn_gain,
    w_gate,
    w_up,
    w_down,
    mlp_gain,
    cotangent,
):
    rows = plan.rows
    mine = plan.block()
    model_width = layer_input.shape[1]
    head_size = model_width // HEADS
    seq_len = segments.shape[0]
    own_tokens = seq_len // rows
    part = own_tokens // 2
    f32 = jnp.float32
    bf16 = jnp.bfloat16
    chunks = range(2)

    def chunk_of(value, k):
        return value[k * part : (k + 1) * part]

    qkv_own = jnp.concatenate([w_query, w_key, w_value], axis=1)
    own_depth, wide = qkv_own.shape
    small_own = jnp.concatenate([query_gain, key_gain, attn_gain, mlp_gain])
    gain_size, post_size = query_gain.shape[0], attn_gain.shape[0]
    cuts = (gain_size, 2 * gain_size, 2 * gain_size + post_size)
    small_size = small_own.shape[0]
    extra = 16

    def lines(vector):
        return jnp.pad(vector, (0, extra * wide - small_size)).reshape(extra, wide)

    own_weight = jnp.concatenate([qkv_own, lines(small_own)], axis=0)
    nearby = plan.send(
        segments, lambda z, r, x, c: (z, r, x, 1 - c) if z == c else None
    )
    segments = jnp.where(plan.same(), segments, nearby)
    own_x = swap_tokens(plan, after(layer_input, segments), 1)
    gathered_x = [plan.token_gather(chunk_of(own_x, k)) for k in chunks]
    both, out_rows, down_rows = gather_weights(
        plan, (after(own_weight, own_x), w_out, w_down), (0, 1, 1), 7
    )
    both = both.reshape(plan.cols, own_depth + extra, wide)
    proj_weight = both[:, :own_depth].reshape(-1, wide)
    small = both[:, own_depth:].reshape(plan.cols, extra * wide)[:, :small_size].astype(f32)
    query_scale, key_scale, attn_scale, mlp_scale = (
        value.reshape(1, -1) for value in jnp.split(small, cuts, axis=1)
    )

    out_full = plan.token_gather(out_rows)
    ff_width = w_gate.shape[1]

    local_width = wide // 3
    token_index = jnp.arange(seq_len, dtype=jnp.int32)
    change = jnp.concatenate([jnp.ones((1,), dtype=bool), segments[1:] != segments[:-1]])
    first = lax.cummax(jnp.where(change, token_index, 0), axis=0)
    places = (token_index - first).astype(f32)
    lane = jnp.arange(head_size, dtype=jnp.int32)
    half = head_size // 2
    freqs = THETA ** (-((lane % half).astype(f32) * 2.0) / head_size)
    angle = places[:, None] * freqs[None, :]
    cosine = jnp.cos(angle)
    sine = jnp.sin(angle) * jnp.where(lane < half, -1.0, 1.0)[None, :]
    tile = min(512, seq_len)
    low = first[::tile] // tile
    last = token_index[tile - 1 :: tile]
    ends = jnp.min(
        jnp.where(change[None, :] & (token_index[None, :] > last[:, None]), token_index, seq_len),
        axis=1,
    )
    high = (ends - 1) // tile
    first_row = first[None, :]

    proj, squares = project(gathered_x, proj_weight, head_size, own_tokens)
    invs = lax.rsqrt(group_sum(plan, squares, 5) / model_width + EPS)
    query_inv, key_inv = invs[:1], invs[1:]
    query, key, value = prepare(
        proj, query_inv, key_inv, cosine, sine, query_scale, key_scale, head_size
    )
    gate_pair = plan.weight_pair(after(w_gate, invs))
    up_pair = plan.weight_pair(after(w_up, query))
    attn_out, log_sum = attend(
        low, first_row, query, key, value, head_size, tile, gate_pair
    )

    attn_tokens = jnp.zeros((own_tokens, model_width), bf16)
    for flip in range(rows):
        other = mine ^ flip
        piece = lax.dynamic_slice(attn_out, (other * own_tokens, 0), (own_tokens, local_width))
        if flip:
            piece = plan.partner(piece, flip)
        attn_tokens = lax.dynamic_update_slice(attn_tokens, piece, (0, other * local_width))

    places, gate_pieces = zip(*plan.weight_pieces(gate_pair), strict=True)
    attn_tokens, *others = lax.optimization_barrier((attn_tokens, *gate_pieces, *up_pair))
    gate_pieces, up_pair = zip(places, others[:-2], strict=True), others[-2:]
    up_pieces = plan.weight_pieces(up_pair)
    ff_weight = join(
        (model_width, 2 * ff_width),
        [
            (c * own_depth, start, piece)
            for start, pieces in ((0, gate_pieces), (ff_width, up_pieces))
            for c, piece in pieces
        ],
    )
    def normed(value):
        inv = lax.rsqrt(jnp.mean(value * value, axis=-1, keepdims=True) + EPS)
        return inv, value * inv

    def norm_grad(inv, hat, scaled):
        mean = jnp.mean(scaled * hat, axis=-1, keepdims=True)
        return (inv * (scaled - hat * mean)).astype(bf16)

    attn_inv, attn_hat, hidden, gathered_h = [], [], [], []
    for k in chunks:
        out_proj = jnp.dot(chunk_of(attn_tokens, k), out_full, preferred_element_type=f32)
        inv, hat = normed(out_proj)
        attn_inv.append(inv)
        attn_hat.append(hat)
        hidden.append(chunk_of(own_x, k).astype(f32) + hat * attn_scale)
        low = hidden[k].astype(bf16)
        if k:
            low = after(low, *(piece for _, piece in up_pieces))
        gathered_h.append(plan.token_gather(low))

    gate_up, activated = [], []
    for k in chunks:
        both = jnp.dot(gathered_h[k], ff_weight, preferred_element_type=f32).astype(bf16)
        gate_up.append(both)
        gate, up = both[:, :ff_width].astype(f32), both[:, ff_width:].astype(f32)
        activated.append((jax.nn.silu(gate) * up).astype(bf16))
    mlp_out, own_cot = multiply_scatter(
        plan, activated, down_rows, False, 2, swapped=cotangent
    )

    outputs, upstream, shard_rows = [], [], []
    mlp_gain_part = 0.0
    for k in chunks:
        inv, hat = normed(chunk_of(mlp_out, k))
        outputs.append((hidden[k] + hat * mlp_scale).astype(bf16))
        upstream.append(chunk_of(own_cot, k).astype(f32))
        mlp_gain_part += jnp.sum(upstream[k] * hat, axis=0)
        shard_rows.append(plan.token_gather(norm_grad(inv, hat, upstream[k] * mlp_scale)))

    ff_grad = []
    for k in chunks:
        ff_grad.append(unit_grad(shard_rows[k], down_rows, gate_up[k]))
    down_grad = sum(contract_rows(activated[k], shard_rows[k]) for k in chunks).astype(bf16)
    ff_weight_grad = sum(contract_rows(gathered_h[k], ff_grad[k]) for k in chunks).astype(bf16)
    hidden_grad_mlp, ff_blocks, layer_output = multiply_scatter(
        plan,
        ff_grad,
        ff_weight,
        True,
        3,
        (ff_weight_grad,),
        (0,),
        swapped=jnp.concatenate(outputs),
    )
    hidden_grad = [upstream[k] + chunk_of(hidden_grad_mlp, k) for k in chunks]
    ff_sum = plan.weight_send(plan.weight_sum(ff_weight_grad, ff_blocks, 0), 0)
    down_blocks = plan.weight_exchange(after(down_grad, ff_blocks), 1)

    attn_gain_part = 0.0
    proj_grads, token_grads = [], []
    for k in chunks:
        attn_gain_part += jnp.sum(hidden_grad[k] * attn_hat[k], axis=0)
        proj_grads.append(norm_grad(attn_inv[k], attn_hat[k], hidden_grad[k] * attn_scale))
        token_grads.append(contract_cols(proj_grads[k], out_full).astype(bf16))
    out_token_grad = jnp.concatenate(token_grads)

    attn_grad = jnp.zeros((seq_len, local_width), bf16)
    for flip in range(rows):
        other = mine ^ flip
        piece = lax.dynamic_slice(
            out_token_grad, (0, other * local_width), (own_tokens, local_width)
        )
        if flip:
            piece = plan.partner(piece, flip)
        attn_grad = lax.dynamic_update_slice(attn_grad, piece, (other * own_tokens, 0))

    out_grad = sum(
        contract_rows(
            attn_out.reshape(rows, 2, part, local_width)[:, k].reshape(-1, local_width),
            plan.token_gather(proj_grads[k]),
        )
        for k in chunks
    ).astype(bf16)
    out_sum = plan.weight_sum(out_grad, plan.weight_exchange(out_grad, 1), 1)
    query_grad, key_grad, value_grad = attend_back(
        high,
        first_row,
        query,
        key,
        value,
        attn_out,
        attn_grad,
        log_sum,
        head_size,
        tile,
        (down_blocks,),
    )
    down_sum = plan.weight_send(plan.weight_sum(down_grad, down_blocks, 1), 1)
    shared = (proj, query_inv, key_inv, cosine, sine, query_scale, key_scale, query_grad, key_grad)
    dots, gain_sums = norm_back(*shared, head_size)
    dots = group_sum(
        plan,
        jnp.concatenate([dots, jnp.stack([attn_gain_part, mlp_gain_part])], axis=1),
        6,
    )
    dots, post_sums = dots[:, :seq_len], dots[:, seq_len:]
    proj_grad_all = proj_back(
        *shared, value_grad, dots, head_size, model_width, (ff_sum,)
    )
    proj_grad_all = after(proj_grad_all, out_sum)
    halves = proj_grad_all.reshape(rows, 2, part, wide)
    proj_weight_grad = sum(
        contract_rows(gathered_x[k], halves[:, k].reshape(-1, wide)) for k in chunks
    ).astype(bf16)
    small = jnp.concatenate(
        [
            gain_sums[0].reshape(plan.cols, -1),
            gain_sums[1].reshape(plan.cols, -1),
            post_sums[0].reshape(plan.cols, -1),
            post_sums[1].reshape(plan.cols, -1),
        ],
        axis=1,
    )
    small = jnp.pad(small, ((0, 0), (0, extra * wide - small_size)))
    small = small.reshape(plan.cols, extra, wide).astype(bf16)
    stacked = jnp.concatenate(
        [proj_weight_grad.reshape(plan.cols, own_depth, wide), small], axis=1
    )
    stacked = stacked.reshape(-1, wide)
    out_sum = plan.weight_send(out_sum, 1)
    stacked = after(stacked, out_sum, down_sum)
    input_grad, _, proj_sum = multiply_scatter(
        plan,
        [proj_grad_all],
        proj_weight,
        True,
        4,
        (stacked,),
        (0,),
        jnp.concatenate(hidden_grad),
    )
    small = proj_sum[own_depth:].reshape(-1)[:small_size]
    query_gain_sum, key_gain_sum, attn_gain_sum, mlp_gain_sum = jnp.split(small, cuts)
    proj_sum = proj_sum[:own_depth]
    own_ff = w_gate.shape[1]
    return (
        layer_output,
        input_grad,
        proj_sum[:, :local_width],
        proj_sum[:, local_width : 2 * local_width],
        proj_sum[:, 2 * local_width :],
        out_sum,
        query_gain_sum,
        key_gain_sum,
        attn_gain_sum,
        ff_sum[:, :own_ff],
        ff_sum[:, own_ff:],
        down_sum,
        mlp_gain_sum,
    )


def solution(mesh):
    tokens = P(("col", "row"), None)
    columns = P("col", "row")
    across = P("row", "col")
    vector = P(("row", "col"))
    return jax.shard_map(
        functools.partial(body, Plan(mesh)),
        mesh=mesh,
        in_specs=(
            tokens,
            P("col"),
            columns,
            columns,
            columns,
            across,
            vector,
            vector,
            P("col"),
            columns,
            columns,
            across,
            P("col"),
            tokens,
        ),
        out_specs=(
            tokens,
            tokens,
            columns,
            columns,
            columns,
            across,
            vector,
            vector,
            P("col"),
            columns,
            columns,
            across,
            P("col"),
        ),
        check_vma=False,
    )
```

```python
import functools

import jax
import jax.numpy as jnp
from jax import lax
from jax.experimental import pallas as pl
from jax.experimental.pallas import tpu as pltpu
from jax.sharding import PartitionSpec as P

HEADS = 16


EPS = 1e-06
THETA = 500000.0
MASKED = -1e30
LOG2E = 1.4426950408889634
BOTH = ("row", "col")
MESH = pl.DeviceIdType.MESH


class Plan:
    def __init__(self, mesh):
        self.rows, self.cols = mesh.shape["row"], mesh.shape["col"]
        self.half = self.rows // 2
        self.across = self.cols // 2
        self.places = [
            (zhi, rest, xx, core)
            for zhi in range(2)
            for rest in range(self.half)
            for xx in range(self.across)
            for core in range(2)
        ]
        self.token_groups = [
            [self.device(zhi, rest, xx, core) for core in range(2) for rest in range(self.half)]
            for xx in range(self.across)
            for zhi in range(2)
        ]

    def device(self, zhi, rest, xx, core):
        return (zhi * self.half + rest) * self.cols + xx * 2 + core

    def here(self):
        row, col = lax.axis_index("row"), lax.axis_index("col")
        return row // self.half, row % self.half, col // 2, col % 2

    def same(self):
        zhi, _, _, core = self.here()
        return zhi == core

    def block(self):
        _, rest, _, core = self.here()
        return core * self.half + rest

    def send(self, value, target):
        pairs = []
        for place in self.places:
            to = target(*place)
            if to is not None:
                pairs.append((self.device(*place), self.device(*to)))
        return lax.ppermute(value, BOTH, pairs)

    def swap(self, value):
        moved = self.send(
            value,
            lambda zhi, rest, xx, core: None if zhi == core else (core, rest, xx, zhi),
        )
        return jnp.where(self.same(), value, moved)

    def partner(self, value, flip):
        def target(zhi, rest, xx, core):
            to = (core * self.half + rest) ^ flip
            return zhi, to % self.half, xx, to // self.half

        return self.send(value, target)

    def token_gather(self, value):
        return lax.all_gather(
            value, BOTH, axis=0, tiled=True, axis_index_groups=self.token_groups
        )

    def weight_pair(self, value):
        def outward(zhi, rest, xx, core):
            return (1 - zhi, rest, xx, core) if zhi == core else (zhi, rest, xx, 1 - core)

        def over(zhi, rest, xx, core):
            return None if zhi == core else (1 - zhi, rest, xx, 1 - core)

        first = self.send(value, outward)
        second = self.send(value, over)
        same = self.same()
        return jnp.where(same, value, first), jnp.where(same, first, second)

    def weight_pieces(self, pair):
        _, _, xx, core = self.here()
        pieces = []
        for flip in range(self.across):
            for j, part in enumerate(pair):
                if flip:
                    part = self.send(part, lambda z, r, x, c: (z, r, x ^ flip, c))
                pieces.append(((xx ^ flip) * 2 + (core ^ j), part))
        return pieces

    def weight_exchange(self, value, axis):
        xx = self.here()[2]
        size = value.shape[axis] // self.across
        received = []
        for step in range(1, self.across):
            part = lax.dynamic_slice_in_dim(value, (xx + step) % self.across * size, size, axis)
            received.append(
                self.send(part, lambda z, r, x, c: (z, r, (x + step) % self.across, c))
            )
        return jnp.stack(received)

    def weight_sum(self, value, received, axis):
        size = value.shape[axis] // self.across
        total = lax.dynamic_slice_in_dim(value, self.here()[2] * size, size, axis)
        total = total.astype(jnp.float32)
        for step in range(self.across - 1):
            total = total + received[step].astype(jnp.float32)
        return total.astype(jnp.bfloat16)

    def weight_send(self, total, axis):
        core = self.here()[3]
        size = total.shape[axis] // 2
        near = lax.dynamic_slice_in_dim(total, core * size, size, axis)
        far = lax.dynamic_slice_in_dim(total, (1 - core) * size, size, axis)
        same = self.same()

        def outward(zhi, rest, xx, core):
            return (zhi, rest, xx, 1 - core) if zhi == core else (1 - zhi, rest, xx, core)

        def over(zhi, rest, xx, core):
            return None if zhi == core else (1 - zhi, rest, xx, 1 - core)

        first = self.send(jnp.where(same, far, near), outward)
        second = self.send(far, over)
        return jnp.where(same, near, second).astype(jnp.float32) + first.astype(jnp.float32)


def join(shape, pieces):
    whole = jnp.zeros(shape, pieces[0][2].dtype)
    for row, col, piece in pieces:
        whole = lax.dynamic_update_slice(whole, piece, (row, col))
    return whole


def after(value, *others):
    return lax.optimization_barrier((value, *others))[0]


def contract_rows(left, right):
    return lax.dot_general(
        left, right, (((0,), (0,)), ((), ())), preferred_element_type=jnp.float32
    )


def contract_cols(left, right):
    return lax.dot_general(
        left, right, (((1,), (1,)), ((), ())), preferred_element_type=jnp.float32
    )


def position(plan):
    row, col = lax.axis_index("row"), lax.axis_index("col")
    zhi, rest, core = row // plan.half, row % plan.half, col % 2
    return zhi, rest, col - core, core


def remote(source, target, send_sem, recv_sem, row, col):
    return pltpu.make_async_remote_copy(
        src_ref=source,
        dst_ref=target,
        send_sem=send_sem,
        recv_sem=recv_sem,
        device_id=(row, col),
        device_id_type=MESH,
    )


def swap_kernel(plan, given, taken, send_sem, recv_sem):
    zhi, rest, base, core = position(plan)
    far_row, near_col = (1 - zhi) * plan.half + rest, base + 1 - core
    barrier = pltpu.get_barrier_semaphore()
    pl.semaphore_signal(barrier, 1, device_id=(far_row, near_col), device_id_type=MESH)
    pl.semaphore_wait(barrier, 1)

    @pl.when(zhi != core)
    def _():
        remote(given, taken, send_sem, recv_sem, far_row, near_col).start()
        remote(given, taken, send_sem, recv_sem, far_row, near_col).wait()

    @pl.when(zhi == core)
    def _():
        pltpu.make_async_copy(given, taken, recv_sem).start()
        pltpu.make_async_copy(given, taken, recv_sem).wait()


def swap_tokens(plan, value, collective_id):
    anywhere = pl.BlockSpec(memory_space=pl.ANY)
    return pl.pallas_call(
        functools.partial(swap_kernel, plan),
        in_specs=[anywhere],
        out_specs=anywhere,
        out_shape=jax.ShapeDtypeStruct(value.shape, value.dtype),
        scratch_shapes=[pltpu.SemaphoreType.DMA, pltpu.SemaphoreType.DMA],
        cost_estimate=pl.CostEstimate(flops=0, bytes_accessed=2**27, transcendentals=0),
        compiler_params=pltpu.CompilerParams(collective_id=collective_id, has_side_effects=True),
    )(value)


def gather_kernel(plan, axes, *refs):
    count = len(axes)
    weights, wholes, sems = refs[:count], refs[count : 2 * count], refs[2 * count :]
    block_sem, block_recv_sem, side_sem, side_recv_sem = sems
    half, across = plan.half, plan.across
    zhi, rest, base, core = position(plan)
    xx = base // 2
    row, col = zhi * half + rest, base + core
    far_row, near_col = (1 - zhi) * half + rest, base + 1 - core
    moved, stays = zhi != core, zhi == core

    barrier = pltpu.get_barrier_semaphore()
    greeted = [(row, near_col), (far_row, col), (far_row, near_col)]
    greeted += [(row, (xx + step) % across * 2 + core) for step in range(1, across)]
    for device in greeted:
        pl.semaphore_signal(barrier, 1, device_id=device, device_id_type=MESH)
    pl.semaphore_wait(barrier, len(greeted))

    def place(index, other, j):
        axis = axes[index]
        size = weights[index].shape[axis]
        at = pl.ds(pl.multiple_of((other * 2 + j) * size, size), size)
        return wholes[index].at[at] if axis == 0 else wholes[index].at[:, at]

    def block_keep(index, j):
        return pltpu.make_async_copy(
            weights[index], place(index, xx, j), block_recv_sem.at[index, j]
        )

    def block_send(index, way, to_row, to_col):
        return remote(
            weights[index],
            place(index, xx, core),
            block_sem.at[index, way],
            block_recv_sem.at[index, core],
            to_row,
            to_col,
        )

    def side(index, step, j):
        at = place(index, xx, j)
        other = (xx + step) % across * 2 + core
        return remote(
            at, at, side_sem.at[index, step - 1, j], side_recv_sem.at[index, step - 1, j], row, other
        )

    for index in range(count):

        @pl.when(moved)
        def _():
            block_send(index, 0, row, near_col).start()
            block_send(index, 1, far_row, near_col).start()

        @pl.when(stays)
        def _():
            block_keep(index, core).start()
            block_send(index, 0, far_row, col).start()

    for index in range(count):
        for j in range(2):
            block_keep(index, j).wait()
            for step in range(1, across):
                side(index, step, j).start()
    for index in range(count):
        for j in range(2):
            for step in range(1, across):
                side(index, step, j).wait()

        @pl.when(moved)
        def _():
            block_send(index, 0, row, near_col).wait_send()
            block_send(index, 1, far_row, near_col).wait_send()

        @pl.when(stays)
        def _():
            block_send(index, 0, far_row, col).wait_send()


def gather_weights(plan, weights, axes, collective_id):
    count = len(weights)
    dma = pltpu.SemaphoreType.DMA
    anywhere = pl.BlockSpec(memory_space=pl.ANY)
    return pl.pallas_call(
        functools.partial(gather_kernel, plan, axes),
        in_specs=[anywhere] * count,
        out_specs=[anywhere] * count,
        out_shape=[
            jax.ShapeDtypeStruct(grow(weight.shape, axis, plan.cols), weight.dtype)
            for weight, axis in zip(weights, axes, strict=True)
        ],
        scratch_shapes=[
            dma((count, 2)),
            dma((count, 2)),
            dma((count, plan.across - 1, 2)),
            dma((count, plan.across - 1, 2)),
        ],
        cost_estimate=pl.CostEstimate(flops=0, bytes_accessed=2**28, transcendentals=0),
        compiler_params=pltpu.CompilerParams(collective_id=collective_id, has_side_effects=True),
    )(*weights)


def sum_kernel(plan, own, out, landed, send_sem, recv_sem):
    half, rows = plan.half, plan.rows
    zhi, rest, base, core = position(plan)

    def device(step):
        block = (core * half + rest + step) % rows
        return zhi * half + block % half, base + block // half

    barrier = pltpu.get_barrier_semaphore()
    for step in range(1, rows):
        pl.semaphore_signal(barrier, 1, device_id=device(step), device_id_type=MESH)
    pl.semaphore_wait(barrier, rows - 1)
    copies = [
        remote(
            own, landed.at[step - 1], send_sem.at[step - 1], recv_sem.at[step - 1], *device(step)
        )
        for step in range(1, rows)
    ]
    for copy in copies:
        copy.start()
    total = own[...]
    for step, copy in enumerate(copies):
        copy.wait_recv()
        total = total + landed[step]
    out[...] = total
    for copy in copies:
        copy.wait_send()


def group_sum(plan, value, collective_id):
    others = plan.rows - 1
    inside = pl.BlockSpec(memory_space=pltpu.VMEM)
    dma = pltpu.SemaphoreType.DMA
    return pl.pallas_call(
        functools.partial(sum_kernel, plan),
        in_specs=[inside],
        out_specs=inside,
        out_shape=jax.ShapeDtypeStruct(value.shape, value.dtype),
        scratch_shapes=[
            pltpu.VMEM((others, *value.shape), value.dtype),
            dma((others,)),
            dma((others,)),
        ],
        cost_estimate=pl.CostEstimate(
            flops=value.size * others, bytes_accessed=2**24, transcendentals=0
        ),
        compiler_params=pltpu.CompilerParams(collective_id=collective_id, has_side_effects=True),
    )(value)


def scatter_kernel(plan, parts, axes, turned, last, swaps, *refs):
    half, across, count = plan.half, plan.across, len(axes)
    lefts, weight, refs = refs[:parts], refs[parts], refs[parts + 1 :]
    grads, refs = refs[:count], refs[count:]
    if last:
        residual, refs = refs[0], refs[1:]
    if swaps:
        given, refs = refs[0], refs[1:]
    out, blocks, refs = refs[0], refs[1 : count + 1], refs[count + 1 :]
    if last:
        sums, refs = refs[0], refs[1:]
    if swaps:
        taken, refs = refs[0], refs[1:]
    loaded, near_out, near_in, far_out, far_in = refs[:5]
    load_sem, near_sem, near_recv_sem, far_sem, far_recv_sem, block_sem, block_recv_sem = refs[5:12]
    refs = refs[12:]
    zhi, rest, base, core = position(plan)
    xx = base // 2
    row, col = zhi * half + rest, base + core
    far_row, near_col = (1 - zhi) * half + rest, base + 1 - core
    moved, stays = zhi != core, zhi == core
    part, width = near_out.shape[1:]
    rows = 2 * part
    tile = min(512, width)

    barrier = pltpu.get_barrier_semaphore()
    side_y = half // 2
    zlo, y = rest // side_y, rest % side_y
    base_row = zhi * half

    def split(unit):
        h, index = unit // half, unit % half
        first = side_y + h * (2 - side_y)
        second = half // first
        ahead = first - 1 - index // second
        aside = second - 1 - index % second
        place = y + h * (zlo - y)
        other = zlo + h * (y - zlo)
        return h, (place + ahead) % first, (other + aside) % second, place, other, ahead

    def chip_of(h, along, beside):
        return (beside + h * (along - beside)) * side_y + along + h * (beside - along)

    greeted = [(row, near_col), (base_row + (1 - zlo) * side_y + y, col)]
    greeted += [(base_row + zlo * side_y + (y + step) % side_y, col) for step in range(1, side_y)]
    if count:
        greeted += [(row, (xx + step) % across * 2 + core) for step in range(1, across)]
    if last:
        greeted += [(far_row, col)]
    if last or swaps:
        greeted += [(far_row, near_col)]
    for device in greeted:
        pl.semaphore_signal(barrier, 1, device_id=device, device_id_type=MESH)

    def block(index, step):
        grad, axis = grads[index], axes[index]
        other = (xx + step) % across
        size = grad.shape[axis] // across
        at = pl.ds(pl.multiple_of(other * size, size), size)
        return remote(
            grad.at[at] if axis == 0 else grad.at[:, at],
            blocks[index].at[step - 1],
            block_sem.at[index, step - 1],
            block_recv_sem.at[index, step - 1],
            row,
            other * 2 + core,
        )

    def load(unit, whose, slot):
        h, along, beside = split(unit)[:3]
        side = (1 - core) if whose == 0 else core
        index = side * half + chip_of(h, along, beside)
        target, sem = loaded.at[slot, whose], load_sem.at[slot, whose]
        if parts == 1:
            at = pl.ds(pl.multiple_of(index * rows + h * part, part), part)
            return [(None, pltpu.make_async_copy(lefts[0].at[at], target, sem))]
        at = pl.ds(pl.multiple_of(index * part, part), part)
        return [
            (h == k, pltpu.make_async_copy(lefts[k].at[at], target, sem)) for k in range(2)
        ]

    def start(copies):
        for when, copy in copies:
            if when is None:
                copy.start()
            else:
                pl.when(when)(copy.start)

    def near(unit, slot):
        return remote(
            near_out.at[slot],
            near_in.at[unit],
            near_sem.at[unit],
            near_recv_sem.at[unit],
            row,
            near_col,
        )

    def far(unit):
        h, along, beside, place, other, ahead = split(unit)
        straight = (ahead + half - 1) // half
        chip = chip_of(h, along, beside + straight * (other - beside))
        return remote(
            far_out.at[unit],
            far_in.at[unit],
            far_sem.at[unit],
            far_recv_sem.at[unit],
            base_row + chip,
            col,
        )

    def product(left, cols):
        if turned:
            return contract_cols(left, weight[cols, :])
        return jnp.dot(left, weight[:, cols], preferred_element_type=jnp.float32)

    def columns(n):
        return pl.ds(pl.multiple_of(n * tile, tile), tile)

    def exchange():
        return remote(given, taken, refs[0], refs[1], far_row, near_col)

    def keep():
        return pltpu.make_async_copy(given, taken, refs[1])

    start(load(0, 0, 0))
    pl.semaphore_wait(barrier, len(greeted))
    if swaps:
        pl.when(moved)(lambda: exchange().start())
        pl.when(stays)(lambda: keep().start())
    for index in range(count):
        for step in range(1, across):
            block(index, step).start()

    def line_sum(h, aside):
        first = side_y if h == 0 else 2
        second = half // first
        at = h * half + second - 1 - aside
        value = far_out[at + (first - 1) * second].astype(jnp.float32)
        for ahead in range(first - 1):
            unit = at + ahead * second
            far(unit).wait_recv()
            value = value + far_in[unit].astype(jnp.float32)
        return value

    def second_stage(h):
        second = 2 if h == 0 else side_y
        for aside in range(second - 1, 0, -1):
            unit = (h + 1) * half - 1 - aside
            far_out[unit] = line_sum(h, aside).astype(far_out.dtype)
            far(unit).start()

    def body(unit, carry):
        slot = unit % 2
        before = unit - 1

        @pl.when(unit + 1 < 2 * half)
        def _():
            start(load(unit + 1, 0, 1 - slot))

        @pl.when(unit < 2 * half)
        def _():
            start(load(unit, 1, 1 - slot))
            load(unit, 0, slot)[0][1].wait()

            @pl.when(unit >= 2)
            def _():
                near(unit - 2, slot).wait_send()

            @pl.loop(0, width // tile)
            def _(n):
                value = product(loaded[slot, 0], columns(n))
                near_out[slot, :, columns(n)] = value.astype(near_out.dtype)

            near(unit, slot).start()

        @pl.when(unit >= 1)
        def _():
            load(before, 1, slot)[0][1].wait()
            near(before, 1 - slot).wait_recv()

            @pl.loop(0, width // tile)
            def _(n):
                value = product(loaded[slot, 1], columns(n))
                value = value + near_in[before, :, columns(n)].astype(jnp.float32)
                far_out[before, :, columns(n)] = value.astype(far_out.dtype)

            @pl.when(split(before)[5] > 0)
            def _():
                far(before).start()

            @pl.when(unit == half + half // 2)
            def _():
                second_stage(0)

        return carry

    lax.fori_loop(0, 2 * half + 1, body, 0)

    def total(h):
        value = line_sum(h, 0)
        second = 2 if h == 0 else side_y
        for aside in range(second - 1, 0, -1):
            unit = (h + 1) * half - 1 - aside
            far(unit).wait_recv()
            value = value + far_in[unit].astype(jnp.float32)
        return value

    if last:
        send_sum, take_sum = finish(
            (zhi, rest, xx, core), (row, col, far_row, near_col), grads, blocks, block, sums, refs
        )
        final, final_sem, final_recv_sem = refs[:3]

        def swap_far(h):
            return remote(
                final.at[h],
                out.at[pl.ds(h * part, part)],
                final_sem.at[h],
                final_recv_sem.at[h],
                far_row,
                near_col,
            )

        def swap_near(h):
            return pltpu.make_async_copy(
                final.at[h], out.at[pl.ds(h * part, part)], final_recv_sem.at[h]
            )

        for h in range(2):
            value = total(h) + residual[h * part : (h + 1) * part, :]
            final[h] = value.astype(final.dtype)

            @pl.when(moved)
            def _():
                swap_far(h).start()

            @pl.when(stays)
            def _():
                swap_near(h).start()

            if h == 0:
                second_stage(1)
                send_sum()

        take_sum()

        for h in range(2):

            @pl.when(moved)
            def _():
                swap_far(h).wait()

            @pl.when(stays)
            def _():
                swap_near(h).wait()

    else:
        second_stage(1)
        for h in range(2):
            out[h * part : (h + 1) * part, :] = total(h)
        for index in range(count):
            for step in range(1, across):
                block(index, step).wait_recv()
    if swaps:
        pl.when(moved)(lambda: exchange().wait())
        pl.when(stays)(lambda: keep().wait())
    for h in range(2):
        for unit in range(h * half, h * half + half - 1):
            far(unit).wait_send()
    for unit in range(2 * half - 2, 2 * half):
        near(unit, unit % 2).wait_send()
    for index in range(count):
        for step in range(1, across):
            block(index, step).wait_send()


def finish(place, devices, grads, blocks, block, sums, refs):
    zhi, _, xx, core = place
    row, col, far_row, near_col = devices
    grad, blocks = grads[0], blocks[0]
    mine, others, pair, landed, mine_sem, pair_sem, landed_sem = refs[3:]
    size = pair.shape[1]
    across = blocks.shape[0] + 1
    own = pltpu.make_async_copy(
        grad.at[pl.ds(pl.multiple_of(xx * 2 * size, size), 2 * size)], mine, mine_sem.at[0]
    )
    rest = [
        pltpu.make_async_copy(blocks.at[step], others.at[step], mine_sem.at[step + 1])
        for step in range(across - 1)
    ]

    def give(index, slot, to_row, to_col, to_slot):
        return remote(
            pair.at[slot],
            landed.at[to_slot],
            pair_sem.at[index],
            landed_sem.at[to_slot],
            to_row,
            to_col,
        )

    to_sibling = give(0, 1 - core, row, near_col, 0)
    to_same = give(0, core, far_row, col, 0)
    to_cross = give(1, 1 - core, far_row, near_col, 1)
    own.start()

    def send_sum():
        for step in range(1, across):
            block(0, step).wait_recv()
            rest[step - 1].start()
        own.wait()
        for copy in rest:
            copy.wait()
        value = mine[...].astype(jnp.float32)
        for step in range(across - 1):
            value = value + others[step].astype(jnp.float32)
        pair[0] = value[:size].astype(pair.dtype)
        pair[1] = value[size:].astype(pair.dtype)

        @pl.when(zhi == core)
        def _():
            to_sibling.start()

        @pl.when(zhi != core)
        def _():
            to_same.start()
            to_cross.start()

    def take_sum():
        @pl.when(zhi == core)
        def _():
            to_sibling.wait_send()
            give(0, core, far_row, col, 0).wait_recv()
            sums[...] = pair[core].astype(jnp.float32) + landed[0].astype(jnp.float32)

        @pl.when(zhi != core)
        def _():
            to_same.wait_send()
            to_cross.wait_send()
            to_same.wait_recv()
            to_cross.wait_recv()
            sums[...] = landed[1].astype(jnp.float32) + landed[0].astype(jnp.float32)

    return send_sum, take_sum


def grow(shape, axis, pieces):
    return tuple(size * pieces if dim == axis else size for dim, size in enumerate(shape))


def cut(shape, axis, pieces):
    return tuple(size // pieces if dim == axis else size for dim, size in enumerate(shape))


def multiply_scatter(
    plan, lefts, weight, turned, collective_id, grads=(), axes=(), residual=None, swapped=None
):
    half, across, count = plan.half, plan.across, len(grads)
    depth = lefts[0].shape[1]
    width = weight.shape[0 if turned else 1]
    rows = sum(left.shape[0] for left in lefts) // plan.rows
    part = rows // 2
    low = jnp.bfloat16
    dma = pltpu.SemaphoreType.DMA
    anywhere = pl.BlockSpec(memory_space=pl.ANY)
    inside = pl.BlockSpec(memory_space=pltpu.VMEM)
    last = residual is not None
    swaps = swapped is not None
    in_specs = [anywhere] * len(lefts) + [inside] + [anywhere] * count + [inside] * last
    in_specs += [anywhere] * swaps
    out_specs = [anywhere if last else inside] + [anywhere] * count + [inside] * last
    out_shape = [jax.ShapeDtypeStruct((rows, width), low if last else jnp.float32)]
    out_shape += [
        jax.ShapeDtypeStruct((across - 1, *cut(grad.shape, axis, across)), low)
        for grad, axis in zip(grads, axes, strict=True)
    ]
    scratch = [
        pltpu.VMEM((2, 2, part, depth), low),
        pltpu.VMEM((2, part, width), low),
        pltpu.VMEM((2 * half, part, width), low),
        pltpu.VMEM((2 * half, part, width), low),
        pltpu.VMEM((2 * half, part, width), low),
        dma((2, 2)),
        dma((2 * half,)),
        dma((2 * half,)),
        dma((2 * half,)),
        dma((2 * half,)),
        dma((max(count, 1), across - 1)),
        dma((max(count, 1), across - 1)),
    ]
    if last:
        size, wide = grads[0].shape[0] // plan.cols, grads[0].shape[1]
        out_shape.append(jax.ShapeDtypeStruct((size, wide), jnp.float32))
        scratch += [
            pltpu.VMEM((2, part, width), low),
            dma((2,)),
            dma((2,)),
            pltpu.VMEM((2 * size, wide), low),
            pltpu.VMEM((across - 1, 2 * size, wide), low),
            pltpu.VMEM((2, size, wide), low),
            pltpu.VMEM((2, size, wide), low),
            dma((across,)),
            dma((2,)),
            dma((2,)),
        ]
    if swaps:
        out_shape.append(jax.ShapeDtypeStruct(swapped.shape, swapped.dtype))
        scratch += [dma, dma]
    return pl.pallas_call(
        functools.partial(scatter_kernel, plan, len(lefts), axes, turned, last, swaps),
        in_specs=in_specs,
        out_specs=out_specs + [anywhere] * swaps,
        out_shape=out_shape,
        scratch_shapes=scratch,
        cost_estimate=pl.CostEstimate(
            flops=2 * rows * plan.rows * depth * width,
            bytes_accessed=20 * rows * plan.rows * width,
            transcendentals=0,
        ),
        compiler_params=pltpu.CompilerParams(
            collective_id=collective_id, has_side_effects=True, vmem_limit_bytes=58 * 2**20
        ),
    )(*lefts, weight, *grads, *([residual] if last else []), *([swapped] if swaps else []))


def unit_grad_kernel(left, weight, both, out):
    width = weight.shape[0]
    grad = contract_cols(left[...], weight[...])
    gate = both[:, :width].astype(jnp.float32)
    up = both[:, width:].astype(jnp.float32)
    sigmoid = jax.nn.sigmoid(gate)
    scaled = grad * sigmoid
    out[:, :width] = (scaled * up * (1.0 + gate * (1.0 - sigmoid))).astype(out.dtype)
    out[:, width:] = (scaled * gate).astype(out.dtype)


def unit_grad(left, weight, both):
    seq_len, depth = left.shape
    rows = min(256, seq_len)
    width = weight.shape[0]
    wide = pl.BlockSpec((rows, 2 * width), lambda i: (i, 0))
    return pl.pallas_call(
        unit_grad_kernel,
        grid=(seq_len // rows,),
        in_specs=[pl.BlockSpec((rows, depth), lambda i: (i, 0)), full(width, depth), wide],
        out_specs=wide,
        out_shape=jax.ShapeDtypeStruct((seq_len, 2 * width), jnp.bfloat16),
        cost_estimate=pl.CostEstimate(
            flops=2 * seq_len * depth * width,
            bytes_accessed=2 * seq_len * (depth + 4 * width),
            transcendentals=seq_len * width,
        ),
        compiler_params=pltpu.CompilerParams(vmem_limit_bytes=40 * 2**20),
    )(left, weight, both)


def full(rows, width):
    return pl.BlockSpec((rows, width), lambda *_: (0, 0))


def turn(values, cosine, sine):
    return values * cosine + pltpu.roll(values, values.shape[-1] // 2, 1) * sine


def column(row_vector, width):
    return jnp.transpose(jnp.broadcast_to(row_vector, (width, row_vector.shape[1])))


def project_kernel(head_size, first, second, weight, proj, squares):
    width = proj.shape[1] // 3
    rows = first.shape[0]
    for chunk, left in enumerate((first, second)):
        at = slice(chunk * rows, (chunk + 1) * rows)
        value = jnp.dot(left[...], weight[...], preferred_element_type=jnp.float32)
        proj[at, :] = value
        for place in range(2):
            total = None
            for start in range(place * width, (place + 1) * width, head_size):
                part = value[:, start : start + head_size] ** 2
                total = part if total is None else total + part
            squares[place : place + 1, at] = jnp.sum(jnp.transpose(total), axis=0, keepdims=True)


def project(lefts, weight, head_size, own_tokens):
    rows, depth = lefts[0].shape
    wide = weight.shape[1]
    part = pl.BlockSpec((own_tokens // 2, depth), lambda i: (i, 0))
    return pl.pallas_call(
        functools.partial(project_kernel, head_size),
        grid=(2 * rows // own_tokens,),
        in_specs=[part, part, full(depth, wide)],
        out_specs=[
            pl.BlockSpec((own_tokens, wide), lambda i: (i, 0)),
            pl.BlockSpec((2, own_tokens), lambda i: (0, i)),
        ],
        out_shape=[
            jax.ShapeDtypeStruct((2 * rows, wide), jnp.float32),
            jax.ShapeDtypeStruct((2, 2 * rows), jnp.float32),
        ],
        cost_estimate=pl.CostEstimate(
            flops=4 * rows * depth * wide,
            bytes_accessed=4 * rows * depth + 8 * rows * wide,
            transcendentals=0,
        ),
        compiler_params=pltpu.CompilerParams(vmem_limit_bytes=40 * 2**20),
    )(*lefts, weight)


def prepare_kernel(
    head_size, proj, query_inv, key_inv, cosine, sine, query_gain, key_gain, query, key, value
):
    width = query.shape[1]
    turns = (cosine[...], sine[...])
    for source, inv, gain, target in (
        (0, query_inv, query_gain, query),
        (width, key_inv, key_gain, key),
    ):
        factor = column(inv[...], head_size)
        for start in range(0, width, head_size):
            part = proj[:, source + start : source + start + head_size]
            scaled = part * factor * gain[:, start : start + head_size]
            target[:, start : start + head_size] = turn(scaled, *turns).astype(target.dtype)
    value[...] = proj[:, 2 * width :].astype(value.dtype)


def prepare(proj, query_inv, key_inv, cosine, sine, query_gain, key_gain, head_size):
    seq_len, width = proj.shape[0], proj.shape[1] // 3
    rows = min(512, seq_len)
    return pl.pallas_call(
        functools.partial(prepare_kernel, head_size),
        grid=(seq_len // rows,),
        in_specs=[
            pl.BlockSpec((rows, 3 * width), lambda i: (i, 0)),
            pl.BlockSpec((1, rows), lambda i: (0, i)),
            pl.BlockSpec((1, rows), lambda i: (0, i)),
            pl.BlockSpec((rows, head_size), lambda i: (i, 0)),
            pl.BlockSpec((rows, head_size), lambda i: (i, 0)),
            full(1, width),
            full(1, width),
        ],
        out_specs=[pl.BlockSpec((rows, width), lambda i: (i, 0))] * 3,
        out_shape=[jax.ShapeDtypeStruct((seq_len, width), jnp.bfloat16)] * 3,
        cost_estimate=pl.CostEstimate(
            flops=10 * seq_len * width, bytes_accessed=seq_len * width * 20, transcendentals=0
        ),
        compiler_params=pltpu.CompilerParams(vmem_limit_bytes=40 * 2**20),
    )(proj, query_inv, key_inv, cosine, sine, query_gain, key_gain)


def allowed(first, key_block, query_block, key_rows, query_rows):
    key_index = key_block * key_rows + lax.broadcasted_iota(
        jnp.int32, (key_rows, query_rows), 0
    )
    query_index = query_block * query_rows + lax.broadcasted_iota(
        jnp.int32, (key_rows, query_rows), 1
    )
    return (key_index <= query_index) & (key_index >= first)


def attend_kernel(rows, low, first, query, key, value, *refs):
    out, log_sum = refs[-2:]
    step = pl.program_id(1)
    head_size = query.shape[1]
    factor = LOG2E * head_size**-0.5
    queries = query[...]
    starts = first[...]

    def one(index, carry):
        top, total, acc = carry
        at = pl.ds(pl.multiple_of(index * rows, rows), rows)
        scores = contract_cols(key[at, :], queries) * factor
        scores = jnp.where(allowed(starts, index, step, rows, rows), scores, MASKED)
        new_top = jnp.maximum(top, jnp.max(scores, axis=0, keepdims=True))
        probs = jnp.exp2(scores - new_top)
        fade = jnp.exp2(top - new_top)
        total = total * fade + jnp.sum(probs, axis=0, keepdims=True)
        acc = acc * fade + contract_rows(value[at, :], probs.astype(jnp.bfloat16))
        return new_top, total, acc

    top, total, acc = lax.fori_loop(
        low[step],
        step + 1,
        one,
        (
            jnp.full((1, rows), MASKED, jnp.float32),
            jnp.zeros((1, rows), jnp.float32),
            jnp.zeros((head_size, rows), jnp.float32),
        ),
    )
    out[...] = jnp.transpose(acc / total).astype(out.dtype)
    log_sum[0] = top + jnp.log2(total)


def attend(low, first, query, key, value, head_size, rows, more):
    seq_len, width = query.shape
    heads = width // head_size
    whole = pl.BlockSpec((seq_len, head_size), lambda h, i, *_: (0, h))
    block = pl.BlockSpec((rows, head_size), lambda h, i, *_: (i, h))
    return pl.pallas_call(
        functools.partial(attend_kernel, rows),
        grid_spec=pltpu.PrefetchScalarGridSpec(
            num_scalar_prefetch=1,
            grid=(heads, seq_len // rows),
            in_specs=[
                pl.BlockSpec((1, rows), lambda h, i, *_: (0, i)),
                block,
                whole,
                whole,
            ]
            + [pl.BlockSpec(memory_space=pl.ANY)] * len(more),
            out_specs=[block, pl.BlockSpec((1, 1, rows), lambda h, i, *_: (h, 0, i))],
        ),
        out_shape=[
            jax.ShapeDtypeStruct((seq_len, width), jnp.bfloat16),
            jax.ShapeDtypeStruct((heads, 1, seq_len), jnp.float32),
        ],
        cost_estimate=pl.CostEstimate(
            flops=seq_len * seq_len * width, bytes_accessed=seq_len * width * 8, transcendentals=0
        ),
        compiler_params=pltpu.CompilerParams(vmem_limit_bytes=40 * 2**20),
    )(low, first, query, key, value, *more)


def attend_back_kernel(
    rows,
    high,
    first,
    query,
    key,
    value,
    out,
    out_grad,
    log_sum,
    *refs,
):
    query_grad, key_grad, value_grad, delta = refs[-4:]
    step = pl.program_id(1)
    seq_len, head_size = query.shape
    factor = LOG2E * head_size**-0.5

    @pl.when(step == 0)
    def _():
        query_grad[...] = jnp.zeros_like(query_grad)

        @pl.loop(0, seq_len // rows)
        def _(index):
            at = pl.ds(pl.multiple_of(index * rows, rows), rows)
            product = out_grad[at, :].astype(jnp.float32) * out[at, :].astype(jnp.float32)
            delta[:, at] = jnp.sum(jnp.transpose(product), axis=0, keepdims=True)

    keys = key[...]
    values = value[...]

    def one(index, carry):
        key_acc, value_acc = carry
        at = pl.ds(pl.multiple_of(index * rows, rows), rows)
        queries = query[at, :]
        grads = out_grad[at, :]
        scores = contract_cols(keys, queries) * factor
        mask = allowed(first[:, at], step, index, rows, rows)
        probs = jnp.exp2(jnp.where(mask, scores - log_sum[0, :, at], MASKED))
        value_acc = value_acc + jnp.dot(
            probs.astype(jnp.bfloat16), grads, preferred_element_type=jnp.float32
        )
        prob_grad = contract_cols(values, grads)
        score_grad = (probs * (prob_grad - delta[:, at])).astype(jnp.bfloat16)
        key_acc = key_acc + jnp.dot(score_grad, queries, preferred_element_type=jnp.float32)
        query_grad[at, :] += contract_rows(score_grad, keys)
        return key_acc, value_acc

    zeros = jnp.zeros((rows, head_size), jnp.float32)
    key_acc, value_acc = lax.fori_loop(step, high[step] + 1, one, (zeros, zeros))
    key_grad[...] = key_acc
    value_grad[...] = value_acc.astype(value_grad.dtype)


def attend_back(high, first, query, key, value, out, out_grad, log_sum, head_size, rows, more):
    seq_len, width = query.shape
    heads = width // head_size
    whole = pl.BlockSpec((seq_len, head_size), lambda h, j, *_: (0, h))
    block = pl.BlockSpec((rows, head_size), lambda h, j, *_: (j, h))
    return pl.pallas_call(
        functools.partial(attend_back_kernel, rows),
        grid_spec=pltpu.PrefetchScalarGridSpec(
            num_scalar_prefetch=1,
            grid=(heads, seq_len // rows),
            in_specs=[
                full(1, seq_len),
                whole,
                block,
                block,
                whole,
                whole,
                pl.BlockSpec((1, 1, seq_len), lambda h, j, *_: (h, 0, 0)),
            ]
            + [pl.BlockSpec(memory_space=pl.ANY)] * len(more),
            out_specs=[whole, block, block],
            scratch_shapes=[pltpu.VMEM((1, seq_len), jnp.float32)],
        ),
        out_shape=[
            jax.ShapeDtypeStruct((seq_len, width), jnp.float32),
            jax.ShapeDtypeStruct((seq_len, width), jnp.float32),
            jax.ShapeDtypeStruct((seq_len, width), jnp.bfloat16),
        ],
        cost_estimate=pl.CostEstimate(
            flops=3 * seq_len * seq_len * width,
            bytes_accessed=seq_len * width * 20,
            transcendentals=0,
        ),
        compiler_params=pltpu.CompilerParams(vmem_limit_bytes=48 * 2**20),
    )(high, first, query, key, value, out, out_grad, log_sum, *more)


def norm_back_kernel(
    head_size,
    proj,
    query_inv,
    key_inv,
    cosine,
    sine,
    query_gain,
    key_gain,
    query_grad,
    key_grad,
    dots,
    gain_sums,
):
    width = query_grad.shape[1]
    turns = (cosine[...], -sine[...])
    scale = head_size**-0.5

    @pl.when(pl.program_id(0) == 0)
    def _():
        gain_sums[...] = jnp.zeros_like(gain_sums)

    for place, (source, inv, gain, grad) in enumerate(
        ((0, query_inv, query_gain, query_grad), (width, key_inv, key_gain, key_grad))
    ):
        factor = column(inv[...], head_size)
        row_part = None
        for start in range(0, width, head_size):
            cols = slice(start, start + head_size)
            hat = proj[:, source + start : source + start + head_size] * factor
            product = turn(grad[:, cols] * scale, *turns) * hat
            gain_sums[place : place + 1, cols] += jnp.sum(product, axis=0, keepdims=True)
            product = product * gain[:, cols]
            row_part = product if row_part is None else row_part + product
        dots[place : place + 1, :] = jnp.sum(jnp.transpose(row_part), axis=0, keepdims=True)


def norm_back(
    proj, query_inv, key_inv, cosine, sine, query_gain, key_gain, query_grad, key_grad, head_size
):
    seq_len, width = query_grad.shape
    rows = min(512, seq_len)
    wide = pl.BlockSpec((rows, width), lambda i: (i, 0))
    return pl.pallas_call(
        functools.partial(norm_back_kernel, head_size),
        grid=(seq_len // rows,),
        in_specs=[
            pl.BlockSpec((rows, 2 * width), lambda i: (i, 0)),
            pl.BlockSpec((1, rows), lambda i: (0, i)),
            pl.BlockSpec((1, rows), lambda i: (0, i)),
            pl.BlockSpec((rows, head_size), lambda i: (i, 0)),
            pl.BlockSpec((rows, head_size), lambda i: (i, 0)),
            full(1, width),
            full(1, width),
            wide,
            wide,
        ],
        out_specs=[pl.BlockSpec((2, rows), lambda i: (0, i)), full(2, width)],
        out_shape=[
            jax.ShapeDtypeStruct((2, seq_len), jnp.float32),
            jax.ShapeDtypeStruct((2, width), jnp.float32),
        ],
        cost_estimate=pl.CostEstimate(
            flops=20 * seq_len * width, bytes_accessed=seq_len * width * 20, transcendentals=0
        ),
        compiler_params=pltpu.CompilerParams(vmem_limit_bytes=40 * 2**20),
    )(proj, query_inv, key_inv, cosine, sine, query_gain, key_gain, query_grad, key_grad)


def proj_back_kernel(
    head_size,
    features,
    proj,
    query_inv,
    key_inv,
    cosine,
    sine,
    query_gain,
    key_gain,
    query_grad,
    key_grad,
    value_grad,
    dots,
    *rest,
):
    out = rest[-1]
    width = query_grad.shape[1]
    turns = (cosine[...], -sine[...])
    scale = head_size**-0.5
    for place, (source, inv, gain, grad) in enumerate(
        ((0, query_inv, query_gain, query_grad), (width, key_inv, key_gain, key_grad))
    ):
        factor = column(inv[...], head_size)
        mean = column(dots[place : place + 1, :] * (1.0 / features), head_size)
        for start in range(0, width, head_size):
            cols = slice(start, start + head_size)
            at = slice(source + start, source + start + head_size)
            hat = proj[:, at] * factor
            scaled = turn(grad[:, cols] * scale, *turns) * gain[:, cols]
            out[:, at] = (factor * (scaled - hat * mean)).astype(out.dtype)
    out[:, 2 * width :] = value_grad[...]


def proj_back(
    proj,
    query_inv,
    key_inv,
    cosine,
    sine,
    query_gain,
    key_gain,
    query_grad,
    key_grad,
    value_grad,
    dots,
    head_size,
    features,
    more,
):
    seq_len, width = query_grad.shape
    rows = min(512, seq_len)
    wide = pl.BlockSpec((rows, width), lambda i: (i, 0))
    return pl.pallas_call(
        functools.partial(proj_back_kernel, head_size, features),
        grid=(seq_len // rows,),
        in_specs=[
            pl.BlockSpec((rows, 2 * width), lambda i: (i, 0)),
            pl.BlockSpec((1, rows), lambda i: (0, i)),
            pl.BlockSpec((1, rows), lambda i: (0, i)),
            pl.BlockSpec((rows, head_size), lambda i: (i, 0)),
            pl.BlockSpec((rows, head_size), lambda i: (i, 0)),
            full(1, width),
            full(1, width),
            wide,
            wide,
            wide,
            pl.BlockSpec((2, rows), lambda i: (0, i)),
        ]
        + [pl.BlockSpec(memory_space=pl.ANY)] * len(more),
        out_specs=pl.BlockSpec((rows, 3 * width), lambda i: (i, 0)),
        out_shape=jax.ShapeDtypeStruct((seq_len, 3 * width), jnp.bfloat16),
        cost_estimate=pl.CostEstimate(
            flops=20 * seq_len * width, bytes_accessed=seq_len * width * 24, transcendentals=0
        ),
        compiler_params=pltpu.CompilerParams(vmem_limit_bytes=40 * 2**20),
    )(
        proj,
        query_inv,
        key_inv,
        cosine,
        sine,
        query_gain,
        key_gain,
        query_grad,
        key_grad,
        value_grad,
        dots,
        *more,
    )


def body(
    plan,
    layer_input,
    segments,
    w_query,
    w_key,
    w_value,
    w_out,
    query_gain,
    key_gain,
    attn_gain,
    w_gate,
    w_up,
    w_down,
    mlp_gain,
    cotangent,
):
    rows = plan.rows
    mine = plan.block()
    model_width = layer_input.shape[1]
    head_size = model_width // HEADS
    seq_len = segments.shape[0]
    own_tokens = seq_len // rows
    part = own_tokens // 2
    f32 = jnp.float32
    bf16 = jnp.bfloat16
    chunks = range(2)

    def chunk_of(value, k):
        return value[k * part : (k + 1) * part]

    qkv_own = jnp.concatenate([w_query, w_key, w_value], axis=1)
    own_depth, wide = qkv_own.shape
    small_own = jnp.concatenate([query_gain, key_gain, attn_gain, mlp_gain])
    gain_size, post_size = query_gain.shape[0], attn_gain.shape[0]
    cuts = (gain_size, 2 * gain_size, 2 * gain_size + post_size)
    small_size = small_own.shape[0]
    extra = 16

    def lines(vector):
        return jnp.pad(vector, (0, extra * wide - small_size)).reshape(extra, wide)

    own_weight = jnp.concatenate([qkv_own, lines(small_own)], axis=0)
    nearby = plan.send(
        segments, lambda z, r, x, c: (z, r, x, 1 - c) if z == c else None
    )
    segments = jnp.where(plan.same(), segments, nearby)
    own_x = swap_tokens(plan, after(layer_input, segments), 1)
    gathered_x = [plan.token_gather(chunk_of(own_x, k)) for k in chunks]
    both, out_rows, down_rows = gather_weights(
        plan, (after(own_weight, own_x), w_out, w_down), (0, 1, 1), 7
    )
    both = both.reshape(plan.cols, own_depth + extra, wide)
    proj_weight = both[:, :own_depth].reshape(-1, wide)
    small = both[:, own_depth:].reshape(plan.cols, extra * wide)[:, :small_size].astype(f32)
    query_scale, key_scale, attn_scale, mlp_scale = (
        value.reshape(1, -1) for value in jnp.split(small, cuts, axis=1)
    )

    out_full = plan.token_gather(out_rows)
    ff_width = w_gate.shape[1]

    local_width = wide // 3
    token_index = jnp.arange(seq_len, dtype=jnp.int32)
    change = jnp.concatenate([jnp.ones((1,), dtype=bool), segments[1:] != segments[:-1]])
    first = lax.cummax(jnp.where(change, token_index, 0), axis=0)
    places = (token_index - first).astype(f32)
    lane = jnp.arange(head_size, dtype=jnp.int32)
    half = head_size // 2
    freqs = THETA ** (-((lane % half).astype(f32) * 2.0) / head_size)
    angle = places[:, None] * freqs[None, :]
    cosine = jnp.cos(angle)
    sine = jnp.sin(angle) * jnp.where(lane < half, -1.0, 1.0)[None, :]
    tile = min(512, seq_len)
    low = first[::tile] // tile
    last = token_index[tile - 1 :: tile]
    ends = jnp.min(
        jnp.where(change[None, :] & (token_index[None, :] > last[:, None]), token_index, seq_len),
        axis=1,
    )
    high = (ends - 1) // tile
    first_row = first[None, :]

    proj, squares = project(gathered_x, proj_weight, head_size, own_tokens)
    invs = lax.rsqrt(group_sum(plan, squares, 5) / model_width + EPS)
    query_inv, key_inv = invs[:1], invs[1:]
    query, key, value = prepare(
        proj, query_inv, key_inv, cosine, sine, query_scale, key_scale, head_size
    )
    gate_pair = plan.weight_pair(after(w_gate, out_rows))
    up_pair = plan.weight_pair(after(w_up, query))
    attn_out, log_sum = attend(
        low, first_row, query, key, value, head_size, tile, gate_pair
    )

    attn_tokens = jnp.zeros((own_tokens, model_width), bf16)
    for flip in range(rows):
        other = mine ^ flip
        piece = lax.dynamic_slice(attn_out, (other * own_tokens, 0), (own_tokens, local_width))
        if flip:
            piece = plan.partner(piece, flip)
        attn_tokens = lax.dynamic_update_slice(attn_tokens, piece, (0, other * local_width))

    places, gate_pieces = zip(*plan.weight_pieces(gate_pair), strict=True)
    attn_tokens, *others = lax.optimization_barrier((attn_tokens, *gate_pieces, *up_pair))
    gate_pieces, up_pair = zip(places, others[:-2], strict=True), others[-2:]
    up_pieces = plan.weight_pieces(up_pair)
    ff_weight = join(
        (model_width, 2 * ff_width),
        [
            (c * own_depth, start, piece)
            for start, pieces in ((0, gate_pieces), (ff_width, up_pieces))
            for c, piece in pieces
        ],
    )
    def normed(value):
        inv = lax.rsqrt(jnp.mean(value * value, axis=-1, keepdims=True) + EPS)
        return inv, value * inv

    def norm_grad(inv, hat, scaled):
        mean = jnp.mean(scaled * hat, axis=-1, keepdims=True)
        return (inv * (scaled - hat * mean)).astype(bf16)

    attn_inv, attn_hat, hidden, gathered_h = [], [], [], []
    for k in chunks:
        out_proj = jnp.dot(chunk_of(attn_tokens, k), out_full, preferred_element_type=f32)
        inv, hat = normed(out_proj)
        attn_inv.append(inv)
        attn_hat.append(hat)
        hidden.append(chunk_of(own_x, k).astype(f32) + hat * attn_scale)
        low = hidden[k].astype(bf16)
        if k:
            low = after(low, *(piece for _, piece in up_pieces))
        gathered_h.append(plan.token_gather(low))

    gate_up, activated = [], []
    for k in chunks:
        both = jnp.dot(gathered_h[k], ff_weight, preferred_element_type=f32).astype(bf16)
        gate_up.append(both)
        gate, up = both[:, :ff_width].astype(f32), both[:, ff_width:].astype(f32)
        activated.append((jax.nn.silu(gate) * up).astype(bf16))
    mlp_out, own_cot = multiply_scatter(
        plan, activated, down_rows, False, 2, swapped=cotangent
    )

    outputs, upstream, shard_rows = [], [], []
    mlp_gain_part = 0.0
    for k in chunks:
        inv, hat = normed(chunk_of(mlp_out, k))
        outputs.append((hidden[k] + hat * mlp_scale).astype(bf16))
        upstream.append(chunk_of(own_cot, k).astype(f32))
        mlp_gain_part += jnp.sum(upstream[k] * hat, axis=0)
        shard_rows.append(plan.token_gather(norm_grad(inv, hat, upstream[k] * mlp_scale)))

    ff_grad = []
    for k in chunks:
        ff_grad.append(unit_grad(shard_rows[k], down_rows, gate_up[k]))
    down_grad = sum(contract_rows(activated[k], shard_rows[k]) for k in chunks).astype(bf16)
    ff_weight_grad = sum(contract_rows(gathered_h[k], ff_grad[k]) for k in chunks).astype(bf16)
    hidden_grad_mlp, ff_blocks, layer_output = multiply_scatter(
        plan,
        ff_grad,
        ff_weight,
        True,
        3,
        (ff_weight_grad,),
        (0,),
        swapped=jnp.concatenate(outputs),
    )
    hidden_grad = [upstream[k] + chunk_of(hidden_grad_mlp, k) for k in chunks]
    ff_sum = plan.weight_send(plan.weight_sum(ff_weight_grad, ff_blocks, 0), 0)
    down_blocks = plan.weight_exchange(after(down_grad, ff_blocks), 1)

    attn_gain_part = 0.0
    proj_grads, token_grads = [], []
    for k in chunks:
        attn_gain_part += jnp.sum(hidden_grad[k] * attn_hat[k], axis=0)
        proj_grads.append(norm_grad(attn_inv[k], attn_hat[k], hidden_grad[k] * attn_scale))
        token_grads.append(contract_cols(proj_grads[k], out_full).astype(bf16))
    out_token_grad = jnp.concatenate(token_grads)

    attn_grad = jnp.zeros((seq_len, local_width), bf16)
    for flip in range(rows):
        other = mine ^ flip
        piece = lax.dynamic_slice(
            out_token_grad, (0, other * local_width), (own_tokens, local_width)
        )
        if flip:
            piece = plan.partner(piece, flip)
        attn_grad = lax.dynamic_update_slice(attn_grad, piece, (other * own_tokens, 0))

    out_grad = sum(
        contract_rows(
            attn_out.reshape(rows, 2, part, local_width)[:, k].reshape(-1, local_width),
            plan.token_gather(proj_grads[k]),
        )
        for k in chunks
    ).astype(bf16)
    out_sum = plan.weight_sum(out_grad, plan.weight_exchange(out_grad, 1), 1)
    query_grad, key_grad, value_grad = attend_back(
        high,
        first_row,
        query,
        key,
        value,
        attn_out,
        attn_grad,
        log_sum,
        head_size,
        tile,
        (down_blocks,),
    )
    down_sum = plan.weight_send(plan.weight_sum(down_grad, down_blocks, 1), 1)
    shared = (proj, query_inv, key_inv, cosine, sine, query_scale, key_scale, query_grad, key_grad)
    dots, gain_sums = norm_back(*shared, head_size)
    dots = group_sum(
        plan,
        jnp.concatenate([dots, jnp.stack([attn_gain_part, mlp_gain_part])], axis=1),
        6,
    )
    dots, post_sums = dots[:, :seq_len], dots[:, seq_len:]
    proj_grad_all = proj_back(
        *shared, value_grad, dots, head_size, model_width, (ff_sum,)
    )
    proj_grad_all = after(proj_grad_all, out_sum)
    halves = proj_grad_all.reshape(rows, 2, part, wide)
    proj_weight_grad = sum(
        contract_rows(gathered_x[k], halves[:, k].reshape(-1, wide)) for k in chunks
    ).astype(bf16)
    small = jnp.concatenate(
        [
            gain_sums[0].reshape(plan.cols, -1),
            gain_sums[1].reshape(plan.cols, -1),
            post_sums[0].reshape(plan.cols, -1),
            post_sums[1].reshape(plan.cols, -1),
        ],
        axis=1,
    )
    small = jnp.pad(small, ((0, 0), (0, extra * wide - small_size)))
    small = small.reshape(plan.cols, extra, wide).astype(bf16)
    stacked = jnp.concatenate(
        [proj_weight_grad.reshape(plan.cols, own_depth, wide), small], axis=1
    )
    stacked = stacked.reshape(-1, wide)
    out_sum = plan.weight_send(out_sum, 1)
    stacked = after(stacked, out_sum, down_sum)
    input_grad, _, proj_sum = multiply_scatter(
        plan,
        [proj_grad_all],
        proj_weight,
        True,
        4,
        (stacked,),
        (0,),
        jnp.concatenate(hidden_grad),
    )
    small = proj_sum[own_depth:].reshape(-1)[:small_size]
    query_gain_sum, key_gain_sum, attn_gain_sum, mlp_gain_sum = jnp.split(small, cuts)
    proj_sum = proj_sum[:own_depth]
    own_ff = w_gate.shape[1]
    return (
        layer_output,
        input_grad,
        proj_sum[:, :local_width],
        proj_sum[:, local_width : 2 * local_width],
        proj_sum[:, 2 * local_width :],
        out_sum,
        query_gain_sum,
        key_gain_sum,
        attn_gain_sum,
        ff_sum[:, :own_ff],
        ff_sum[:, own_ff:],
        down_sum,
        mlp_gain_sum,
    )


def solution(mesh):
    tokens = P(("col", "row"), None)
    columns = P("col", "row")
    across = P("row", "col")
    vector = P(("row", "col"))
    return jax.shard_map(
        functools.partial(body, Plan(mesh)),
        mesh=mesh,
        in_specs=(
            tokens,
            P("col"),
            columns,
            columns,
            columns,
            across,
            vector,
            vector,
            P("col"),
            columns,
            columns,
            across,
            P("col"),
            tokens,
        ),
        out_specs=(
            tokens,
            tokens,
            columns,
            columns,
            columns,
            across,
            vector,
            vector,
            P("col"),
            columns,
            columns,
            across,
            P("col"),
        ),
        check_vma=False,
    )
```
